32 devices in a mesh: expert: 16 (over z, y, core), fsdp: 2 (over x).
Axes of the slice: x: 2, y: 2, z: 4, core: 2. Of those that a mesh axis runs over, the one named last changes fastest.
Arguments:
- tokens: bfloat16 [4096, 2048], P(('expert', 'fsdp')), may hold values from -6 to 6
- cotangent: bfloat16 [4096, 2048], P(('expert', 'fsdp')), may hold values from -6 to 6
- routes: int32 [4096, 6], P(('expert', 'fsdp')), may hold values from 0 to 15, all different within a row; in each aligned block of 128 rows (0 to 127, 128 to 255, ...) at most 60 rows name the same one
- lengths: int32 [16], P('expert'), may hold values from 64 to 256, as said below
- attn_gain: bfloat16 [2048], P(('expert', 'fsdp')), may hold values from 0.099609375 to 1.8984375
- q_weight: bfloat16 [2048, 3072], P(('expert', 'fsdp')), may hold values from -0.1875 to 0.1875
- kva_weight: bfloat16 [2048, 576], P(('expert', 'fsdp')), may hold values from -0.125 to 0.125
- kv_gain: bfloat16 [512], P(('expert', 'fsdp')), may hold values from 0.099609375 to 1.8984375
- kvb_weight: bfloat16 [512, 4096], P(('expert', 'fsdp')), may hold values from -0.25 to 0.25
- out_weight: bfloat16 [2048, 2048], P(('expert', 'fsdp')), may hold values from -1 to 1
- ffn_gain: bfloat16 [2048], P(('expert', 'fsdp')), may hold values from 0.099609375 to 1.8984375
- router_weight: bfloat16 [2048, 16], P(('expert', 'fsdp')), may hold values from -0.0625 to 0.0625
- shared_gate: bfloat16 [2048, 1408], P(('expert', 'fsdp')), may hold values from -0.125 to 0.125
- shared_up: bfloat16 [2048, 1408], P(('expert', 'fsdp')), may hold values from -0.125 to 0.125
- shared_down: bfloat16 [1408, 2048], P(('expert', 'fsdp')), may hold values from -0.15625 to 0.15625
- expert_gate: bfloat16 [16, 2048, 1408], P('expert', 'fsdp'), may hold values from -0.125 to 0.125
- expert_up: bfloat16 [16, 2048, 1408], P('expert', 'fsdp'), may hold values from -0.125 to 0.125
- expert_down: bfloat16 [16, 1408, 2048], P('expert', None, 'fsdp'), may hold values from -6 to 6
Outputs:
- mixed: bfloat16 [4096, 2048], P(('expert', 'fsdp'))
- tokens_grad: float32 [4096, 2048], P(('expert', 'fsdp'))
- balance: float32 [], replicated
- attn_gain_grad: float32 [2048], P(('expert', 'fsdp'))
- q_weight_grad: float32 [2048, 3072], P(('expert', 'fsdp'))
- kva_weight_grad: float32 [2048, 576], P(('expert', 'fsdp'))
- kv_gain_grad: float32 [512], P(('expert', 'fsdp'))
- kvb_weight_grad: float32 [512, 4096], P(('expert', 'fsdp'))
- out_weight_grad: float32 [2048, 2048], P(('expert', 'fsdp'))
- ffn_gain_grad: float32 [2048], P(('expert', 'fsdp'))
- router_weight_grad: float32 [2048, 16], P(('expert', 'fsdp'))
- shared_gate_grad: float32 [2048, 1408], P(('expert', 'fsdp'))
- shared_up_grad: float32 [2048, 1408], P(('expert', 'fsdp'))
- shared_down_grad: float32 [1408, 2048], P(('expert', 'fsdp'))
- expert_gate_grad: float32 [16, 2048, 1408], P('expert', 'fsdp')
- expert_up_grad: float32 [16, 2048, 1408], P('expert', 'fsdp')
- expert_down_grad: float32 [16, 1408, 2048], P('expert', None, 'fsdp')
The draws below stay inside these ranges and needn't reach their ends.
Inputs may be any that keep to these rules, and one draw needn't show every extreme that they name: `routes`: in each device's 128 rows (aligned blocks) no expert is named by more than 60 pairs, and in every draw some expert is named by exactly 60 in some block. Valid slots are the first ones of a sequence; lengths never fall from one sequence to the next; the first sequence has a quarter of its slots valid and the last is full.
All inputs are finite; a program needn't handle non-finite values.
Results may differ from the reference program's by a relative error of at most 0.024.
Values may be sent and summed in bfloat16 or wider, within the bound.
A program may use at most 384 MiB of HBM per device.

```python
import math
import jax
import jax.numpy as jnp
import numpy as np
from jax import lax

D = 2048
H = 16
DN = 128
DR = 64
DV = 128
KVR = 512
FFE = 1408
FFS = 1408
TOPK = 6
TOK_DEV = 128
EXPERTS = 16
SEQ = 256
SEQS = 16
TOKENS = 4096
CAP = 60
DEVICES = 32


def draw_lengths(key, part):
    first_key = jax.random.fold_in(key, 7)
    drawn = jax.random.randint(first_key, (SEQS,), SEQ // 4, SEQ + 1)
    drawn = drawn.at[0].set(SEQ // 4)
    drawn = drawn.at[SEQS - 1].set(SEQ)
    return jnp.sort(drawn).astype(jnp.int32)


def block_scale(key, shape, shards, least, top_value):
    factor_of = 1.0
    for dim, blocks in shards:
        draws = jax.random.uniform(jax.random.fold_in(jax.random.fold_in(key, 6), dim), (blocks,), jnp.float32, least / len(shards), top_value / len(shards))
        factor_of = factor_of * jnp.repeat(jnp.exp(draws), shape[dim] // blocks).reshape((-1,) + (1,) * (len(shape) - 1 - dim))
    return factor_of


def assign_block(stream_key, own, number, rows, amount, top, bound, slope):
    sequence = jax.random.permutation(stream_key, amount)
    crowded, usual = load_shares(amount, rows * top, bound, slope, True), load_shares(amount, rows * top, bound, slope, False)
    places = jnp.arange(amount)

    def named(sizes, turn):
        used = int((sizes > 0).sum())
        fixed = max(1, used // 4)
        moved = fixed + (places - fixed + turn * (used - fixed)) % max(1, amount - fixed)
        return jnp.zeros((amount,), jnp.int32).at[sequence[jnp.where(places < fixed, places, moved)]].set(jnp.asarray(sizes, jnp.int32))

    sizes = jnp.where(number % 4 == 0, named(crowded, number // 4), named(usual, number - number // 4 - 1))
    mixed = jax.random.permutation(jax.random.fold_in(own, 3), amount)
    source_of, receiver = mixed[0:amount // 2 * 2:2], mixed[1:amount // 2 * 2:2]
    room = jnp.minimum(sizes[source_of] - 1, bound - sizes[receiver]) // 2
    room = jnp.where((source_of == sequence[0]) | (receiver == sequence[0]) | (sizes[receiver] == 0), 0, jnp.maximum(room, 0))
    moved = jax.random.randint(jax.random.fold_in(own, 4), (amount // 2,), 0, 1 << 20) % (room + 1)
    sizes = sizes.at[source_of].add(-moved).at[receiver].add(moved)
    labels = jnp.searchsorted(jnp.cumsum(sizes), jnp.arange(rows * top), side="right").astype(jnp.int32)
    table = labels.reshape(top, rows).T
    table = table[jax.random.permutation(jax.random.fold_in(own, 1), rows)]
    turn = jax.random.randint(jax.random.fold_in(own, 2), (rows, 1), 0, top)
    return jnp.take_along_axis(table, (jnp.arange(top)[None, :] + turn) % top, axis=1)


def load_shares(count, total, bound, slope, full):
    weights = [(1 << 20) // math.isqrt(rank ** slope) + 1 for rank in range(1, count + 1)]
    largest = bound if full else min(bound, max(-(-total // count), total * weights[0] // sum(weights)))
    least = 1 if total - largest >= count - 1 else 0
    holding, spare = [largest] + [least] * (count - 1), total - largest - least * (count - 1)
    while spare > 0:
        candidates = [i for i in range(1, count) if holding[i] < largest] or [i for i in range(1, count) if holding[i] < bound]
        mass, remaining = sum([weights[i] for i in candidates]), spare
        for i in candidates:
            more = min(bound - holding[i], max(1, remaining * weights[i] // mass), spare)
            holding[i] = holding[i] + more
            spare = spare - more
    return np.array(holding)


def bell_draw(rng, shape, scale, bound, pieces=(), kind=jnp.bfloat16):
    factor_of = block_scale(rng, shape, pieces, -0.22, 0.18) if pieces else 1.0
    values = jax.random.normal(rng, shape, jnp.float32) * scale * factor_of
    return jnp.minimum(jnp.maximum(values, -bound), bound).astype(kind)


def setup_inputs(seed: int = 0) -> dict:
    splits = jax.random.split(jax.random.key(seed), 19)
    tokens = bell_draw(splits[0], (TOKENS, D), 1.0, 6.0, ((0, 32),))
    cotangent = bell_draw(splits[1], (TOKENS, D), 1.0, 6.0, ((0, 32),))
    routes_keys = jax.random.split(jax.random.fold_in(splits[2], 1), TOKENS // TOK_DEV)
    routes_turns = jax.random.permutation(jax.random.fold_in(splits[2], 3), TOKENS // TOK_DEV)
    routes = jax.vmap(lambda own, number: assign_block(jax.random.fold_in(splits[2], 2), own, number, TOK_DEV, EXPERTS, TOPK, CAP, 1))(routes_keys, routes_turns).reshape((TOKENS, TOPK))
    lengths = draw_lengths(jax.random.fold_in(splits[18], 71), 0)
    attn_gain = jnp.clip(1.0 + 0.18 * jax.random.normal(splits[4], (D,), jnp.float32), 0.099609375, 1.8984375).astype(jnp.bfloat16)
    q_weight = bell_draw(splits[5], (D, H * (DN + DR)), (D // 2) ** -0.5, 0.1875, ((0, 32),))
    kva_weight = bell_draw(splits[6], (D, KVR + DR), D ** -0.5, 0.125, ((0, 32),))
    kv_gain = jnp.clip(1.0 + 0.18 * jax.random.normal(splits[7], (KVR,), jnp.float32), 0.099609375, 1.8984375).astype(jnp.bfloat16)
    kvb_weight = bell_draw(splits[8], (KVR, H * (DN + DV)), KVR ** -0.5, 0.25, ((0, 32),))
    out_weight = bell_draw(splits[9], (H * DV, D), (H * DV // 64) ** -0.5, 1.0, ((0, 32),))
    ffn_gain = jnp.clip(1.0 + 0.18 * jax.random.normal(splits[10], (D,), jnp.float32), 0.099609375, 1.8984375).astype(jnp.bfloat16)
    router_weight = bell_draw(splits[11], (D, EXPERTS), (4 * D) ** -0.5, 0.0625, ((0, 32),))
    shared_gate = bell_draw(splits[12], (D, FFS), D ** -0.5, 0.125, ((0, 32),))
    shared_up = bell_draw(splits[13], (D, FFS), D ** -0.5, 0.125, ((0, 32),))
    shared_down = bell_draw(splits[14], (FFS, D), FFS ** -0.5, 0.15625, ((0, 32),))
    expert_gate = bell_draw(splits[15], (EXPERTS, D, FFE), D ** -0.5, 0.125, ((0, 16), (1, 2)))
    expert_up = bell_draw(splits[16], (EXPERTS, D, FFE), D ** -0.5, 0.125, ((0, 16), (1, 2)))
    expert_down = bell_draw(splits[17], (EXPERTS, FFE, D), 1.0, 6.0, ((0, 16), (2, 2)))
    return dict(tokens=tokens, cotangent=cotangent, routes=routes, lengths=lengths, attn_gain=attn_gain, q_weight=q_weight, kva_weight=kva_weight, kv_gain=kv_gain, kvb_weight=kvb_weight, out_weight=out_weight, ffn_gain=ffn_gain, router_weight=router_weight, shared_gate=shared_gate, shared_up=shared_up, shared_down=shared_down, expert_gate=expert_gate, expert_up=expert_up, expert_down=expert_down)


epsilon = 1e-06
balance_weight = 0.001
masked_value = -1e+30
highest = lax.Precision.HIGHEST

@jax.custom_vjp
def low(v):
    return lax.optimization_barrier(v.astype(jnp.bfloat16)).astype(jnp.float32)

@jax.custom_vjp
def low_back(v):
    return v

def low_keep(v):
    return (low(v), None)

def low_pass(kept, grad):
    return (grad,)

def back_keep(v):
    return (v, None)

def back_low(kept, grad):
    return (low(grad),)
low.defvjp(low_keep, low_pass)
low_back.defvjp(back_keep, back_low)

def rms_scale(vector, gain_row):
    return vector * lax.rsqrt(lax.optimization_barrier(jnp.mean(vector * vector, axis=-1, keepdims=True)) + epsilon) * gain_row

def rope_tables(positions):
    half_width = DR // 2
    frequency = 10000.0 ** (-jnp.arange(half_width, dtype=jnp.float32) / half_width)
    angles = positions.astype(jnp.float32)[:, None] * frequency[None, :]
    return (jnp.cos(angles), jnp.sin(angles))

def rotate(vector, cosine, sine_vals):
    half_width = vector.shape[-1] // 2
    first_half = vector[..., :half_width]
    second_half = vector[..., half_width:]
    return jnp.concatenate([first_half * cosine - second_half * sine_vals, second_half * cosine + first_half * sine_vals], axis=-1)

def attend(packed):
    query_seq, keyval_seq, rot_seq, seq_length = packed
    raw_scores = jnp.einsum('thd,shd->hts', query_seq[..., :DN], keyval_seq[..., :DN], precision=highest) + jnp.einsum('thr,sr->hts', query_seq[..., DN:], rot_seq, precision=highest)
    place_row = jnp.arange(SEQ, dtype=jnp.int32)
    allowed = (place_row[None, :] <= place_row[:, None]) & (place_row[None, :] < seq_length)
    scores = low_back(jnp.where(allowed[None], raw_scores * (DN + DR) ** (-0.5), masked_value))
    weights = low(jax.nn.softmax(scores, axis=-1))
    context = jnp.einsum('hts,shd->thd', weights, keyval_seq[..., DN:], precision=highest)
    return low(low_back(context))

def route_lists(routes):
    flat_routes = routes.reshape(-1)

    def expert_list(expert):
        chosen = flat_routes == expert
        pair_index = jnp.nonzero(chosen, size=DEVICES * CAP, fill_value=0)[0].astype(jnp.int32)
        live_mask = (jnp.arange(DEVICES * CAP, dtype=jnp.int32) < jnp.sum(chosen.astype(jnp.int32))).astype(jnp.float32)
        return (pair_index, live_mask)
    return lax.map(expert_list, jnp.arange(EXPERTS, dtype=jnp.int32))

def forward(params, tokens_f, routes, lengths, valid_mask, pair_index, live_mask):
    attn_gain, q_weight, kva_weight, kv_gain, kvb_weight, out_weight, ffn_gain, router_weight, shared_gate, shared_up, shared_down, expert_gate, expert_up, expert_down = params
    positions = jnp.arange(TOKENS, dtype=jnp.int32) % SEQ
    cosine, sine_vals = rope_tables(positions)
    normed = low(rms_scale(tokens_f, attn_gain))
    query_proj = low_back(jnp.dot(normed, q_weight, precision=highest)).reshape(TOKENS, H, DN + DR)
    query_all = low(jnp.concatenate([query_proj[..., :DN], rotate(query_proj[..., DN:], cosine[:, None, :], sine_vals[:, None, :])], axis=-1))
    compressed = low_back(jnp.dot(normed, kva_weight, precision=highest))
    latent = low(rms_scale(compressed[:, :KVR], kv_gain))
    key_rot = low(rotate(compressed[:, KVR:], cosine, sine_vals))
    keyval = low(low_back(jnp.dot(latent, kvb_weight, precision=highest))).reshape(TOKENS, H, DN + DV)
    context = lax.map(jax.checkpoint(attend), (query_all.reshape(SEQS, SEQ, H, DN + DR), keyval.reshape(SEQS, SEQ, H, DN + DV), key_rot.reshape(SEQS, SEQ, DR), lengths))
    context = context.reshape(TOKENS, H * DV)
    residual = tokens_f + low_back(jnp.dot(context, out_weight, precision=highest))
    normed_two = low(rms_scale(residual, ffn_gain))
    router_probs = jax.nn.softmax(low_back(jnp.dot(normed_two, router_weight, precision=highest)), axis=-1)
    hot_pairs = (routes[:, :, None] == jnp.arange(EXPERTS, dtype=jnp.int32)[None, None, :]).astype(jnp.float32)
    gate_vals = lax.optimization_barrier(jnp.sum(hot_pairs * router_probs[:, None, :], axis=-1))
    route_counts = lax.optimization_barrier(jnp.sum(hot_pairs * valid_mask[:, None, None], axis=(0, 1)))
    valid_total = jnp.sum(valid_mask)
    share_vals = lax.optimization_barrier(jnp.sum(router_probs * valid_mask[:, None], axis=0)) / valid_total
    balance = jnp.sum(EXPERTS / (TOPK * valid_total) * route_counts * share_vals)
    shared_g = low_back(jnp.dot(normed_two, shared_gate, precision=highest))
    shared_u = low_back(jnp.dot(normed_two, shared_up, precision=highest))
    shared_act = low(jax.nn.silu(shared_g) * shared_u)
    shared_out = jnp.dot(shared_act, shared_down, precision=highest)
    flat_gates = gate_vals.reshape(-1)

    def expert_rows(packed):
        gate_w, up_w, down_w, index_row, live_row = packed
        rows_in = low_back(normed_two[index_row // TOPK])
        gate_h = low_back(jnp.dot(rows_in, gate_w, precision=highest))
        up_h = low_back(jnp.dot(rows_in, up_w, precision=highest))
        act_h = low(jax.nn.silu(gate_h) * up_h)
        out_h = low(low_back(jnp.dot(act_h, down_w, precision=highest)))
        return out_h * (flat_gates[index_row] * live_row)[:, None]
    contrib = lax.map(jax.checkpoint(expert_rows), (expert_gate, expert_up, expert_down, pair_index, live_mask))
    routed = jnp.zeros((TOKENS, D), jnp.float32).at[(pair_index // TOPK).reshape(-1)].add(contrib.reshape(-1, D))
    mixed = residual + shared_out + routed
    return (mixed, balance)

def reference(tokens, cotangent, routes, lengths, attn_gain, q_weight, kva_weight, kv_gain, kvb_weight, out_weight, ffn_gain, router_weight, shared_gate, shared_up, shared_down, expert_gate, expert_up, expert_down):
    params = tuple((w.astype(jnp.float32) for w in (attn_gain, q_weight, kva_weight, kv_gain, kvb_weight, out_weight, ffn_gain, router_weight, shared_gate, shared_up, shared_down, expert_gate, expert_up, expert_down)))
    row_ids = jnp.arange(TOKENS, dtype=jnp.int32)
    valid_mask = (row_ids % SEQ < lengths[row_ids // SEQ]).astype(jnp.float32)
    pair_index, live_mask = route_lists(routes)
    fill_scale = TOKENS / jnp.sum(valid_mask)

    def run(params_in, tokens_in):
        return forward(params_in, tokens_in, routes, lengths, valid_mask, pair_index, live_mask)
    (mixed, balance), pull = jax.vjp(run, params, tokens.astype(jnp.float32))
    grads, tokens_grad = pull((cotangent.astype(jnp.float32) * (valid_mask * fill_scale)[:, None], jnp.ones_like(balance) * balance_weight))
    return (mixed.astype(jnp.bfloat16), tokens_grad, balance, grads[0], grads[1], grads[2], grads[3], grads[4], grads[5], grads[6], grads[7], grads[8], grads[9], grads[10], grads[11], grads[12], grads[13])
```

```python
import jax
import jax.numpy as jnp
from jax import lax
from jax.sharding import PartitionSpec as P

D = 2048
H = 16
DN = 128
DR = 64
DV = 128
KVR = 512
TOPK = 6


epsilon = 1e-06
balance_weight = 0.001
masked_value = -1e30


def rms_norm(vector, gain_row):
    inverse = lax.rsqrt(jnp.mean(vector * vector, axis=-1, keepdims=True) + epsilon)
    return (vector * inverse * gain_row, inverse)


def norm_back(grad_in, vector, inverse, gain_row):
    scaled = grad_in * gain_row
    gain_grad = jnp.sum(grad_in * vector * inverse, axis=0)
    vector_grad = inverse * scaled - vector * inverse**3 * jnp.mean(
        scaled * vector, axis=-1, keepdims=True
    )
    return (vector_grad, gain_grad)


def rope_tables(positions):
    half_width = DR // 2
    frequency = 10000.0 ** (-jnp.arange(half_width, dtype=jnp.float32) / half_width)
    angles = positions.astype(jnp.float32)[:, None] * frequency[None, :]
    return (jnp.cos(angles), jnp.sin(angles))


def rotate(vector, cosine, sine_vals):
    half_width = vector.shape[-1] // 2
    first_half = vector[..., :half_width]
    second_half = vector[..., half_width:]
    return jnp.concatenate(
        [
            first_half * cosine - second_half * sine_vals,
            second_half * cosine + first_half * sine_vals,
        ],
        axis=-1,
    )


def rotate_back(grad_in, cosine, sine_vals):
    half_width = grad_in.shape[-1] // 2
    first_half = grad_in[..., :half_width]
    second_half = grad_in[..., half_width:]
    return jnp.concatenate(
        [
            first_half * cosine + second_half * sine_vals,
            second_half * cosine - first_half * sine_vals,
        ],
        axis=-1,
    )


def silu_slope(vector):
    sigmoid_vals = jax.nn.sigmoid(vector)
    return sigmoid_vals * (1.0 + vector * (1.0 - sigmoid_vals))


def gather_all(shard):
    return lax.all_gather(shard, ("expert", "fsdp"), axis=0, tiled=True)


def gather_plane(shard):
    return lax.all_gather(shard, "expert", axis=0, tiled=True)


def scatter_all(partial):
    return lax.psum_scatter(
        partial.astype(jnp.bfloat16), ("expert", "fsdp"), scatter_dimension=0, tiled=True
    ).astype(jnp.float32)


def scatter_plane(partial):
    return lax.psum_scatter(partial, "expert", scatter_dimension=0, tiled=True)


def from_peers(block):
    size = lax.axis_size("fsdp")
    return [block] + [
        lax.ppermute(block, "fsdp", [(j, (j - r) % size) for j in range(size)])
        for r in range(1, size)
    ]


def sum_to_peers(term):
    size = lax.axis_size("fsdp")
    arrived = [
        lax.ppermute(term(r), "fsdp", [(j, (j + r) % size) for j in range(size)])
        for r in range(1, size)
    ]
    return arrived


def body(
    tokens,
    cotangent,
    routes,
    lengths,
    attn_gain,
    q_weight,
    kva_weight,
    kv_gain,
    kvb_weight,
    out_weight,
    ffn_gain,
    router_weight,
    shared_gate,
    shared_up,
    shared_down,
    expert_gate,
    expert_up,
    expert_down,
):
    bf16, f32 = jnp.bfloat16, jnp.float32
    tok_rows, dim = tokens.shape
    peers = lax.axis_size("fsdp")
    group = lax.axis_size("expert")
    fid, eid = lax.axis_index("fsdp"), lax.axis_index("expert")
    seq_len = tok_rows * peers
    slot_total = seq_len * group
    expert_count = router_weight.shape[1]
    capacity = max(4, 5 * tok_rows * TOPK // (4 * expert_count))
    capacity = -(-capacity // 16) * 16
    half = dim // peers
    plane_rows = group * tok_rows
    pairs = group * capacity

    def roll_in(array, axis):
        return jnp.roll(array, -fid * half, axis=axis)

    def roll_out(array, axis):
        return jnp.roll(array, fid * half, axis=axis)

    positions = fid * tok_rows + jnp.arange(tok_rows, dtype=jnp.int32)
    seq_length = lengths[0]
    valid_mask = (positions < seq_length).astype(f32)
    expert_ids = jnp.arange(expert_count, dtype=jnp.int32)
    hot_sum = jnp.sum((routes[:, :, None] == expert_ids[None, None, :]).astype(f32), axis=1)
    local_counts = jnp.sum(hot_sum * valid_mask[:, None], axis=0)

    def lane_row(vector):
        return jnp.pad(vector.astype(f32), (0, tok_rows - vector.shape[0]))[None, :]

    small = jnp.concatenate(
        [routes.T.astype(f32)]
        + [lane_row(v) for v in (attn_gain, ffn_gain, kv_gain, local_counts, lengths)]
        + [jnp.zeros((16 - TOPK - 5, tok_rows), f32)],
        axis=0,
    )
    gate_parts = from_peers(expert_gate[0])
    up_parts = from_peers(expert_up[0])
    down_parts = from_peers(expert_down[0])
    small_all = gather_all(small[None])
    w_compress = gather_all(kva_weight)
    w_expand = gather_all(kvb_weight)
    w_query = gather_all(q_weight)
    w_output = gather_all(out_weight)
    w_router = gather_all(router_weight)
    gain_attn = small_all[:, TOPK, : attn_gain.shape[0]].reshape(-1)
    gain_ffn = small_all[:, TOPK + 1, : ffn_gain.shape[0]].reshape(-1)
    gain_latent = small_all[:, TOPK + 2, : kv_gain.shape[0]].reshape(-1)
    route_counts = jnp.sum(small_all[:, TOPK + 3, :expert_count], axis=0)
    all_lengths = small_all.reshape(group, peers, 16, tok_rows)[:, 0, TOPK + 4, 0]
    valid_total = jnp.sum(all_lengths)
    fill_scale = slot_total / valid_total
    plane_small = lax.dynamic_index_in_dim(
        small_all.reshape(group, peers, 16, tok_rows), fid, axis=1, keepdims=False
    )
    units = shared_gate.shape[1] // group
    pieces = jnp.concatenate(
        [
            shared_gate.reshape(-1, group, units),
            shared_up.reshape(-1, group, units),
        ],
        axis=2,
    ).transpose(1, 0, 2)
    pieces = lax.all_to_all(pieces, "expert", split_axis=0, concat_axis=0, tiled=True)
    gu_weight = jnp.roll(jnp.stack(from_peers(pieces)), fid, axis=0)
    gu_weight = gu_weight.transpose(1, 0, 2, 3).reshape(dim, 2 * units)
    gu_weight = roll_in(gu_weight, 0)
    sd_weight = jnp.roll(jnp.stack(from_peers(shared_down)), fid, axis=0).reshape(units, dim)
    sd_weight = roll_in(sd_weight, 1)
    cosine, sine_vals = rope_tables(positions)
    tokens_f = tokens.astype(f32)
    cot_plane = gather_plane(roll_in(cotangent, 1))
    normed_one, inverse_one = rms_norm(tokens_f, gain_attn)
    hidden_one = normed_one.astype(bf16)
    query_proj = jnp.dot(hidden_one, w_query, preferred_element_type=f32).reshape(
        tok_rows, H, DN + DR
    )
    query_all = jnp.concatenate(
        [
            query_proj[..., :DN],
            rotate(query_proj[..., DN:], cosine[:, None, :], sine_vals[:, None, :]),
        ],
        axis=-1,
    ).astype(bf16)
    compressed = jnp.dot(hidden_one, w_compress, preferred_element_type=f32)
    latent_raw = compressed[:, :KVR]
    latent_norm, inverse_kv = rms_norm(latent_raw, gain_latent)
    latent = latent_norm.astype(bf16)
    key_rot = rotate(compressed[:, KVR:], cosine, sine_vals).astype(bf16)
    all_latent, all_rot = (
        lax.all_gather(latent, "fsdp", axis=0, tiled=True),
        lax.all_gather(key_rot, "fsdp", axis=0, tiled=True),
    )
    keyval = jnp.dot(all_latent, w_expand, preferred_element_type=f32).astype(bf16)
    keyval = keyval.reshape(seq_len, H, DN + DV)
    key_nope = keyval[..., :DN]
    value_all = keyval[..., DN:]
    query_nope = query_all[..., :DN]
    query_rope = query_all[..., DN:]
    score_scale = (DN + DR) ** (-0.5)
    key_place = jnp.arange(seq_len, dtype=jnp.int32)
    allowed = (key_place[None, :] <= positions[:, None]) & (key_place[None, :] < seq_length)
    raw_scores = jnp.einsum(
        "thd,shd->hts", query_nope, key_nope, preferred_element_type=f32
    ) + jnp.einsum("thr,sr->hts", query_rope, all_rot, preferred_element_type=f32)
    scores = jnp.where(allowed[None], raw_scores * score_scale, masked_value)
    row_max = jnp.max(scores, axis=-1, keepdims=True)
    exp_scores = jnp.exp(scores - row_max)
    probs_attn = exp_scores / jnp.sum(exp_scores, axis=-1, keepdims=True)
    probs_low = probs_attn.astype(bf16)
    context = (
        jnp.einsum("hts,shd->thd", probs_low, value_all, preferred_element_type=f32)
        .reshape(tok_rows, H * DV)
        .astype(bf16)
    )
    residual = tokens_f + jnp.dot(context, w_output, preferred_element_type=f32)
    normed_two, inverse_two = rms_norm(residual, gain_ffn)
    hidden_two = normed_two.astype(bf16)
    hid_plane = gather_plane(roll_in(hidden_two, 1))
    router_probs = jax.nn.softmax(jnp.dot(hidden_two, w_router, preferred_element_type=f32), axis=-1)
    local_shares = jnp.sum(router_probs * valid_mask[:, None], axis=0)
    frequency = expert_count / (TOPK * valid_total) * route_counts
    d_probs_own = balance_weight * valid_mask[:, None] * frequency[None, :] / valid_total
    dlog_own = (
        router_probs * (d_probs_own - jnp.sum(router_probs * d_probs_own, axis=-1, keepdims=True))
    ).astype(bf16)
    named = jnp.any(plane_small[:, :TOPK, :] == eid.astype(f32), axis=1)
    rank = jnp.cumsum(named.astype(jnp.int32), axis=1) - 1
    slots = jnp.arange(capacity, dtype=jnp.int32)
    picker = (named[:, None, :] & (rank[:, None, :] == slots[None, :, None])).astype(bf16)
    plane_valid = (positions[None, :] < all_lengths[:, None]).astype(f32)
    plane_scale = (plane_valid * fill_scale).reshape(plane_rows, 1)
    hid3 = hid_plane.reshape(group, tok_rows, dim)
    cot3 = cot_plane.reshape(group, tok_rows, dim)
    rows_in = jnp.einsum("sji,sid->sjd", picker, hid3, preferred_element_type=f32)
    rows_in = rows_in.astype(bf16).reshape(pairs, dim)
    rows_cot = jnp.einsum("sji,sid->sjd", picker, cot3, preferred_element_type=f32)
    rows_cot = rows_cot.astype(bf16).reshape(pairs, dim)
    rows_scale = fill_scale * jnp.sum(
        picker.astype(f32) * plane_valid[:, None, :], axis=-1
    ).reshape(pairs, 1)
    w_router_in = roll_in(w_router, 0)
    probs_rows = jax.nn.softmax(jnp.dot(rows_in, w_router_in, preferred_element_type=f32), axis=-1)
    own_expert = (expert_ids == eid).astype(f32)[None, :]
    gate_rows = jnp.sum(probs_rows * own_expert, axis=-1, keepdims=True)

    def cut(array, r):
        return array[:, r * half : (r + 1) * half]

    def summed(term):
        total = term(0)
        for r in range(1, peers):
            total = total + term(r)
        return total

    hidden_g = summed(lambda r: jnp.dot(cut(rows_in, r), gate_parts[r], preferred_element_type=f32))
    hidden_u = summed(lambda r: jnp.dot(cut(rows_in, r), up_parts[r], preferred_element_type=f32))
    act = (jax.nn.silu(hidden_g) * hidden_u).astype(bf16)
    out_rows = jnp.concatenate(
        [jnp.dot(act, w, preferred_element_type=f32).astype(bf16) for w in down_parts], axis=1
    )
    d_gate = rows_scale * jnp.sum(
        rows_cot.astype(f32) * out_rows.astype(f32), axis=-1, keepdims=True
    )
    weighted = (gate_rows * out_rows.astype(f32)).astype(bf16)
    d_out = (gate_rows * rows_scale * rows_cot.astype(f32)).astype(bf16)
    d_act = summed(
        lambda r: lax.dot_general(
            cut(d_out, r), down_parts[r], (((1,), (1,)), ((), ())), preferred_element_type=f32
        )
    )
    d_hidden_g = (d_act * hidden_u * silu_slope(hidden_g)).astype(bf16)
    d_hidden_u = (d_act * jax.nn.silu(hidden_g)).astype(bf16)

    def outer(left, right):
        return lax.dot_general(left, right, (((0,), (0,)), ((), ())), preferred_element_type=f32)

    def with_peers(term):
        arrived = sum_to_peers(lambda r: term(r).astype(bf16))
        total = term(0)
        for block in arrived:
            total = total + block.astype(f32)
        return total

    egate_grad = with_peers(lambda r: outer(cut(rows_in, r), d_hidden_g))[None]
    eup_grad = with_peers(lambda r: outer(cut(rows_in, r), d_hidden_u))[None]
    edown_grad = with_peers(lambda r: outer(act, cut(d_out, r)))[None]
    dlog_rows = (gate_rows * d_gate * (own_expert - probs_rows)).astype(bf16)

    def back(left, weight):
        return lax.dot_general(left, weight, (((1,), (1,)), ((), ())), preferred_element_type=f32)

    d_rows = jnp.concatenate(
        [back(d_hidden_g, gate_parts[r]) + back(d_hidden_u, up_parts[r]) for r in range(peers)],
        axis=1,
    )
    d_rows = (d_rows + back(dlog_rows, w_router_in)).astype(bf16)
    gu = jnp.dot(hid_plane, gu_weight, preferred_element_type=f32)
    shared_g, shared_u = gu[:, :units], gu[:, units:]
    shared_act = jax.nn.silu(shared_g) * shared_u
    d_shared_act = back(cot_plane, sd_weight) * plane_scale
    d_gu = jnp.concatenate(
        [
            d_shared_act * shared_u * silu_slope(shared_g),
            d_shared_act * jax.nn.silu(shared_g),
        ],
        axis=1,
    ).astype(bf16)
    shared_low = shared_act.astype(bf16)
    d_sd = outer((shared_act * plane_scale).astype(bf16), cot_plane)
    d_gu_weight = outer(hid_plane, d_gu)
    out_part = jnp.einsum(
        "sji,sjd->sid", picker, weighted.reshape(group, capacity, dim), preferred_element_type=f32
    ).reshape(plane_rows, dim) + jnp.dot(shared_low, sd_weight, preferred_element_type=f32)
    back_part = jnp.einsum(
        "sji,sjd->sid", picker, d_rows.reshape(group, capacity, dim), preferred_element_type=f32
    ).reshape(plane_rows, dim) + back(d_gu, gu_weight)
    d_hidden_two = scatter_plane(back_part.astype(bf16))
    out_sum = scatter_plane(out_part.astype(bf16))
    mixed = (residual + roll_out(out_sum, 1).astype(f32)).astype(bf16)
    d_hidden_two = roll_out(d_hidden_two, 1).astype(f32) + back(dlog_own, w_router)
    router_grad = roll_out(outer(rows_in, dlog_rows), 0) + outer(hidden_two, dlog_own)
    d_gu_blocks = roll_out(d_gu_weight, 0).reshape(group, peers, dim // (group * peers), 2 * units)

    def gu_term(r):
        return lax.dynamic_index_in_dim(d_gu_blocks, (fid + r) % peers, axis=1, keepdims=False)

    gu_sum = gu_term(0)
    for block in sum_to_peers(gu_term):
        gu_sum = gu_sum + block
    gu_sum = lax.all_to_all(gu_sum, "expert", split_axis=0, concat_axis=0, tiled=True)
    gu_sum = gu_sum.transpose(1, 0, 2)
    sgate_grad = gu_sum[:, :, :units].reshape(shared_gate.shape)
    sup_grad = gu_sum[:, :, units:].reshape(shared_up.shape)
    d_sd_blocks = roll_out(d_sd, 1).reshape(peers, units // peers, dim)

    def sd_term(r):
        return lax.dynamic_index_in_dim(d_sd_blocks, (fid + r) % peers, axis=0, keepdims=False)

    sdown_grad = sd_term(0)
    for block in sum_to_peers(sd_term):
        sdown_grad = sdown_grad + block
    grad_out = cotangent.astype(f32) * (valid_mask * fill_scale)[:, None]
    d_residual, d_ffn_gain = norm_back(d_hidden_two, residual, inverse_two, gain_ffn)
    d_residual = d_residual + grad_out
    d_residual_low = d_residual.astype(bf16)
    d_output_w = outer(context, d_residual_low)
    d_context = back(d_residual_low, w_output).astype(bf16).reshape(tok_rows, H, DV)
    d_value = jnp.einsum("hts,thd->shd", probs_low, d_context, preferred_element_type=f32)
    d_weights = jnp.einsum("thd,shd->hts", d_context, value_all, preferred_element_type=f32)
    d_scores = (
        probs_attn * (d_weights - jnp.sum(probs_attn * d_weights, axis=-1, keepdims=True))
    ).astype(bf16)
    d_query_nope = score_scale * jnp.einsum(
        "hts,shd->thd", d_scores, key_nope, preferred_element_type=f32
    )
    d_query_rope = score_scale * jnp.einsum(
        "hts,sr->thr", d_scores, all_rot, preferred_element_type=f32
    )
    d_key_nope = score_scale * jnp.einsum(
        "hts,thd->shd", d_scores, query_nope, preferred_element_type=f32
    )
    d_key_rot = score_scale * jnp.einsum(
        "hts,thr->sr", d_scores, query_rope, preferred_element_type=f32
    )
    d_keyval_all = jnp.concatenate([d_key_nope, d_value], axis=-1).reshape(
        peers, tok_rows, H * (DN + DV)
    )
    d_key_rot = d_key_rot.reshape(peers, tok_rows, DR)

    def own_rows(array, r):
        return lax.dynamic_index_in_dim(array, (fid + r) % peers, axis=0, keepdims=False)

    own_dkeyval = with_peers(lambda r: own_rows(d_keyval_all, r))
    own_dkeyrot = with_peers(lambda r: own_rows(d_key_rot, r))
    d_keyval = own_dkeyval.astype(bf16)
    d_expand_w = outer(latent, d_keyval)
    d_latent = back(d_keyval, w_expand)
    d_latent_raw, d_latent_gain = norm_back(d_latent, latent_raw, inverse_kv, gain_latent)
    d_compressed = jnp.concatenate(
        [d_latent_raw, rotate_back(own_dkeyrot, cosine, sine_vals)], axis=-1
    ).astype(bf16)
    d_compress_w = outer(hidden_one, d_compressed)
    d_query = (
        jnp.concatenate(
            [d_query_nope, rotate_back(d_query_rope, cosine[:, None, :], sine_vals[:, None, :])],
            axis=-1,
        )
        .reshape(tok_rows, H * (DN + DR))
        .astype(bf16)
    )
    d_query_w = outer(hidden_one, d_query)
    d_hidden_one = back(d_query, w_query) + back(d_compressed, w_compress)
    d_tokens, d_attn_gain = norm_back(d_hidden_one, tokens_f, inverse_one, gain_attn)
    tokens_grad = d_tokens + d_residual
    smalls = lax.psum(
        jnp.concatenate([d_attn_gain, d_latent_gain, d_ffn_gain, local_shares]), ("expert", "fsdp")
    )
    device = eid * peers + fid

    def own_piece(start, size):
        count = size // (group * peers)
        return lax.dynamic_slice(smalls, (start + device * count,), (count,))

    attn_gain_grad = own_piece(0, dim)
    kv_gain_grad = own_piece(dim, KVR)
    ffn_gain_grad = own_piece(dim + KVR, dim)
    share_sums = smalls[2 * dim + KVR :]
    balance = jnp.sum(frequency * (share_sums / valid_total))
    return (
        mixed,
        tokens_grad,
        balance,
        attn_gain_grad,
        scatter_all(d_query_w),
        scatter_all(d_compress_w),
        kv_gain_grad,
        scatter_all(d_expand_w),
        scatter_all(d_output_w),
        ffn_gain_grad,
        scatter_all(router_grad),
        sgate_grad,
        sup_grad,
        sdown_grad,
        egate_grad,
        eup_grad,
        edown_grad,
    )


def solution(mesh):
    return jax.shard_map(
        body,
        mesh=mesh,
        in_specs=(
            P(("expert", "fsdp"), None),
            P(("expert", "fsdp"), None),
            P(("expert", "fsdp"), None),
            P("expert"),
            P(("expert", "fsdp")),
            P(("expert", "fsdp"), None),
            P(("expert", "fsdp"), None),
            P(("expert", "fsdp")),
            P(("expert", "fsdp"), None),
            P(("expert", "fsdp"), None),
            P(("expert", "fsdp")),
            P(("expert", "fsdp"), None),
            P(("expert", "fsdp"), None),
            P(("expert", "fsdp"), None),
            P(("expert", "fsdp"), None),
            P("expert", "fsdp", None),
            P("expert", "fsdp", None),
            P("expert", None, "fsdp"),
        ),
        out_specs=(
            P(("expert", "fsdp"), None),
            P(("expert", "fsdp"), None),
            P(),
            P(("expert", "fsdp")),
            P(("expert", "fsdp"), None),
            P(("expert", "fsdp"), None),
            P(("expert", "fsdp")),
            P(("expert", "fsdp"), None),
            P(("expert", "fsdp"), None),
            P(("expert", "fsdp")),
            P(("expert", "fsdp"), None),
            P(("expert", "fsdp"), None),
            P(("expert", "fsdp"), None),
            P(("expert", "fsdp"), None),
            P("expert", "fsdp", None),
            P("expert", "fsdp", None),
            P("expert", None, "fsdp"),
        ),
        check_vma=False,
    )
```

```python
import functools

import jax
import jax.numpy as jnp
from jax import lax
from jax.experimental import pallas as pl
from jax.experimental.pallas import tpu as pltpu
from jax.sharding import PartitionSpec as P

D = 2048
H = 16
DN = 128
DR = 64
DV = 128
KVR = 512
TOPK = 6


epsilon = 1e-06
balance_weight = 0.001
masked_value = -1e30


def rms_norm(vector, gain_row):
    inverse = lax.rsqrt(jnp.mean(vector * vector, axis=-1, keepdims=True) + epsilon)
    return (vector * inverse * gain_row, inverse)


def norm_back(grad_in, vector, inverse, gain_row):
    scaled = grad_in * gain_row
    gain_grad = jnp.sum(grad_in * vector * inverse, axis=0)
    vector_grad = inverse * scaled - vector * inverse**3 * jnp.mean(
        scaled * vector, axis=-1, keepdims=True
    )
    return (vector_grad, gain_grad)


def rope_tables(positions):
    half_width = DR // 2
    frequency = 10000.0 ** (-jnp.arange(half_width, dtype=jnp.float32) / half_width)
    angles = positions.astype(jnp.float32)[:, None] * frequency[None, :]
    return (jnp.cos(angles), jnp.sin(angles))


def rotate(vector, cosine, sine_vals):
    half_width = vector.shape[-1] // 2
    first_half = vector[..., :half_width]
    second_half = vector[..., half_width:]
    return jnp.concatenate(
        [
            first_half * cosine - second_half * sine_vals,
            second_half * cosine + first_half * sine_vals,
        ],
        axis=-1,
    )


def rotate_back(grad_in, cosine, sine_vals):
    half_width = grad_in.shape[-1] // 2
    first_half = grad_in[..., :half_width]
    second_half = grad_in[..., half_width:]
    return jnp.concatenate(
        [
            first_half * cosine + second_half * sine_vals,
            second_half * cosine - first_half * sine_vals,
        ],
        axis=-1,
    )


def silu_slope(vector):
    sigmoid_vals = jax.nn.sigmoid(vector)
    return sigmoid_vals * (1.0 + vector * (1.0 - sigmoid_vals))


MESH_IDS = pl.DeviceIdType.MESH


class Place:
    def __init__(self, group, peers, wide):
        self.wide = wide
        self.depth = min(4, group // 2)
        self.tall = group // 2 // self.depth
        self.across = peers if wide else 1
        self.peers = peers
        self.units = self.depth * self.tall * self.across
        self.slots = 2 * self.units

    def here(self):
        e = lax.axis_index("expert")
        self.fsdp = lax.axis_index("fsdp")
        self.c = e % 2
        self.y = e // 2 % self.tall
        self.z = e // (2 * self.tall)
        self.x = self.fsdp if self.wide else 0
        return self

    def slot(self, z, y, c, x):
        return ((z * self.tall + y) * 2 + c) * self.across + x

    def device(self, z, y, c, x=None):
        return ((z * self.tall + y) * 2 + c, self.fsdp if x is None else x)

    def greet(self, swapping):
        barrier = pltpu.get_barrier_semaphore()
        partners = self.peers if swapping or self.wide else 1
        count = 1 + (self.tall - 1) + (partners - 1)

        def signal(target):
            pl.semaphore_signal(barrier, inc=1, device_id=target, device_id_type=MESH_IDS)

        signal(self.device(self.z, self.y, 1 - self.c))
        for k in range(1, self.tall):
            signal(self.device(self.z, (self.y + k) % self.tall, self.c))
        for k in range(1, partners):
            signal(self.device(self.z, self.y, self.c, (self.fsdp + k) % self.peers))

        @pl.when(self.z > 0)
        def _():
            signal(self.device(self.z - 1, self.y, self.c))

        @pl.when(self.z < self.depth - 1)
        def _():
            signal(self.device(self.z + 1, self.y, self.c))

        last = self.depth - 1
        pl.semaphore_wait(barrier, count + 2 - self.z // last - (last - self.z) // last)


def remote(src, dst, send_sem, recv_sem, target):
    return pltpu.make_async_remote_copy(
        src_ref=src,
        dst_ref=dst,
        send_sem=send_sem,
        recv_sem=recv_sem,
        device_id=target,
        device_id_type=MESH_IDS,
    )


class Swaps:
    def __init__(self, place, shifts, given, taken, send_sem, recv_sem):
        self.copies = [
            remote(
                given[i],
                taken[i],
                send_sem.at[i],
                recv_sem.at[i],
                place.device(place.z, place.y, place.c, (place.fsdp + shift) % place.peers),
            )
            for i, shift in enumerate(shifts)
        ]

    def start(self):
        for copy in self.copies:
            copy.start()

    def wait(self):
        for copy in self.copies:
            copy.wait()


def gather_kernel(place, count, shifts, *refs):
    total = count + len(shifts)
    ins, outs = refs[:count], refs[total : total + count]
    given, taken = refs[count:total], refs[total + count : 2 * total]
    near, xs, ys, cs, rc, zs, got, given_sem, taken_sem = refs[2 * total :]
    p = place.here()
    depth, tall, across = p.depth, p.tall, p.across
    p.greet(len(shifts) > 0)
    sibling = p.device(p.z, p.y, 1 - p.c)

    def unit(z, y, x):
        return (z * tall + y) * across + x

    def block(a, z, y, x):
        return outs[a].at[p.slot(z, y, p.c, x)]

    def to_z(a, src, z, x, way):
        return remote(
            src,
            block(a, z, p.y, x),
            zs.at[a, way, z * across + x],
            got.at[a, unit(z, p.y, x)],
            p.device(p.z + 2 * way - 1, p.y, p.c),
        )

    def to_y(a, src, z, x, k):
        return remote(
            src,
            block(a, z, p.y, x),
            ys.at[a],
            got.at[a, unit(z, p.y, x)],
            p.device(p.z, (p.y + k) % tall, p.c),
        )

    def to_sibling(a, src, z, y, x):
        return remote(src, block(a, z, y, x), cs.at[a], rc.at[a], sibling)

    def arrived(a, z, y, x):
        remote(block(a, z, y, x), block(a, z, y, x), cs.at[a], got.at[a, unit(z, y, x)], sibling).wait_recv()

    def spread(a, src, z, x, ways):
        for way in ways:

            @pl.when((p.z < depth - 1) if way else (p.z > 0))
            def _():
                to_z(a, src, z, x, way).start()

        for k in range(1, tall):
            to_y(a, src, z, x, k).start()
        to_sibling(a, src, z, p.y, x).start()

    def over_x(step):
        if across == 1:
            step(0)
        else:
            lax.fori_loop(0, across, lambda k, _: (step((p.x + k) % across), 0)[1], 0)

    for a in range(count):
        for k in range(1, across):
            remote(
                ins[a],
                block(a, p.z, p.y, p.x),
                xs.at[a],
                got.at[a, unit(p.z, p.y, p.x)],
                p.device(p.z, p.y, p.c, (p.x + k) % across),
            ).start()
        spread(a, ins[a], p.z, p.x, (0, 1))
        pltpu.make_async_copy(ins[a], block(a, p.z, p.y, p.x), near.at[a]).start()

    swaps = Swaps(p, shifts, given, taken, given_sem, taken_sem)
    swaps.start()
    for k in range(1, across):
        x = (p.x + k) % across
        for a in range(count):
            arrived(a, p.z, p.y, x)
            spread(a, block(a, p.z, p.y, x), p.z, x, (0, 1))

    def from_y(z):
        def step(x):
            for k in range(1, tall):
                y = (p.y + k) % tall
                for a in range(count):
                    arrived(a, z, y, x)
                    to_sibling(a, block(a, z, y, x), z, y, x).start()

        over_x(step)

    for d in range(1, depth + 1):
        if d < depth:

            @pl.when(p.z >= d)
            def _(d=d):
                def step(x):
                    for a in range(count):
                        arrived(a, p.z - d, p.y, x)
                        spread(a, block(a, p.z - d, p.y, x), p.z - d, x, (1,))

                over_x(step)

            @pl.when(p.z + d < depth)
            def _(d=d):
                def step(x):
                    for a in range(count):
                        arrived(a, p.z + d, p.y, x)
                        spread(a, block(a, p.z + d, p.y, x), p.z + d, x, (0,))

                over_x(step)

        if d == 1:
            from_y(p.z)
        else:

            @pl.when(p.z >= d - 1)
            def _(d=d):
                from_y(p.z - d + 1)

            @pl.when(p.z + d - 1 < depth)
            def _(d=d):
                from_y(p.z + d - 1)

    for a in range(count):
        pltpu.make_async_copy(ins[a], block(a, p.z, p.y, p.x), near.at[a]).wait()

        def many(number, send, recv):
            part = outs[a].at[pl.ds(0, number)]
            return remote(part, part, send.at[a], recv.at[a], sibling)

        if across > 1:
            many(across - 1, xs, rc).wait_send()
        if tall > 1:
            many((tall - 1) * depth * across, ys, rc).wait_send()
        many(p.units, cs, rc).wait()
        for z in range(depth):
            for way in (0, 1):

                @pl.when(
                    ((p.z >= z) & (p.z < depth - 1)) if way else ((p.z <= z) & (p.z > 0))
                )
                def _(z=z, way=way, a=a):
                    for x in range(across):
                        to_z(a, block(a, z, p.y, x), z, x, way).wait_send()

    swaps.wait()


def split_swaps(swapped):
    return [w for w, _ in swapped], [shift for _, shift in swapped]


def gather(shards, wide, collective_id, swapped=()):
    group, peers = lax.axis_size("expert"), lax.axis_size("fsdp")
    place = Place(group, peers, wide)
    given, shifts = split_swaps(swapped)
    count, extra = len(shards), len(given)
    dma = pltpu.SemaphoreType.DMA
    return pl.pallas_call(
        functools.partial(gather_kernel, place, count, shifts),
        out_shape=[jax.ShapeDtypeStruct((place.slots,) + s.shape, s.dtype) for s in shards]
        + [jax.ShapeDtypeStruct(s.shape, s.dtype) for s in given],
        in_specs=[pl.BlockSpec(memory_space=pl.ANY)] * (count + extra),
        out_specs=[pl.BlockSpec(memory_space=pl.ANY)] * (count + extra),
        scratch_shapes=[dma((count,))] * 5
        + [
            dma((count, 2, place.depth * place.across)),
            dma((count, place.units)),
            dma((max(extra, 1),)),
            dma((max(extra, 1),)),
        ],
        compiler_params=pltpu.CompilerParams(
            collective_id=collective_id, has_side_effects=True, vmem_limit_bytes=58 << 20
        ),
        name=f"gather{collective_id}",
    )(*shards, *given)


def scatter_kernel(place, count, shifts, *refs):
    total = count + len(shifts)
    ins, outs = refs[:count], refs[total : total + count]
    given, taken = refs[count:total], refs[total + count : 2 * total]
    refs = refs[2 * total :]
    held, side, rows_y, rows_z, rows_x = (refs[i * count : (i + 1) * count] for i in range(5))
    la, rc, yr, zr, zs, cs, ys, xs, xr, given_sem, taken_sem = refs[5 * count :]
    p = place.here()
    depth, tall, across = p.depth, p.tall, p.across
    p.greet(len(shifts) > 0)
    sibling = p.device(p.z, p.y, 1 - p.c)
    half = max(depth // 2, 1)

    def in_order(step):
        lower = 1 - p.z // half

        def right(total):
            def go(j, _):
                step(depth - 1 - j // across, (p.x + 1 + j % across) % across, 1)
                return 0

            lax.fori_loop(0, total * across, go, 0)

        def left(total):
            def go(j, _):
                step(j // across, (p.x + 1 + j % across) % across, 0)
                return 0

            lax.fori_loop(0, total * across, go, 0)

        right((depth - 1 - p.z) * lower)
        left(p.z)
        right((depth - 1 - p.z) * (1 - lower))

        def own(j, _):
            step(p.z, (p.x + 1 + j) % across, None)
            return 0

        lax.fori_loop(0, across, own, 0)

    def local(a, k, z, y, x):
        return pltpu.make_async_copy(ins[a].at[p.slot(z, y, p.c, x)], held[a].at[k, y], la.at[a, k])

    def begin(z, x, way):
        k = z * across + x
        for a in range(count):
            for y in range(tall):
                remote(
                    ins[a].at[p.slot(z, y, 1 - p.c, x)],
                    side[a].at[k, y],
                    cs.at[a],
                    rc.at[a, k],
                    sibling,
                ).start()
                local(a, k, z, y, x).start()

    def add(a, target, sources):
        rows = ins[a].shape[1]
        chunk = 16 if rows % 16 == 0 else rows

        def go(i, _):
            part = pl.ds(i * chunk, chunk)
            total = target[part].astype(jnp.float32)
            for source in sources:
                total = total + source[part].astype(jnp.float32)
            target[part] = total.astype(target.dtype)
            return 0

        lax.fori_loop(0, rows // chunk, go, 0)

    def first(z, x, way):
        k = z * across + x
        for a in range(count):
            pltpu.make_async_copy(held[a].at[k], held[a].at[k], la.at[a, k]).wait()
            remote(side[a].at[k], side[a].at[k], cs.at[a], rc.at[a, k], sibling).wait_recv()
            for j in range(1, tall):
                y = (p.y + j) % tall
                add(a, held[a].at[k, y], [side[a].at[k, y]])
                remote(
                    held[a].at[k, y],
                    rows_y[a].at[k, tall - j - 1],
                    ys.at[a],
                    yr.at[a, k],
                    p.device(p.z, y, p.c),
                ).start()
            add(a, held[a].at[k, p.y], [side[a].at[k, p.y]])

    def second(z, x, way):
        k = z * across + x
        for a in range(count):
            mine = held[a].at[k, p.y]
            if tall > 1:
                remote(rows_y[a].at[k], rows_y[a].at[k], cs.at[a], yr.at[a, k], sibling).wait_recv()
                add(a, mine, [rows_y[a].at[k, j] for j in range(tall - 1)])

            def from_z(index):
                part = rows_z[a].at[index]
                remote(part, part, cs.at[a], zr.at[a, index], sibling).wait_recv()
                add(a, mine, [part])

            def send(index, target):
                remote(mine, rows_z[a].at[index], zs.at[a, k], zr.at[a, index], target).start()

            if way is None or way == 1:
                pl.when(p.z > 0)(functools.partial(from_z, k))
            if way is None:
                pl.when(p.z < depth - 1)(functools.partial(from_z, depth * across + x))
            if way == 0:
                pl.when(p.z < depth - 1)(functools.partial(from_z, k))
            if way == 1:
                send(k, p.device(p.z + 1, p.y, p.c))
            if way == 0:
                left = p.device(p.z - 1, p.y, p.c)

                @pl.when(z == p.z - 1)
                def _():
                    send(depth * across + x, left)

                @pl.when(z < p.z - 1)
                def _():
                    send(k, left)

            if way is None and across > 1:

                @pl.when(x != p.x)
                def _():
                    remote(
                        mine,
                        rows_x[a].at[(p.x - x + across) % across - 1],
                        xs.at[a],
                        xr.at[a],
                        p.device(p.z, p.y, p.c, x),
                    ).start()

    swaps = Swaps(p, shifts, given, taken, given_sem, taken_sem)
    swaps.start()
    in_order(begin)
    in_order(first)
    in_order(second)
    k = p.z * across + p.x
    for a in range(count):
        mine = held[a].at[k, p.y]
        sources = []
        if across > 1:
            remote(rows_x[a], rows_x[a], xs.at[a], xr.at[a], sibling).wait()
            sources = [rows_x[a].at[j] for j in range(across - 1)]
        rows = ins[a].shape[1]
        chunk = 16 if rows % 16 == 0 else rows

        def go(i, _):
            part = pl.ds(i * chunk, chunk)
            total = mine[part].astype(jnp.float32)
            for source in sources:
                total = total + source[part].astype(jnp.float32)
            outs[a][part] = total
            return 0

        lax.fori_loop(0, rows // chunk, go, 0)
        remote(side[a], side[a], cs.at[a], rc.at[a, 0], sibling).wait_send()
        if tall > 1:
            remote(rows_y[a], rows_y[a], ys.at[a], rc.at[a, 0], sibling).wait_send()

        def wait_z(k, _):
            @pl.when(k // across != p.z)
            def _():
                remote(mine, rows_z[a].at[0], zs.at[a, k], rc.at[a, 0], sibling).wait_send()

            return 0

        lax.fori_loop(0, depth * across, wait_z, 0)

    swaps.wait()


def scatter(partials, wide, collective_id, swapped=()):
    group, peers = lax.axis_size("expert"), lax.axis_size("fsdp")
    place = Place(group, peers, wide)
    given, shifts = split_swaps(swapped)
    count, extra = len(partials), len(given)
    dma = pltpu.SemaphoreType.DMA
    items = place.depth * place.across

    def room(*lead):
        return [pltpu.VMEM(lead + s.shape[1:], s.dtype) for s in partials]

    return pl.pallas_call(
        functools.partial(scatter_kernel, place, count, shifts),
        out_shape=[jax.ShapeDtypeStruct(s.shape[1:], jnp.float32) for s in partials]
        + [jax.ShapeDtypeStruct(s.shape, s.dtype) for s in given],
        in_specs=[pl.BlockSpec(memory_space=pl.ANY)] * (count + extra),
        out_specs=[pl.BlockSpec(memory_space=pltpu.VMEM)] * count
        + [pl.BlockSpec(memory_space=pl.ANY)] * extra,
        scratch_shapes=room(items, place.tall)
        + room(items, place.tall)
        + room(items, max(place.tall - 1, 1))
        + room(items + place.across)
        + room(max(place.across - 1, 1))
        + [
            dma((count, items)),
            dma((count, items)),
            dma((count, items)),
            dma((count, items + place.across)),
            dma((count, items)),
            dma((count,)),
            dma((count,)),
            dma((count,)),
            dma((count,)),
            dma((max(extra, 1),)),
            dma((max(extra, 1),)),
        ],
        compiler_params=pltpu.CompilerParams(
            collective_id=collective_id, has_side_effects=True, vmem_limit_bytes=60 << 20
        ),
        name=f"scatter{collective_id}",
    )(*partials, *given)


def dot_plain(left, right):
    return jnp.dot(left, right, preferred_element_type=jnp.float32)


def dot_across(left, right):
    return lax.dot_general(left, right, (((1,), (1,)), ((), ())), preferred_element_type=jnp.float32)


def ffn_kernel(peers, sources, numbers, fill, *refs):
    hid, cot, pick, turned = refs[:4]
    gates, ups, downs = (refs[4 + i * peers : 4 + (i + 1) * peers] for i in range(3))
    router, shared_in, shared_out = refs[4 + 3 * peers : 7 + 3 * peers]
    out_part, back_part, rows, d_out, act, d_g, d_u, d_log, s_act, s_grad = refs[7 + 3 * peers :]
    f32, bf16 = jnp.float32, jnp.bfloat16
    step = pl.program_id(0)
    slots, capacity, tok_rows = pick.shape
    width = hid.shape[2] // peers
    eid, start = numbers[0], numbers[1]
    scale = fill[0]

    def length(s):
        return numbers[2 + step * sources + s]

    scales = []
    cots = []
    for s in range(sources):
        part = pl.ds(s * capacity, capacity)
        rows[part, :] = dot_plain(pick[s], hid[s]).astype(bf16)
        cots.append(dot_plain(pick[s], cot[s]))
        lane = start + lax.broadcasted_iota(jnp.int32, (1, tok_rows), 1)
        alive = jnp.where(lane < length(s), scale, 0.0)
        scales.append(jnp.sum(pick[s].astype(f32) * alive, axis=1, keepdims=True))
    row_scale = jnp.concatenate(scales, axis=0)
    row_cot = jnp.concatenate(cots, axis=0)
    rows_now = rows[...]
    logits = dot_plain(rows_now, router[...])
    top = jnp.max(logits, axis=1, keepdims=True)
    powers = jnp.exp(logits - top)
    probs = powers / jnp.sum(powers, axis=1, keepdims=True)
    own = (lax.broadcasted_iota(jnp.int32, (1, probs.shape[1]), 1) == eid).astype(f32)
    gate = jnp.sum(probs * own, axis=1, keepdims=True)

    def cut(array, r):
        return array[:, r * width : (r + 1) * width]

    def summed(terms):
        total = terms[0]
        for term in terms[1:]:
            total = total + term
        return total

    g = summed([dot_plain(cut(rows_now, r), gates[r][...]) for r in range(peers)])
    u = summed([dot_plain(cut(rows_now, r), ups[r][...]) for r in range(peers)])
    sigma = 1.0 / (1.0 + jnp.exp(-g))
    act_now = (g * sigma * u).astype(bf16)
    act[...] = act_now
    d_now = ((gate * row_scale) * row_cot).astype(bf16)
    d_out[...] = d_now
    d_gate = jnp.zeros_like(gate)
    weighted = []
    for r in range(peers):
        out = dot_plain(act_now, downs[r][...]).astype(bf16).astype(f32)
        d_gate = d_gate + jnp.sum(cut(row_cot, r) * out, axis=1, keepdims=True)
        weighted.append((gate * out).astype(bf16))
    d_gate = d_gate * row_scale
    d_act = summed([dot_across(cut(d_now, r), downs[r][...]) for r in range(peers)])
    dg_now = (d_act * u * (sigma * (1.0 + g * (1.0 - sigma)))).astype(bf16)
    du_now = (d_act * (g * sigma)).astype(bf16)
    d_g[...] = dg_now
    d_u[...] = du_now
    dl_now = (gate * d_gate * (own - probs)).astype(bf16)
    d_log[...] = dl_now
    d_rows = []
    for r in range(peers):
        total = dot_across(dg_now, gates[r][...]) + dot_across(du_now, ups[r][...])
        total = total + dot_across(dl_now, router[pl.ds(r * width, width), :])
        d_rows.append(total.astype(bf16))
    units = shared_out.shape[0]
    total_rows = sources * tok_rows
    hid_all = hid[...].reshape(total_rows, hid.shape[2])
    cot_all = cot[...].reshape(total_rows, hid.shape[2])
    both = dot_plain(hid_all, shared_in[...])
    sg, su = both[:, :units], both[:, units:]
    s_sigma = 1.0 / (1.0 + jnp.exp(-sg))
    s_now = sg * s_sigma * su
    column = lax.broadcasted_iota(jnp.int32, (tok_rows, 1), 0) + start
    alive = jnp.concatenate(
        [jnp.where(column < length(s), scale, 0.0) for s in range(sources)], axis=0
    )
    d_s = dot_across(cot_all, shared_out[...]) * alive
    s_act[...] = (s_now * alive).astype(bf16)
    s_low = s_now.astype(bf16)
    d_sg = (d_s * su * (s_sigma * (1.0 + sg * (1.0 - s_sigma)))).astype(bf16)
    d_su = (d_s * (sg * s_sigma)).astype(bf16)
    s_grad[:, pl.ds(0, units)] = d_sg
    s_grad[:, pl.ds(units, units)] = d_su
    for s in range(sources):
        part = slice(s * capacity, (s + 1) * capacity)
        span = slice(s * tok_rows, (s + 1) * tok_rows)
        for r in range(peers):
            columns = pl.ds(r * width, width)
            out_part[s, :, columns] = (
                dot_plain(turned[s], weighted[r][part])
                + dot_plain(s_low[span], shared_out[:, columns])
            ).astype(bf16)
            back_part[s, :, columns] = (
                dot_plain(turned[s], d_rows[r][part])
                + dot_across(d_sg[span], shared_in[columns, pl.ds(0, units)])
                + dot_across(d_su[span], shared_in[columns, pl.ds(units, units)])
            ).astype(bf16)


def ffn(numbers, fill, hid, cot, pick, turned, gates, ups, downs, router, shared_in, shared_out):
    group, tok_rows, dim = hid.shape
    capacity = pick.shape[1]
    peers = len(gates)
    sources = max(1, min(4, 256 // capacity))
    hidden = gates[0].shape[1]
    units = shared_out.shape[0]
    rows = sources * capacity
    bf16 = jnp.bfloat16

    def whole(array):
        return pl.BlockSpec(
            array.shape, lambda i, *_: (0,) * array.ndim, pipeline_mode=pl.Buffered(1)
        )

    def tile(*shape):
        return pl.BlockSpec(shape, lambda i, *_: (i,) + (0,) * (len(shape) - 1))

    pairs = group * capacity
    weights = [*gates, *ups, *downs, router, shared_in, shared_out]
    return pl.pallas_call(
        functools.partial(ffn_kernel, peers, sources),
        out_shape=[
            jax.ShapeDtypeStruct((group, tok_rows, dim), bf16),
            jax.ShapeDtypeStruct((group, tok_rows, dim), bf16),
            jax.ShapeDtypeStruct((pairs, dim), bf16),
            jax.ShapeDtypeStruct((pairs, dim), bf16),
            jax.ShapeDtypeStruct((pairs, hidden), bf16),
            jax.ShapeDtypeStruct((pairs, hidden), bf16),
            jax.ShapeDtypeStruct((pairs, hidden), bf16),
            jax.ShapeDtypeStruct((pairs, router.shape[1]), bf16),
            jax.ShapeDtypeStruct((group * tok_rows, units), bf16),
            jax.ShapeDtypeStruct((group * tok_rows, 2 * units), bf16),
        ],
        grid_spec=pltpu.PrefetchScalarGridSpec(
            num_scalar_prefetch=2,
            grid=(group // sources,),
            in_specs=[
                tile(sources, tok_rows, dim),
                tile(sources, tok_rows, dim),
                tile(sources, capacity, tok_rows),
                tile(sources, tok_rows, capacity),
            ]
            + [whole(w) for w in weights],
            out_specs=[
                tile(sources, tok_rows, dim),
                tile(sources, tok_rows, dim),
                tile(rows, dim),
                tile(rows, dim),
                tile(rows, hidden),
                tile(rows, hidden),
                tile(rows, hidden),
                tile(rows, router.shape[1]),
                tile(sources * tok_rows, units),
                tile(sources * tok_rows, 2 * units),
            ],
        ),
        compiler_params=pltpu.CompilerParams(vmem_limit_bytes=62 << 20),
        cost_estimate=pl.CostEstimate(
            flops=18 * pairs * dim * hidden, bytes_accessed=60 << 20, transcendentals=1 << 22
        ),
        name="ffn",
    )(numbers, fill, hid, cot, pick, turned, *weights)


def from_peers(block):
    size = lax.axis_size("fsdp")
    return [block] + [
        lax.ppermute(block, "fsdp", [(j, (j - r) % size) for j in range(size)])
        for r in range(1, size)
    ]


def sum_to_peers(term):
    size = lax.axis_size("fsdp")
    arrived = [
        lax.ppermute(term(r), "fsdp", [(j, (j + r) % size) for j in range(size)])
        for r in range(1, size)
    ]
    return arrived


def body(
    tokens,
    cotangent,
    routes,
    lengths,
    attn_gain,
    q_weight,
    kva_weight,
    kv_gain,
    kvb_weight,
    out_weight,
    ffn_gain,
    router_weight,
    shared_gate,
    shared_up,
    shared_down,
    expert_gate,
    expert_up,
    expert_down,
):
    bf16, f32 = jnp.bfloat16, jnp.float32
    tok_rows, dim = tokens.shape
    peers = lax.axis_size("fsdp")
    group = lax.axis_size("expert")
    fid, eid = lax.axis_index("fsdp"), lax.axis_index("expert")
    seq_len = tok_rows * peers
    slot_total = seq_len * group
    expert_count = router_weight.shape[1]
    capacity = max(4, 5 * tok_rows * TOPK // (4 * expert_count))
    capacity = -(-capacity // 16) * 16
    half = dim // peers
    plane_rows = group * tok_rows
    pairs = group * capacity

    def roll_in(array, axis):
        return jnp.roll(array, -fid * half, axis=axis)

    def roll_out(array, axis):
        return jnp.roll(array, fid * half, axis=axis)

    positions = fid * tok_rows + jnp.arange(tok_rows, dtype=jnp.int32)
    seq_length = lengths[0]
    valid_mask = (positions < seq_length).astype(f32)
    expert_ids = jnp.arange(expert_count, dtype=jnp.int32)
    hot_sum = jnp.sum((routes[:, :, None] == expert_ids[None, None, :]).astype(f32), axis=1)
    local_counts = jnp.sum(hot_sum * valid_mask[:, None], axis=0)

    def lane_row(vector):
        return jnp.pad(vector.astype(f32), (0, tok_rows - vector.shape[0]))[None, :]

    small = jnp.concatenate(
        [routes.T.astype(f32)]
        + [lane_row(v) for v in (attn_gain, ffn_gain, kv_gain, local_counts, lengths)]
        + [jnp.zeros((16 - TOPK - 5, tok_rows), f32)],
        axis=0,
    )
    devices = group * peers
    turns = range(1, peers)
    w_query, w_compress, w_expand, w_output, w_router, small_all, *more = gather(
        [q_weight, kva_weight, kvb_weight, out_weight, router_weight, small],
        True,
        0,
        [(expert_gate[0], -r) for r in turns] + [(expert_up[0], -r) for r in turns],
    )
    gate_parts = [expert_gate[0]] + more[: peers - 1]
    up_parts = [expert_up[0]] + more[peers - 1 :]
    w_query, w_compress, w_expand, w_output, w_router = (
        w.reshape(-1, w.shape[-1]) for w in (w_query, w_compress, w_expand, w_output, w_router)
    )
    gain_attn = small_all[:, TOPK, : attn_gain.shape[0]].reshape(-1)
    gain_ffn = small_all[:, TOPK + 1, : ffn_gain.shape[0]].reshape(-1)
    gain_latent = small_all[:, TOPK + 2, : kv_gain.shape[0]].reshape(-1)
    route_counts = jnp.sum(small_all[:, TOPK + 3, :expert_count], axis=0)
    all_lengths = small_all.reshape(group, peers, 16, tok_rows)[:, 0, TOPK + 4, 0]
    valid_total = jnp.sum(all_lengths)
    fill_scale = slot_total / valid_total
    plane_small = lax.dynamic_index_in_dim(
        small_all.reshape(group, peers, 16, tok_rows), fid, axis=1, keepdims=False
    )
    units = shared_gate.shape[1] // group
    pieces = jnp.concatenate(
        [
            shared_gate.reshape(-1, group, units),
            shared_up.reshape(-1, group, units),
        ],
        axis=2,
    ).transpose(1, 0, 2)
    pieces = lax.all_to_all(pieces, "expert", split_axis=0, concat_axis=0, tiled=True)
    gu_weight = jnp.roll(jnp.stack(from_peers(pieces)), fid, axis=0)
    gu_weight = gu_weight.transpose(1, 0, 2, 3).reshape(dim, 2 * units)
    lanes_more = -units % 128
    gu_weight = jnp.concatenate(
        [
            jnp.pad(gu_weight[:, :units], ((0, 0), (0, lanes_more))),
            jnp.pad(gu_weight[:, units:], ((0, 0), (0, lanes_more))),
        ],
        axis=1,
    )
    gu_weight = roll_in(gu_weight, 0)
    sd_weight = jnp.roll(jnp.stack(from_peers(shared_down)), fid, axis=0).reshape(units, dim)
    sd_weight = jnp.pad(roll_in(sd_weight, 1), ((0, lanes_more), (0, 0)))
    cosine, sine_vals = rope_tables(positions)
    tokens_f = tokens.astype(f32)
    normed_one, inverse_one = rms_norm(tokens_f, gain_attn)
    hidden_one = normed_one.astype(bf16)
    query_proj = lax.optimization_barrier(
        jnp.dot(hidden_one, w_query, preferred_element_type=f32)
    ).reshape(tok_rows, H, DN + DR)
    query_all = jnp.concatenate(
        [
            query_proj[..., :DN],
            rotate(query_proj[..., DN:], cosine[:, None, :], sine_vals[:, None, :]),
        ],
        axis=-1,
    ).astype(bf16)
    compressed = jnp.dot(hidden_one, w_compress, preferred_element_type=f32)
    latent_raw = compressed[:, :KVR]
    latent_norm, inverse_kv = rms_norm(latent_raw, gain_latent)
    latent = latent_norm.astype(bf16)
    key_rot = rotate(compressed[:, KVR:], cosine, sine_vals).astype(bf16)
    latent_rot = lax.all_gather(
        jnp.concatenate([latent, key_rot], axis=1), "fsdp", axis=0, tiled=True
    )
    all_latent, all_rot = latent_rot[:, :KVR], latent_rot[:, KVR:]
    keyval = jnp.dot(all_latent, w_expand, preferred_element_type=f32).astype(bf16)
    keyval = keyval.reshape(seq_len, H, DN + DV)
    key_nope = keyval[..., :DN]
    value_all = keyval[..., DN:]
    query_nope = query_all[..., :DN]
    query_rope = query_all[..., DN:]
    score_scale = (DN + DR) ** (-0.5)
    key_place = jnp.arange(seq_len, dtype=jnp.int32)
    allowed = (key_place[None, :] <= positions[:, None]) & (key_place[None, :] < seq_length)
    raw_scores = jnp.einsum(
        "thd,shd->hts", query_nope, key_nope, preferred_element_type=f32
    ) + jnp.einsum("thr,sr->hts", query_rope, all_rot, preferred_element_type=f32)
    scores = jnp.where(allowed[None], raw_scores * score_scale, masked_value)
    row_max = jnp.max(scores, axis=-1, keepdims=True)
    exp_scores = jnp.exp(scores - row_max)
    probs_attn = exp_scores / jnp.sum(exp_scores, axis=-1, keepdims=True)
    probs_low = probs_attn.astype(bf16)
    context = (
        jnp.einsum("hts,shd->thd", probs_low, value_all, preferred_element_type=f32)
        .reshape(tok_rows, H * DV)
        .astype(bf16)
    )
    residual = tokens_f + jnp.dot(context, w_output, preferred_element_type=f32)
    normed_two, inverse_two = rms_norm(residual, gain_ffn)
    hidden_two = normed_two.astype(bf16)
    hid3, cot3, *more = gather(
        [roll_in(hidden_two, 1), roll_in(cotangent, 1)],
        False,
        1,
        [(expert_down[0], -r) for r in turns],
    )
    down_parts = [expert_down[0]] + more
    hid_plane, cot_plane = hid3.reshape(plane_rows, dim), cot3.reshape(plane_rows, dim)
    router_probs = jax.nn.softmax(jnp.dot(hidden_two, w_router, preferred_element_type=f32), axis=-1)
    local_shares = jnp.sum(router_probs * valid_mask[:, None], axis=0)
    frequency = expert_count / (TOPK * valid_total) * route_counts
    d_probs_own = balance_weight * valid_mask[:, None] * frequency[None, :] / valid_total
    dlog_own = (
        router_probs * (d_probs_own - jnp.sum(router_probs * d_probs_own, axis=-1, keepdims=True))
    ).astype(bf16)
    named = jnp.any(plane_small[:, :TOPK, :] == eid.astype(f32), axis=1)
    rank = jnp.cumsum(named.astype(jnp.int32), axis=1) - 1
    slots = jnp.arange(capacity, dtype=jnp.int32)
    picker = (named[:, None, :] & (rank[:, None, :] == slots[None, :, None])).astype(bf16)
    turned = (named[:, :, None] & (rank[:, :, None] == slots[None, None, :])).astype(bf16)
    numbers = jnp.concatenate(
        [jnp.stack([eid, fid * tok_rows]).astype(jnp.int32), all_lengths.astype(jnp.int32)]
    )
    w_router_in = roll_in(w_router, 0)
    (
        out_part,
        back_part,
        rows_in,
        d_out,
        act,
        d_hidden_g,
        d_hidden_u,
        dlog_rows,
        shared_scaled,
        d_gu,
    ) = ffn(
        numbers,
        fill_scale.reshape(1),
        hid3,
        cot3,
        picker,
        turned,
        gate_parts,
        up_parts,
        down_parts,
        w_router_in,
        gu_weight,
        sd_weight,
    )

    def cut(array, r):
        return array[:, r * half : (r + 1) * half]

    def outer(left, right):
        return lax.dot_general(left, right, (((0,), (0,)), ((), ())), preferred_element_type=f32)

    def back(left, weight):
        return lax.dot_general(left, weight, (((1,), (1,)), ((), ())), preferred_element_type=f32)

    def gate_term(r):
        return outer(cut(rows_in, r), d_hidden_g)

    def up_term(r):
        return outer(cut(rows_in, r), d_hidden_u)

    def down_term(r):
        return outer(act, cut(d_out, r))

    def with_peers(term):
        arrived = sum_to_peers(lambda r: term(r).astype(bf16))
        total = term(0)
        for block in arrived:
            total = total + block.astype(f32)
        return total

    def plus(total, blocks):
        for block in blocks:
            total = total + block.astype(f32)
        return total

    d_sd = outer(shared_scaled, cot_plane)[:units]
    d_gu_weight = outer(hid_plane, d_gu)
    d_gu_weight = jnp.concatenate(
        [d_gu_weight[:, :units], d_gu_weight[:, units + lanes_more : 2 * units + lanes_more]], axis=1
    )
    d_hidden_two, out_sum, *gate_blocks = scatter(
        [back_part, out_part], False, 2, [(gate_term(r).astype(bf16), r) for r in turns]
    )
    egate_grad = plus(gate_term(0), gate_blocks)[None]
    mixed = (residual + roll_out(out_sum, 1)).astype(bf16)
    d_hidden_two = roll_out(d_hidden_two, 1) + back(dlog_own, w_router)
    router_grad = roll_out(outer(rows_in, dlog_rows), 0) + outer(hidden_two, dlog_own)
    d_gu_blocks = roll_out(d_gu_weight, 0).reshape(group, peers, dim // (group * peers), 2 * units)

    def gu_term(r):
        return lax.dynamic_index_in_dim(d_gu_blocks, (fid + r) % peers, axis=1, keepdims=False)

    gu_sum = gu_term(0)
    for block in sum_to_peers(gu_term):
        gu_sum = gu_sum + block
    gu_sum = lax.all_to_all(gu_sum, "expert", split_axis=0, concat_axis=0, tiled=True)
    gu_sum = gu_sum.transpose(1, 0, 2)
    sgate_grad = gu_sum[:, :, :units].reshape(shared_gate.shape)
    sup_grad = gu_sum[:, :, units:].reshape(shared_up.shape)
    d_sd_blocks = roll_out(d_sd, 1).reshape(peers, units // peers, dim)

    def sd_term(r):
        return lax.dynamic_index_in_dim(d_sd_blocks, (fid + r) % peers, axis=0, keepdims=False)

    sdown_grad = sd_term(0)
    for block in sum_to_peers(sd_term):
        sdown_grad = sdown_grad + block
    grad_out = cotangent.astype(f32) * (valid_mask * fill_scale)[:, None]
    d_residual, d_ffn_gain = norm_back(d_hidden_two, residual, inverse_two, gain_ffn)
    d_residual = d_residual + grad_out
    d_residual_low = d_residual.astype(bf16)
    d_output_w = outer(context, d_residual_low)
    d_context = back(d_residual_low, w_output).astype(bf16).reshape(tok_rows, H, DV)
    d_value = jnp.einsum("hts,thd->shd", probs_low, d_context, preferred_element_type=f32)
    d_weights = jnp.einsum("thd,shd->hts", d_context, value_all, preferred_element_type=f32)
    d_scores = (
        probs_attn * (d_weights - jnp.sum(probs_attn * d_weights, axis=-1, keepdims=True))
    ).astype(bf16)
    d_query_nope = score_scale * jnp.einsum(
        "hts,shd->thd", d_scores, key_nope, preferred_element_type=f32
    )
    d_query_rope = score_scale * jnp.einsum(
        "hts,sr->thr", d_scores, all_rot, preferred_element_type=f32
    )
    d_key_nope = score_scale * jnp.einsum(
        "hts,thd->shd", d_scores, query_nope, preferred_element_type=f32
    )
    d_key_rot = score_scale * jnp.einsum(
        "hts,thr->sr", d_scores, query_rope, preferred_element_type=f32
    )
    d_keyval_all = jnp.concatenate([d_key_nope, d_value], axis=-1).reshape(
        seq_len, H * (DN + DV)
    )

    def own_rows(array, r):
        return lax.dynamic_slice_in_dim(array, (fid + r) % peers * tok_rows, tok_rows, axis=0)

    own_dkeyval = with_peers(lambda r: own_rows(d_keyval_all, r))
    own_dkeyrot = with_peers(lambda r: own_rows(d_key_rot, r))
    d_keyval = own_dkeyval.astype(bf16)
    d_expand_w = outer(latent, d_keyval)
    d_latent = back(d_keyval, w_expand)
    d_latent_raw, d_latent_gain = norm_back(d_latent, latent_raw, inverse_kv, gain_latent)
    d_compressed = jnp.concatenate(
        [d_latent_raw, rotate_back(own_dkeyrot, cosine, sine_vals)], axis=-1
    ).astype(bf16)
    d_compress_w = outer(hidden_one, d_compressed)
    d_query = (
        jnp.concatenate(
            [d_query_nope, rotate_back(d_query_rope, cosine[:, None, :], sine_vals[:, None, :])],
            axis=-1,
        )
        .reshape(tok_rows, H * (DN + DR))
        .astype(bf16)
    )
    d_query_w = outer(hidden_one, d_query)
    d_hidden_one = back(d_query, w_query) + back(d_compressed, w_compress)
    d_tokens, d_attn_gain = norm_back(d_hidden_one, tokens_f, inverse_one, gain_attn)
    tokens_grad = d_tokens + d_residual
    def lanes(vector):
        piece = vector.reshape(devices, -1)
        return jnp.pad(piece, ((0, 0), (0, tok_rows - piece.shape[1])))

    small_grads = jnp.stack(
        [
            lanes(d_attn_gain),
            lanes(d_latent_gain),
            lanes(d_ffn_gain),
            lanes(jnp.tile(local_shares, devices)),
        ]
        + [jnp.zeros((devices, tok_rows), f32)] * 4,
        axis=1,
    )
    dense = [
        w.astype(bf16).reshape(devices, -1, w.shape[-1])
        for w in (d_query_w, d_compress_w, d_expand_w, d_output_w, router_grad)
    ]
    q_grad, kva_grad, kvb_grad, out_grad, router_out, smalls, *blocks = scatter(
        dense + [small_grads],
        True,
        3,
        [(up_term(r).astype(bf16), r) for r in turns]
        + [(down_term(r).astype(bf16), r) for r in turns],
    )
    eup_grad = plus(up_term(0), blocks[: peers - 1])[None]
    edown_grad = plus(down_term(0), blocks[peers - 1 :])[None]
    attn_gain_grad = smalls[0, : attn_gain.shape[0]]
    kv_gain_grad = smalls[1, : kv_gain.shape[0]]
    ffn_gain_grad = smalls[2, : ffn_gain.shape[0]]
    balance = jnp.sum(frequency * (smalls[3, :expert_count] / valid_total))
    return (
        mixed,
        tokens_grad,
        balance,
        attn_gain_grad,
        q_grad,
        kva_grad,
        kv_gain_grad,
        kvb_grad,
        out_grad,
        ffn_gain_grad,
        router_out,
        sgate_grad,
        sup_grad,
        sdown_grad,
        egate_grad,
        eup_grad,
        edown_grad,
    )


def solution(mesh):
    return jax.shard_map(
        body,
        mesh=mesh,
        in_specs=(
            P(("expert", "fsdp"), None),
            P(("expert", "fsdp"), None),
            P(("expert", "fsdp"), None),
            P("expert"),
            P(("expert", "fsdp")),
            P(("expert", "fsdp"), None),
            P(("expert", "fsdp"), None),
            P(("expert", "fsdp")),
            P(("expert", "fsdp"), None),
            P(("expert", "fsdp"), None),
            P(("expert", "fsdp")),
            P(("expert", "fsdp"), None),
            P(("expert", "fsdp"), None),
            P(("expert", "fsdp"), None),
            P(("expert", "fsdp"), None),
            P("expert", "fsdp", None),
            P("expert", "fsdp", None),
            P("expert", None, "fsdp"),
        ),
        out_specs=(
            P(("expert", "fsdp"), None),
            P(("expert", "fsdp"), None),
            P(),
            P(("expert", "fsdp")),
            P(("expert", "fsdp"), None),
            P(("expert", "fsdp"), None),
            P(("expert", "fsdp")),
            P(("expert", "fsdp"), None),
            P(("expert", "fsdp"), None),
            P(("expert", "fsdp")),
            P(("expert", "fsdp"), None),
            P(("expert", "fsdp"), None),
            P(("expert", "fsdp"), None),
            P(("expert", "fsdp"), None),
            P("expert", "fsdp", None),
            P("expert", "fsdp", None),
            P("expert", None, "fsdp"),
        ),
        check_vma=False,
    )
```

```python
import functools

import jax
import jax.numpy as jnp
from jax import lax
from jax.experimental import pallas as pl
from jax.experimental.pallas import tpu as pltpu
from jax.sharding import PartitionSpec as P

D = 2048
H = 16
DN = 128
DR = 64
DV = 128
KVR = 512
TOPK = 6


epsilon = 1e-06
balance_weight = 0.001
masked_value = -1e30


def rms_norm(vector, gain_row):
    inverse = lax.rsqrt(jnp.mean(vector * vector, axis=-1, keepdims=True) + epsilon)
    return (vector * inverse * gain_row, inverse)


def norm_back(grad_in, vector, inverse, gain_row):
    scaled = grad_in * gain_row
    gain_grad = jnp.sum(grad_in * vector * inverse, axis=0)
    vector_grad = inverse * scaled - vector * inverse**3 * jnp.mean(
        scaled * vector, axis=-1, keepdims=True
    )
    return (vector_grad, gain_grad)


def rope_tables(positions):
    half_width = DR // 2
    frequency = 10000.0 ** (-jnp.arange(half_width, dtype=jnp.float32) / half_width)
    angles = positions.astype(jnp.float32)[:, None] * frequency[None, :]
    return (jnp.cos(angles), jnp.sin(angles))


def rotate(vector, cosine, sine_vals):
    half_width = vector.shape[-1] // 2
    first_half = vector[..., :half_width]
    second_half = vector[..., half_width:]
    return jnp.concatenate(
        [
            first_half * cosine - second_half * sine_vals,
            second_half * cosine + first_half * sine_vals,
        ],
        axis=-1,
    )


def rotate_back(grad_in, cosine, sine_vals):
    half_width = grad_in.shape[-1] // 2
    first_half = grad_in[..., :half_width]
    second_half = grad_in[..., half_width:]
    return jnp.concatenate(
        [
            first_half * cosine + second_half * sine_vals,
            second_half * cosine - first_half * sine_vals,
        ],
        axis=-1,
    )


def silu_slope(vector):
    sigmoid_vals = jax.nn.sigmoid(vector)
    return sigmoid_vals * (1.0 + vector * (1.0 - sigmoid_vals))


MESH_IDS = pl.DeviceIdType.MESH


class Place:
    def __init__(self, group, peers, wide):
        self.wide = wide
        self.depth = min(4, group // 2)
        self.tall = group // 2 // self.depth
        self.across = peers if wide else 1
        self.peers = peers
        self.units = self.depth * self.tall * self.across
        self.slots = 2 * self.units

    def here(self):
        e = lax.axis_index("expert")
        self.fsdp = lax.axis_index("fsdp")
        self.c = e % 2
        self.y = e // 2 % self.tall
        self.z = e // (2 * self.tall)
        self.x = self.fsdp if self.wide else 0
        return self

    def detour(self, z):
        return (self.depth - 1) * (1 - z % 2)

    def partner(self):
        return self.z + 1 - self.z % 2 * 2

    def slot(self, z, y, c, x):
        return ((z * self.tall + y) * 2 + c) * self.across + x

    def device(self, z, y, c, x=None):
        return ((z * self.tall + y) * 2 + c, self.fsdp if x is None else x)

    def greet(self, swapping):
        barrier = pltpu.get_barrier_semaphore()
        partners = self.peers if swapping or self.wide else 1
        count = 1 + (self.tall - 1) + (partners - 1)

        def signal(target):
            pl.semaphore_signal(barrier, inc=1, device_id=target, device_id_type=MESH_IDS)

        signal(self.device(self.z, self.y, 1 - self.c))
        for k in range(1, self.tall):
            signal(self.device(self.z, (self.y + k) % self.tall, self.c))
        for k in range(1, partners):
            signal(self.device(self.z, self.y, self.c, (self.fsdp + k) % self.peers))

        @pl.when(self.z > 0)
        def _():
            signal(self.device(self.z - 1, self.y, self.c))

        @pl.when(self.z < self.depth - 1)
        def _():
            signal(self.device(self.z + 1, self.y, self.c))

        last = self.depth - 1
        pl.semaphore_wait(barrier, count + 2 - self.z // last - (last - self.z) // last)


def remote(src, dst, send_sem, recv_sem, target):
    return pltpu.make_async_remote_copy(
        src_ref=src,
        dst_ref=dst,
        send_sem=send_sem,
        recv_sem=recv_sem,
        device_id=target,
        device_id_type=MESH_IDS,
    )


class Swaps:
    def __init__(self, place, shifts, given, taken, send_sem, recv_sem):
        self.copies = [
            remote(
                given[i],
                taken[i],
                send_sem.at[i],
                recv_sem.at[i],
                place.device(place.z, place.y, place.c, (place.fsdp + shift) % place.peers),
            )
            for i, shift in enumerate(shifts)
        ]

    def start(self):
        for copy in self.copies:
            copy.start()

    def wait(self):
        for copy in self.copies:
            copy.wait()


def gather_kernel(place, count, shifts, *refs):
    total = count + len(shifts)
    ins, outs = refs[:count], refs[total : total + count]
    given, taken = refs[count:total], refs[total + count : 2 * total]
    near, xs, ys, cs, rc, zs, got, given_sem, taken_sem, es = refs[2 * total :]
    p = place.here()
    depth, tall, across = p.depth, p.tall, p.across
    p.greet(len(shifts) > 0)
    sibling = p.device(p.z, p.y, 1 - p.c)

    def unit(z, y, x):
        return (z * tall + y) * across + x

    def block(a, z, y, x):
        return outs[a].at[p.slot(z, y, p.c, x)]

    def to_z(a, src, z, x, way):
        return remote(
            src,
            block(a, z, p.y, x),
            zs.at[a, way, z * across + x],
            got.at[a, unit(z, p.y, x)],
            p.device(p.z + 2 * way - 1, p.y, p.c),
        )

    def to_y(a, src, z, x, k):
        return remote(
            src,
            block(a, z, p.y, x),
            ys.at[a],
            got.at[a, unit(z, p.y, x)],
            p.device(p.z, (p.y + k) % tall, p.c),
        )

    def to_sibling(a, src, z, y, x):
        return remote(src, block(a, z, y, x), cs.at[a], rc.at[a], sibling)

    def arrived(a, z, y, x):
        remote(block(a, z, y, x), block(a, z, y, x), cs.at[a], got.at[a, unit(z, y, x)], sibling).wait_recv()

    def spread(a, src, z, x, ways):
        for way in ways:

            @pl.when((p.z < depth - 1) if way else (p.z > 0))
            def _():
                to_z(a, src, z, x, way).start()

        @pl.when((p.c == 1) | (z != p.detour(p.z)))
        def _():
            for k in range(1, tall):
                to_y(a, src, z, x, k).start()

        to_sibling(a, src, z, p.y, x).start()

    def to_partner(a, z, y, x, k):
        return remote(
            block(a, z, y, x),
            block(a, z, y, x),
            es.at[a, x * max(tall - 1, 1) + k - 1],
            got.at[a, unit(z, y, x)],
            p.device(p.partner(), p.y, p.c),
        )

    def over_x(step):
        if across == 1:
            step(0)
        else:
            lax.fori_loop(0, across, lambda k, _: (step((p.x + k) % across), 0)[1], 0)

    for a in range(count):
        for k in range(1, across):
            remote(
                ins[a],
                block(a, p.z, p.y, p.x),
                xs.at[a],
                got.at[a, unit(p.z, p.y, p.x)],
                p.device(p.z, p.y, p.c, (p.x + k) % across),
            ).start()
        spread(a, ins[a], p.z, p.x, (0, 1))
        pltpu.make_async_copy(ins[a], block(a, p.z, p.y, p.x), near.at[a]).start()

    swaps = Swaps(p, shifts, given, taken, given_sem, taken_sem)
    swaps.start()
    for k in range(1, across):
        x = (p.x + k) % across
        for a in range(count):
            arrived(a, p.z, p.y, x)
            spread(a, block(a, p.z, p.y, x), p.z, x, (0, 1))

    def from_y(z):
        def step(x):
            for k in range(1, tall):
                y = (p.y + k) % tall
                for a in range(count):
                    arrived(a, z, y, x)

                    @pl.when((p.c == 0) & (z == p.detour(p.partner())))
                    def _(a=a, y=y, k=k):
                        to_partner(a, z, y, x, k).start()

                    to_sibling(a, block(a, z, y, x), z, y, x).start()

        over_x(step)

    for d in range(1, depth + 1):
        if d < depth:

            @pl.when(p.z >= d)
            def _(d=d):
                def step(x):
                    for a in range(count):
                        arrived(a, p.z - d, p.y, x)
                        spread(a, block(a, p.z - d, p.y, x), p.z - d, x, (1,))

                over_x(step)

            @pl.when(p.z + d < depth)
            def _(d=d):
                def step(x):
                    for a in range(count):
                        arrived(a, p.z + d, p.y, x)
                        spread(a, block(a, p.z + d, p.y, x), p.z + d, x, (0,))

                over_x(step)

        if d == 1:
            from_y(p.z)
        else:

            @pl.when(p.z >= d - 1)
            def _(d=d):
                from_y(p.z - d + 1)

            @pl.when(p.z + d - 1 < depth)
            def _(d=d):
                from_y(p.z + d - 1)

    for a in range(count):
        pltpu.make_async_copy(ins[a], block(a, p.z, p.y, p.x), near.at[a]).wait()

        def many(number, send, recv):
            part = outs[a].at[pl.ds(0, number)]
            return remote(part, part, send.at[a], recv.at[a], sibling)

        if across > 1:
            many(across - 1, xs, rc).wait_send()
        if tall > 1:

            @pl.when(p.c == 1)
            def _():
                many((tall - 1) * depth * across, ys, rc).wait_send()

            @pl.when(p.c == 0)
            def _(a=a):
                many((tall - 1) * (depth - 1) * across, ys, rc).wait_send()
                for x in range(across):
                    for k in range(1, tall):
                        to_partner(a, 0, p.y, x, k).wait_send()

        many(p.units, cs, rc).wait()
        for z in range(depth):
            for way in (0, 1):

                @pl.when(
                    ((p.z >= z) & (p.z < depth - 1)) if way else ((p.z <= z) & (p.z > 0))
                )
                def _(z=z, way=way, a=a):
                    for x in range(across):
                        to_z(a, block(a, z, p.y, x), z, x, way).wait_send()

    swaps.wait()


def split_swaps(swapped):
    return [w for w, _ in swapped], [shift for _, shift in swapped]


def gather(shards, wide, collective_id, swapped=()):
    group, peers = lax.axis_size("expert"), lax.axis_size("fsdp")
    place = Place(group, peers, wide)
    given, shifts = split_swaps(swapped)
    count, extra = len(shards), len(given)
    dma = pltpu.SemaphoreType.DMA
    return pl.pallas_call(
        functools.partial(gather_kernel, place, count, shifts),
        out_shape=[jax.ShapeDtypeStruct((place.slots,) + s.shape, s.dtype) for s in shards]
        + [jax.ShapeDtypeStruct(s.shape, s.dtype) for s in given],
        in_specs=[pl.BlockSpec(memory_space=pl.ANY)] * (count + extra),
        out_specs=[pl.BlockSpec(memory_space=pl.ANY)] * (count + extra),
        scratch_shapes=[dma((count,))] * 5
        + [
            dma((count, 2, place.depth * place.across)),
            dma((count, place.units)),
            dma((max(extra, 1),)),
            dma((max(extra, 1),)),
            dma((count, place.across * max(place.tall - 1, 1))),
        ],
        compiler_params=pltpu.CompilerParams(
            collective_id=collective_id, has_side_effects=True, vmem_limit_bytes=58 << 20
        ),
        name=f"gather{collective_id}",
    )(*shards, *given)


class Products:
    def __init__(self, lefts, rights, results, held_left, held_right, sems):
        self.parts = list(zip(lefts, rights, results, held_left, held_right))
        self.sems = sems

    def copies(self, i):
        left, right, _, held_left, held_right = self.parts[i]
        return (
            pltpu.make_async_copy(left, held_left, self.sems.at[i, 0]),
            pltpu.make_async_copy(right, held_right, self.sems.at[i, 1]),
        )

    def start(self):
        for i in range(len(self.parts)):
            for copy in self.copies(i):
                copy.start()

    def run(self, i):
        for copy in self.copies(i):
            copy.wait()
        _, _, result, left, right = self.parts[i]
        wide = left.shape[1]
        chunk = 256 if wide % 256 == 0 else 128

        def go(j, _):
            part = pl.ds(pl.multiple_of(j * chunk, chunk), chunk)
            result[part, :] = dot_turned(left[:, part], right[...]).astype(result.dtype)
            return 0

        lax.fori_loop(0, wide // chunk, go, 0)


def scatter_kernel(place, count, shifts, pairs, *refs):
    total = count + len(shifts)
    ins, given = refs[:count], refs[count:total]
    lefts, rights = refs[total : total + pairs], refs[total + pairs : total + 2 * pairs]
    refs = refs[total + 2 * pairs :]
    outs, taken, results = refs[:count], refs[count:total], refs[total : total + pairs]
    held_left, held_right = (
        refs[total + (i + 1) * pairs : total + (i + 2) * pairs] for i in range(2)
    )
    refs = refs[total + 3 * pairs :]
    held, side, rows_y, rows_z, rows_x, rows_e = (
        refs[i * count : (i + 1) * count] for i in range(6)
    )
    la, rc, yr, zr, zs, cs, ys, xs, xr, given_sem, taken_sem, es, er, product_sem = refs[6 * count :]
    p = place.here()
    depth, tall, across = p.depth, p.tall, p.across
    p.greet(len(shifts) > 0)
    sibling = p.device(p.z, p.y, 1 - p.c)
    half = max(depth // 2, 1)

    def in_order(step):
        lower = 1 - p.z // half

        def right(total, done):
            def go(j, _):
                step(depth - 1 - j // across, (p.x + 1 + j % across) % across, 1, done * across + j)
                return 0

            lax.fori_loop(0, total * across, go, 0)

        def left(total, done):
            def go(j, _):
                step(j // across, (p.x + 1 + j % across) % across, 0, done * across + j)
                return 0

            lax.fori_loop(0, total * across, go, 0)

        early = (depth - 1 - p.z) * lower
        right(early, 0)
        left(p.z, early)
        right((depth - 1 - p.z) * (1 - lower), early + p.z)

        def own(j, _):
            step(p.z, (p.x + 1 + j) % across, None, (depth - 1) * across + j)
            return 0

        lax.fori_loop(0, across, own, 0)

    def local(a, k, z, y, x):
        return pltpu.make_async_copy(ins[a].at[p.slot(z, y, p.c, x)], held[a].at[k, y], la.at[a, k])

    def begin(z, x, way, number):
        k = z * across + x
        for a in range(count):
            for y in range(tall):
                remote(
                    ins[a].at[p.slot(z, y, 1 - p.c, x)],
                    side[a].at[k, y],
                    cs.at[a],
                    rc.at[a, k],
                    sibling,
                ).start()
                local(a, k, z, y, x).start()

    def add(a, target, sources):
        rows = ins[a].shape[1]
        chunk = 16 if rows % 16 == 0 else rows

        def go(i, _):
            part = pl.ds(i * chunk, chunk)
            total = target[part].astype(jnp.float32)
            for source in sources:
                total = total + source[part].astype(jnp.float32)
            target[part] = total.astype(target.dtype)
            return 0

        lax.fori_loop(0, rows // chunk, go, 0)

    def first(z, x, way, number):
        k = z * across + x
        for a in range(count):
            pltpu.make_async_copy(held[a].at[k], held[a].at[k], la.at[a, k]).wait()
            remote(side[a].at[k], side[a].at[k], cs.at[a], rc.at[a, k], sibling).wait_recv()
            for j in range(1, tall):
                y = (p.y + j) % tall
                mine = held[a].at[k, y]

                def along_y(sources, mine=mine, j=j, y=y, a=a):
                    add(a, mine, sources)
                    remote(
                        mine,
                        rows_y[a].at[k, tall - j - 1],
                        ys.at[a],
                        yr.at[a, k],
                        p.device(p.z, y, p.c),
                    ).start()

                @pl.when((p.c == 0) & (z == p.detour(p.z)))
                def _(mine=mine, j=j, y=y, a=a):
                    add(a, mine, [side[a].at[k, y]])
                    remote(
                        mine,
                        rows_e[a].at[x, j - 1],
                        es.at[a],
                        er.at[a, x * (tall - 1) + j - 1],
                        p.device(p.partner(), p.y, p.c),
                    ).start()

                @pl.when((p.c == 0) & (z == p.detour(p.partner())))
                def _(j=j, y=y, a=a, along_y=along_y):
                    part = rows_e[a].at[x, j - 1]
                    remote(
                        part, part, cs.at[a], er.at[a, x * (tall - 1) + j - 1], sibling
                    ).wait_recv()
                    along_y([side[a].at[k, y], part])

                @pl.when((p.c == 1) | ((z != p.detour(p.z)) & (z != p.detour(p.partner()))))
                def _(y=y, a=a, along_y=along_y):
                    along_y([side[a].at[k, y]])

            add(a, held[a].at[k, p.y], [side[a].at[k, p.y]])

    products = Products(lefts, rights, results, held_left, held_right, product_sem)

    def second(z, x, way, number):
        k = z * across + x
        for i in range(pairs):
            if (way is None) == (i >= (depth - 1) * across):
                pl.when(number == i)(functools.partial(products.run, i))
        for a in range(count):
            mine = held[a].at[k, p.y]
            if tall > 1:

                @pl.when((p.c == 1) | (z != p.detour(p.z)))
                def _(a=a, mine=mine):
                    part = rows_y[a].at[k]
                    remote(part, part, cs.at[a], yr.at[a, k], sibling).wait_recv()
                    add(a, mine, [rows_y[a].at[k, j] for j in range(tall - 1)])

            def from_z(index):
                part = rows_z[a].at[index]
                remote(part, part, cs.at[a], zr.at[a, index], sibling).wait_recv()
                add(a, mine, [part])

            def send(index, target):
                remote(mine, rows_z[a].at[index], zs.at[a, k], zr.at[a, index], target).start()

            if way is None or way == 1:
                pl.when(p.z > 0)(functools.partial(from_z, k))
            if way is None:
                pl.when(p.z < depth - 1)(functools.partial(from_z, depth * across + x))
            if way == 0:
                pl.when(p.z < depth - 1)(functools.partial(from_z, k))
            if way == 1:
                send(k, p.device(p.z + 1, p.y, p.c))
            if way == 0:
                left = p.device(p.z - 1, p.y, p.c)

                @pl.when(z == p.z - 1)
                def _():
                    send(depth * across + x, left)

                @pl.when(z < p.z - 1)
                def _():
                    send(k, left)

            if way is None and across > 1:

                @pl.when(x != p.x)
                def _():
                    remote(
                        mine,
                        rows_x[a].at[(p.x - x + across) % across - 1],
                        xs.at[a],
                        xr.at[a],
                        p.device(p.z, p.y, p.c, x),
                    ).start()

    swaps = Swaps(p, shifts, given, taken, given_sem, taken_sem)
    swaps.start()
    in_order(begin)
    products.start()
    in_order(first)
    in_order(second)
    k = p.z * across + p.x
    for a in range(count):
        mine = held[a].at[k, p.y]
        sources = []
        if across > 1:
            remote(rows_x[a], rows_x[a], xs.at[a], xr.at[a], sibling).wait()
            sources = [rows_x[a].at[j] for j in range(across - 1)]
        rows = ins[a].shape[1]
        chunk = 16 if rows % 16 == 0 else rows

        def go(i, _):
            part = pl.ds(i * chunk, chunk)
            total = mine[part].astype(jnp.float32)
            for source in sources:
                total = total + source[part].astype(jnp.float32)
            outs[a][part] = total
            return 0

        lax.fori_loop(0, rows // chunk, go, 0)
        remote(side[a], side[a], cs.at[a], rc.at[a, 0], sibling).wait_send()
        if tall > 1:

            @pl.when(p.c == 1)
            def _(a=a):
                remote(rows_y[a], rows_y[a], ys.at[a], rc.at[a, 0], sibling).wait_send()

            @pl.when(p.c == 0)
            def _(a=a):
                part = rows_y[a].at[pl.ds(0, (depth - 1) * across)]
                remote(part, part, ys.at[a], rc.at[a, 0], sibling).wait_send()
                remote(rows_e[a], rows_e[a], es.at[a], rc.at[a, 0], sibling).wait_send()

        def wait_z(k, _):
            @pl.when(k // across != p.z)
            def _():
                remote(mine, rows_z[a].at[0], zs.at[a, k], rc.at[a, 0], sibling).wait_send()

            return 0

        lax.fori_loop(0, depth * across, wait_z, 0)

    swaps.wait()


def scatter(partials, wide, collective_id, swapped=(), products=()):
    group, peers = lax.axis_size("expert"), lax.axis_size("fsdp")
    place = Place(group, peers, wide)
    given, shifts = split_swaps(swapped)
    count, extra, pairs = len(partials), len(given), len(products)
    lefts, rights = [v[0] for v in products], [v[1] for v in products]
    dma = pltpu.SemaphoreType.DMA
    items = place.depth * place.across

    def room(*lead):
        return [pltpu.VMEM(lead + s.shape[1:], s.dtype) for s in partials]

    return pl.pallas_call(
        functools.partial(scatter_kernel, place, count, shifts, pairs),
        out_shape=[jax.ShapeDtypeStruct(s.shape[1:], jnp.float32) for s in partials]
        + [jax.ShapeDtypeStruct(s.shape, s.dtype) for s in given]
        + [jax.ShapeDtypeStruct((v.shape[1], w.shape[1]), kind) for v, w, kind in products],
        in_specs=[pl.BlockSpec(memory_space=pl.ANY)] * (count + extra + 2 * pairs),
        out_specs=[pl.BlockSpec(memory_space=pltpu.VMEM)] * count
        + [pl.BlockSpec(memory_space=pl.ANY)] * extra
        + [pl.BlockSpec(memory_space=pltpu.VMEM)] * pairs,
        scratch_shapes=[pltpu.VMEM(v.shape, v.dtype) for v in lefts + rights]
        + room(items, place.tall)
        + room(items, place.tall)
        + room(items, max(place.tall - 1, 1))
        + room(items + place.across)
        + room(max(place.across - 1, 1))
        + room(place.across, max(place.tall - 1, 1))
        + [
            dma((count, items)),
            dma((count, items)),
            dma((count, items)),
            dma((count, items + place.across)),
            dma((count, items)),
            dma((count,)),
            dma((count,)),
            dma((count,)),
            dma((count,)),
            dma((max(extra, 1),)),
            dma((max(extra, 1),)),
            dma((count,)),
            dma((count, place.across * max(place.tall - 1, 1))),
            dma((max(pairs, 1), 2)),
        ],
        compiler_params=pltpu.CompilerParams(
            collective_id=collective_id, has_side_effects=True, vmem_limit_bytes=60 << 20
        ),
        name=f"scatter{collective_id}",
    )(*partials, *given, *lefts, *rights)


def dot_plain(left, right):
    return jnp.dot(left, right, preferred_element_type=jnp.float32)


def dot_across(left, right):
    return lax.dot_general(left, right, (((1,), (1,)), ((), ())), preferred_element_type=jnp.float32)


def dot_turned(left, right):
    return lax.dot_general(left, right, (((0,), (0,)), ((), ())), preferred_element_type=jnp.float32)


def ffn_kernel(peers, sources, numbers, fill, *refs):
    hid, cot, ranks = refs[:3]
    gates, ups, downs = (refs[3 + i * peers : 3 + (i + 1) * peers] for i in range(3))
    router, shared_in, shared_out = refs[3 + 3 * peers : 6 + 3 * peers]
    refs = refs[6 + 3 * peers :]
    rows, d_out = refs[:peers], refs[peers : 2 * peers]
    out_part, back_part, act, d_g, d_u, d_log, s_act, s_grad = refs[2 * peers : 8 + 2 * peers]
    rows_here, cots_here = refs[8 + 2 * peers :]
    f32, bf16 = jnp.float32, jnp.bfloat16
    step = pl.program_id(0)
    tok_rows = hid.shape[1]
    capacity = rows_here.shape[0] // sources
    width = hid.shape[2] // peers
    eid, start, fid = numbers[0], numbers[1], numbers[2]
    scale = fill[0]

    def length(s):
        return numbers[3 + step * sources + s]

    def columns(r):
        return pl.ds(pl.multiple_of((fid + r) % peers * width, width), width)

    scales = []
    picks = []
    for s in range(sources):
        part = pl.ds(s * capacity, capacity)
        slot = lax.broadcasted_iota(jnp.int32, (capacity, tok_rows), 0).astype(f32)
        pick = jnp.where(ranks[s] == slot, 1.0, 0.0)
        lane = start + lax.broadcasted_iota(jnp.int32, (1, tok_rows), 1)
        alive = jnp.where(lane < length(s), scale, 0.0)
        scales.append(jnp.sum(pick * alive, axis=1, keepdims=True))
        pick = pick.astype(bf16)
        picks.append(pick)
        rows_here[part, :] = dot_plain(pick, hid[s]).astype(bf16)
        cots_here[part, :] = dot_plain(pick, cot[s]).astype(bf16)
    row_scale = jnp.concatenate(scales, axis=0)
    logits = dot_plain(rows_here[...], router[...])
    top = jnp.max(logits, axis=1, keepdims=True)
    powers = jnp.exp(logits - top)
    probs = powers / jnp.sum(powers, axis=1, keepdims=True)
    own = (lax.broadcasted_iota(jnp.int32, (1, probs.shape[1]), 1) == eid).astype(f32)
    gate = jnp.sum(probs * own, axis=1, keepdims=True)

    for r in range(peers):
        rows[r][...] = rows_here[:, columns(r)]

    def summed(terms):
        total = terms[0]
        for term in terms[1:]:
            total = total + term
        return total

    g = summed([dot_plain(rows[r][...], gates[r][...]) for r in range(peers)])
    u = summed([dot_plain(rows[r][...], ups[r][...]) for r in range(peers)])
    sigma = 1.0 / (1.0 + jnp.exp(-g))
    act_now = (g * sigma * u).astype(bf16)
    act[...] = act_now
    d_gate = jnp.zeros_like(gate)
    weighted = []
    for r in range(peers):
        out = dot_plain(act_now, downs[r][...]).astype(bf16).astype(f32)
        row_cot = cots_here[:, columns(r)].astype(f32)
        d_out[r][...] = ((gate * row_scale) * row_cot).astype(bf16)
        d_gate = d_gate + jnp.sum(row_cot * out, axis=1, keepdims=True)
        weighted.append((gate * out).astype(bf16))
    d_gate = d_gate * row_scale
    d_act = summed([dot_across(d_out[r][...], downs[r][...]) for r in range(peers)])
    dg_now = (d_act * u * (sigma * (1.0 + g * (1.0 - sigma)))).astype(bf16)
    du_now = (d_act * (g * sigma)).astype(bf16)
    d_g[...] = dg_now
    d_u[...] = du_now
    dl_now = (gate * d_gate * (own - probs)).astype(bf16)
    d_log[...] = dl_now
    d_rows = []
    for r in range(peers):
        total = dot_across(dg_now, gates[r][...]) + dot_across(du_now, ups[r][...])
        total = total + dot_across(dl_now, router[columns(r), :])
        d_rows.append(total.astype(bf16))
    units = shared_out.shape[0]
    total_rows = sources * tok_rows
    hid_all = hid[...].reshape(total_rows, hid.shape[2])
    cot_all = cot[...].reshape(total_rows, hid.shape[2])
    both = dot_plain(hid_all, shared_in[...])
    sg, su = both[:, :units], both[:, units:]
    s_sigma = 1.0 / (1.0 + jnp.exp(-sg))
    s_now = sg * s_sigma * su
    column = lax.broadcasted_iota(jnp.int32, (tok_rows, 1), 0) + start
    alive = jnp.concatenate(
        [jnp.where(column < length(s), scale, 0.0) for s in range(sources)], axis=0
    )
    d_s = dot_across(cot_all, shared_out[...]) * alive
    s_act[...] = (s_now * alive).astype(bf16)
    s_low = s_now.astype(bf16)
    d_sg = (d_s * su * (s_sigma * (1.0 + sg * (1.0 - s_sigma)))).astype(bf16)
    d_su = (d_s * (sg * s_sigma)).astype(bf16)
    s_grad[:, pl.ds(0, units)] = d_sg
    s_grad[:, pl.ds(units, units)] = d_su
    for s in range(sources):
        part = slice(s * capacity, (s + 1) * capacity)
        span = slice(s * tok_rows, (s + 1) * tok_rows)
        for r in range(peers):
            out_part[s, :, columns(r)] = (
                dot_turned(picks[s], weighted[r][part])
                + dot_plain(s_low[span], shared_out[:, columns(r)])
            ).astype(bf16)
            back_part[s, :, columns(r)] = (
                dot_turned(picks[s], d_rows[r][part])
                + dot_across(d_sg[span], shared_in[columns(r), pl.ds(0, units)])
                + dot_across(d_su[span], shared_in[columns(r), pl.ds(units, units)])
            ).astype(bf16)


def ffn(capacity, numbers, fill, hid, cot, ranks, gates, ups, downs, router, shared_in, shared_out):
    group, tok_rows, dim = hid.shape
    peers = len(gates)
    sources = max(1, min(4, 256 // capacity))
    hidden = gates[0].shape[1]
    units = shared_out.shape[0]
    rows = sources * capacity
    bf16 = jnp.bfloat16

    def whole(array):
        return pl.BlockSpec(
            array.shape, lambda i, *_: (0,) * array.ndim, pipeline_mode=pl.Buffered(1)
        )

    def tile(*shape):
        return pl.BlockSpec(shape, lambda i, *_: (i,) + (0,) * (len(shape) - 1))

    pairs = group * capacity
    weights = [*gates, *ups, *downs, router, shared_in, shared_out]
    return pl.pallas_call(
        functools.partial(ffn_kernel, peers, sources),
        out_shape=[jax.ShapeDtypeStruct((pairs, dim // peers), bf16)] * (2 * peers)
        + [
            jax.ShapeDtypeStruct((group, tok_rows, dim), bf16),
            jax.ShapeDtypeStruct((group, tok_rows, dim), bf16),
            jax.ShapeDtypeStruct((pairs, hidden), bf16),
            jax.ShapeDtypeStruct((pairs, hidden), bf16),
            jax.ShapeDtypeStruct((pairs, hidden), bf16),
            jax.ShapeDtypeStruct((pairs, router.shape[1]), bf16),
            jax.ShapeDtypeStruct((group * tok_rows, units), bf16),
            jax.ShapeDtypeStruct((group * tok_rows, 2 * units), bf16),
        ],
        grid_spec=pltpu.PrefetchScalarGridSpec(
            num_scalar_prefetch=2,
            grid=(group // sources,),
            in_specs=[
                tile(sources, tok_rows, dim),
                tile(sources, tok_rows, dim),
                tile(sources, 1, tok_rows),
            ]
            + [whole(w) for w in weights],
            out_specs=[tile(rows, dim // peers)] * (2 * peers)
            + [
                tile(sources, tok_rows, dim),
                tile(sources, tok_rows, dim),
                tile(rows, hidden),
                tile(rows, hidden),
                tile(rows, hidden),
                tile(rows, router.shape[1]),
                tile(sources * tok_rows, units),
                tile(sources * tok_rows, 2 * units),
            ],
            scratch_shapes=[pltpu.VMEM((rows, dim), bf16)] * 2,
        ),
        compiler_params=pltpu.CompilerParams(vmem_limit_bytes=62 << 20),
        cost_estimate=pl.CostEstimate(
            flops=18 * pairs * dim * hidden, bytes_accessed=60 << 20, transcendentals=1 << 22
        ),
        name="ffn",
    )(numbers, fill, hid, cot, ranks, *weights)


def from_peers(block):
    size = lax.axis_size("fsdp")
    return [block] + [
        lax.ppermute(block, "fsdp", [(j, (j - r) % size) for j in range(size)])
        for r in range(1, size)
    ]


def sum_to_peers(term):
    size = lax.axis_size("fsdp")
    arrived = [
        lax.ppermute(term(r), "fsdp", [(j, (j + r) % size) for j in range(size)])
        for r in range(1, size)
    ]
    return arrived


def body(
    tokens,
    cotangent,
    routes,
    lengths,
    attn_gain,
    q_weight,
    kva_weight,
    kv_gain,
    kvb_weight,
    out_weight,
    ffn_gain,
    router_weight,
    shared_gate,
    shared_up,
    shared_down,
    expert_gate,
    expert_up,
    expert_down,
):
    bf16, f32 = jnp.bfloat16, jnp.float32
    tok_rows, dim = tokens.shape
    peers = lax.axis_size("fsdp")
    group = lax.axis_size("expert")
    fid, eid = lax.axis_index("fsdp"), lax.axis_index("expert")
    seq_len = tok_rows * peers
    slot_total = seq_len * group
    expert_count = router_weight.shape[1]
    capacity = max(4, 5 * tok_rows * TOPK // (4 * expert_count))
    capacity = -(-capacity // 16) * 16
    half = dim // peers
    plane_rows = group * tok_rows
    pairs = group * capacity

    positions = fid * tok_rows + jnp.arange(tok_rows, dtype=jnp.int32)
    seq_length = lengths[0]
    valid_mask = (positions < seq_length).astype(f32)
    expert_ids = jnp.arange(expert_count, dtype=jnp.int32)
    hot_sum = jnp.sum((routes[:, :, None] == expert_ids[None, None, :]).astype(f32), axis=1)
    local_counts = jnp.sum(hot_sum * valid_mask[:, None], axis=0)

    def lane_row(vector):
        return jnp.pad(vector.astype(f32), (0, tok_rows - vector.shape[0]))[None, :]

    small = jnp.concatenate(
        [routes.T.astype(f32)]
        + [lane_row(v) for v in (attn_gain, ffn_gain, kv_gain, local_counts, lengths)]
        + [jnp.zeros((16 - TOPK - 5, tok_rows), f32)],
        axis=0,
    )
    devices = group * peers
    turns = range(1, peers)
    w_query, w_compress, w_expand, w_output, w_router, small_all, *more = gather(
        [q_weight, kva_weight, kvb_weight, out_weight, router_weight, small],
        True,
        0,
        [(expert_gate[0], -r) for r in turns] + [(expert_up[0], -r) for r in turns],
    )
    gate_parts = [expert_gate[0]] + more[: peers - 1]
    up_parts = [expert_up[0]] + more[peers - 1 :]
    w_query, w_compress, w_expand, w_output, w_router = (
        w.reshape(-1, w.shape[-1]) for w in (w_query, w_compress, w_expand, w_output, w_router)
    )
    gain_attn = small_all[:, TOPK, : attn_gain.shape[0]].reshape(-1)
    gain_ffn = small_all[:, TOPK + 1, : ffn_gain.shape[0]].reshape(-1)
    gain_latent = small_all[:, TOPK + 2, : kv_gain.shape[0]].reshape(-1)
    route_counts = jnp.sum(small_all[:, TOPK + 3, :expert_count], axis=0)
    all_lengths = small_all.reshape(group, peers, 16, tok_rows)[:, 0, TOPK + 4, 0]
    valid_total = jnp.sum(all_lengths)
    fill_scale = slot_total / valid_total
    plane_small = lax.dynamic_index_in_dim(
        small_all.reshape(group, peers, 16, tok_rows), fid, axis=1, keepdims=False
    )
    units = shared_gate.shape[1] // group
    lanes_more = -units % 128
    pieces = jnp.concatenate(
        [
            jnp.pad(w.reshape(-1, group, units), ((0, 0), (0, 0), (0, lanes_more)))
            for w in (shared_gate, shared_up)
        ],
        axis=2,
    ).transpose(1, 0, 2)
    pieces = lax.all_to_all(pieces, "expert", split_axis=0, concat_axis=0, tiled=True)
    sd_weight = jnp.roll(jnp.stack(from_peers(shared_down)), fid, axis=0).reshape(units, dim)
    sd_weight = jnp.pad(sd_weight, ((0, lanes_more), (0, 0)))
    cosine, sine_vals = rope_tables(positions)
    tokens_f = tokens.astype(f32)
    cot_ready, small_all = lax.optimization_barrier((cotangent, small_all))
    cot_plane = lax.all_gather(cot_ready, "expert", axis=0, tiled=True)
    normed_one, inverse_one = rms_norm(tokens_f, gain_attn)
    hidden_one = normed_one.astype(bf16)
    query_proj = lax.optimization_barrier(
        jnp.dot(hidden_one, w_query, preferred_element_type=f32)
    ).reshape(tok_rows, H, DN + DR)
    query_all = jnp.concatenate(
        [
            query_proj[..., :DN],
            rotate(query_proj[..., DN:], cosine[:, None, :], sine_vals[:, None, :]),
        ],
        axis=-1,
    ).astype(bf16)
    compressed = jnp.dot(hidden_one, w_compress, preferred_element_type=f32)
    latent_raw = compressed[:, :KVR]
    latent_norm, inverse_kv = rms_norm(latent_raw, gain_latent)
    latent = latent_norm.astype(bf16)
    key_rot = rotate(compressed[:, KVR:], cosine, sine_vals).astype(bf16)
    latent_rot = lax.all_gather(
        jnp.concatenate([latent, key_rot], axis=1), "fsdp", axis=0, tiled=True
    )
    down_own, latent_rot = lax.optimization_barrier((expert_down[0], latent_rot))
    down_parts = from_peers(down_own)
    all_latent, all_rot = latent_rot[:, :KVR], latent_rot[:, KVR:]
    keyval = jnp.dot(all_latent, w_expand, preferred_element_type=f32).astype(bf16)
    keyval = keyval.reshape(seq_len, H, DN + DV)
    key_nope = keyval[..., :DN]
    value_all = keyval[..., DN:]
    query_nope = query_all[..., :DN]
    query_rope = query_all[..., DN:]
    score_scale = (DN + DR) ** (-0.5)
    key_place = jnp.arange(seq_len, dtype=jnp.int32)
    allowed = (key_place[None, :] <= positions[:, None]) & (key_place[None, :] < seq_length)
    raw_scores = jnp.einsum(
        "thd,shd->hts", query_nope, key_nope, preferred_element_type=f32
    ) + jnp.einsum("thr,sr->hts", query_rope, all_rot, preferred_element_type=f32)
    scores = jnp.where(allowed[None], raw_scores * score_scale, masked_value)
    row_max = jnp.max(scores, axis=-1, keepdims=True)
    exp_scores = jnp.exp(scores - row_max)
    probs_attn = exp_scores / jnp.sum(exp_scores, axis=-1, keepdims=True)
    probs_low = probs_attn.astype(bf16)
    context = (
        jnp.einsum("hts,shd->thd", probs_low, value_all, preferred_element_type=f32)
        .reshape(tok_rows, H * DV)
        .astype(bf16)
    )
    residual = tokens_f + jnp.dot(context, w_output, preferred_element_type=f32)
    normed_two, inverse_two = rms_norm(residual, gain_ffn)
    hidden_two = normed_two.astype(bf16)
    hid3, *more = gather([hidden_two], False, 1, [(pieces, -r) for r in turns])
    gu_weight = jnp.roll(jnp.stack([pieces] + more), fid, axis=0)
    gu_weight = gu_weight.transpose(1, 0, 2, 3).reshape(dim, -1)
    hid_plane = hid3.reshape(plane_rows, dim)
    cot3 = cot_plane.reshape(group, tok_rows, dim)
    router_probs = jax.nn.softmax(jnp.dot(hidden_two, w_router, preferred_element_type=f32), axis=-1)
    local_shares = jnp.sum(router_probs * valid_mask[:, None], axis=0)
    frequency = expert_count / (TOPK * valid_total) * route_counts
    d_probs_own = balance_weight * valid_mask[:, None] * frequency[None, :] / valid_total
    dlog_own = (
        router_probs * (d_probs_own - jnp.sum(router_probs * d_probs_own, axis=-1, keepdims=True))
    ).astype(bf16)
    named = jnp.any(plane_small[:, :TOPK, :] == eid.astype(f32), axis=1)
    place = jnp.arange(tok_rows)
    before = (place[:, None] < place[None, :]).astype(bf16)
    ranks = jnp.dot(named.astype(bf16), before, preferred_element_type=f32)
    ranks = jnp.where(named, ranks, -1.0)[:, None, :]
    numbers = jnp.concatenate(
        [jnp.stack([eid, fid * tok_rows, fid]).astype(jnp.int32), all_lengths.astype(jnp.int32)]
    )
    made = ffn(
        capacity,
        numbers,
        fill_scale.reshape(1),
        hid3,
        cot3,
        ranks,
        gate_parts,
        up_parts,
        down_parts,
        w_router,
        gu_weight,
        sd_weight,
    )

    rows_in, d_out = made[:peers], made[peers : 2 * peers]
    out_part, back_part, act, d_hidden_g, d_hidden_u, dlog_rows, shared_scaled, d_gu = made[
        2 * peers :
    ]

    def outer(left, right):
        return lax.dot_general(left, right, (((0,), (0,)), ((), ())), preferred_element_type=f32)

    def back(left, weight):
        return lax.dot_general(left, weight, (((1,), (1,)), ((), ())), preferred_element_type=f32)

    def gate_term(r):
        return outer(rows_in[r], d_hidden_g)

    def up_term(r):
        return outer(rows_in[r], d_hidden_u)

    def down_term(r):
        return outer(act, d_out[r])

    def with_peers(term):
        arrived = sum_to_peers(lambda r: term(r).astype(bf16))
        total = term(0)
        for block in arrived:
            total = total + block.astype(f32)
        return total

    def plus(total, blocks):
        for block in blocks:
            total = total + block.astype(f32)
        return total

    d_hidden_two, *more = scatter(
        [back_part],
        False,
        2,
        [(gate_term(r).astype(bf16), r) for r in turns],
        [
            (hid_plane, d_gu, bf16),
            (shared_scaled, cot_plane, bf16),
            (rows_in[1], d_hidden_u, bf16),
            (act, d_out[1], bf16),
        ]
        if peers == 2
        else [],
    )
    gate_blocks = more[: peers - 1]
    if peers == 2:
        d_gu_weight, d_sd, *others = more[1:]
    else:
        d_gu_weight = outer(hid_plane, d_gu).astype(bf16)
        d_sd = outer(shared_scaled, cot_plane).astype(bf16)
        others = [up_term(r).astype(bf16) for r in turns]
        others = others + [down_term(r).astype(bf16) for r in turns]
    d_sd = d_sd[:units]
    out_part, d_hidden_two = lax.optimization_barrier((out_part, d_hidden_two))
    out_sum = lax.psum_scatter(
        out_part.reshape(plane_rows, dim), "expert", scatter_dimension=0, tiled=True
    )
    egate_grad = plus(gate_term(0), gate_blocks)[None]
    d_hidden_two = d_hidden_two + back(dlog_own, w_router)
    router_parts = jnp.stack([outer(rows_in[r], dlog_rows) for r in range(peers)])
    router_grad = jnp.roll(router_parts, fid, axis=0).reshape(dim, -1) + outer(hidden_two, dlog_own)
    d_gu_blocks = d_gu_weight.reshape(group, peers, dim // (group * peers), -1)
    d_sd_blocks = d_sd.reshape(peers, units // peers, dim)

    def gu_term(r):
        return lax.dynamic_index_in_dim(d_gu_blocks, (fid + r) % peers, axis=1, keepdims=False)

    def sd_term(r):
        return lax.dynamic_index_in_dim(d_sd_blocks, (fid + r) % peers, axis=0, keepdims=False)

    gu_sum = plus(gu_term(0).astype(f32), sum_to_peers(gu_term)).astype(bf16)
    sdown_grad = plus(sd_term(0).astype(f32), sum_to_peers(sd_term))
    grad_out = cotangent.astype(f32) * (valid_mask * fill_scale)[:, None]
    d_residual, d_ffn_gain = norm_back(d_hidden_two, residual, inverse_two, gain_ffn)
    d_residual = d_residual + grad_out
    d_residual_low = d_residual.astype(bf16)
    d_output_w = outer(context, d_residual_low)
    d_context = back(d_residual_low, w_output).astype(bf16).reshape(tok_rows, H, DV)
    d_value = jnp.einsum("hts,thd->shd", probs_low, d_context, preferred_element_type=f32)
    d_weights = jnp.einsum("thd,shd->hts", d_context, value_all, preferred_element_type=f32)
    d_scores = (
        probs_attn * (d_weights - jnp.sum(probs_attn * d_weights, axis=-1, keepdims=True))
    ).astype(bf16)
    d_query_nope = score_scale * jnp.einsum(
        "hts,shd->thd", d_scores, key_nope, preferred_element_type=f32
    )
    d_query_rope = score_scale * jnp.einsum(
        "hts,sr->thr", d_scores, all_rot, preferred_element_type=f32
    )
    d_key_nope = score_scale * jnp.einsum(
        "hts,thd->shd", d_scores, query_nope, preferred_element_type=f32
    )
    d_key_rot = score_scale * jnp.einsum(
        "hts,thr->sr", d_scores, query_rope, preferred_element_type=f32
    )
    d_keyval_all = jnp.concatenate([d_key_nope, d_value], axis=-1).reshape(
        seq_len, H * (DN + DV)
    )

    def own_rows(array, r):
        return lax.dynamic_slice_in_dim(array, (fid + r) % peers * tok_rows, tok_rows, axis=0)

    own_dkeyval = with_peers(lambda r: own_rows(d_keyval_all, r))
    own_dkeyrot = with_peers(lambda r: own_rows(d_key_rot, r))
    gu_sum, own_dkeyval = lax.optimization_barrier((gu_sum, own_dkeyval))
    gu_sum = lax.all_to_all(gu_sum, "expert", split_axis=0, concat_axis=0, tiled=True)
    d_keyval = own_dkeyval.astype(bf16)
    d_expand_w = outer(latent, d_keyval)
    d_latent = back(d_keyval, w_expand)
    d_latent_raw, d_latent_gain = norm_back(d_latent, latent_raw, inverse_kv, gain_latent)
    d_compressed = jnp.concatenate(
        [d_latent_raw, rotate_back(own_dkeyrot, cosine, sine_vals)], axis=-1
    ).astype(bf16)
    d_compress_w = outer(hidden_one, d_compressed)
    d_query = (
        jnp.concatenate(
            [d_query_nope, rotate_back(d_query_rope, cosine[:, None, :], sine_vals[:, None, :])],
            axis=-1,
        )
        .reshape(tok_rows, H * (DN + DR))
        .astype(bf16)
    )
    d_query_w = outer(hidden_one, d_query)
    d_hidden_one = back(d_query, w_query) + back(d_compressed, w_compress)
    d_tokens, d_attn_gain = norm_back(d_hidden_one, tokens_f, inverse_one, gain_attn)
    tokens_grad = d_tokens + d_residual
    def lanes(vector):
        piece = vector.reshape(devices, -1)
        return jnp.pad(piece, ((0, 0), (0, tok_rows - piece.shape[1])))

    small_grads = jnp.stack(
        [
            lanes(d_attn_gain),
            lanes(d_latent_gain),
            lanes(d_ffn_gain),
            lanes(jnp.tile(local_shares, devices)),
        ]
        + [jnp.zeros((devices, tok_rows), f32)] * 4,
        axis=1,
    )
    dense = [
        w.astype(bf16).reshape(devices, -1, w.shape[-1])
        for w in (d_query_w, d_compress_w, d_expand_w, d_output_w, router_grad)
    ]
    q_grad, kva_grad, kvb_grad, out_grad, router_out, smalls, *blocks = scatter(
        dense + [small_grads],
        True,
        3,
        [(w, r) for w, r in zip(others, [*turns, *turns])],
    )
    gu_sum, out_sum, smalls = lax.optimization_barrier((gu_sum, out_sum, smalls))
    mixed = (residual + out_sum.astype(f32)).astype(bf16)
    gu_sum = gu_sum.astype(f32).transpose(1, 0, 2)
    sgate_grad = gu_sum[:, :, :units].reshape(shared_gate.shape)
    sup_grad = gu_sum[:, :, units + lanes_more : 2 * units + lanes_more].reshape(shared_up.shape)
    eup_grad = plus(up_term(0), blocks[: peers - 1])[None]
    edown_grad = plus(down_term(0), blocks[peers - 1 :])[None]
    attn_gain_grad = smalls[0, : attn_gain.shape[0]]
    kv_gain_grad = smalls[1, : kv_gain.shape[0]]
    ffn_gain_grad = smalls[2, : ffn_gain.shape[0]]
    balance = jnp.sum(frequency * (smalls[3, :expert_count] / valid_total))
    return (
        mixed,
        tokens_grad,
        balance,
        attn_gain_grad,
        q_grad,
        kva_grad,
        kv_gain_grad,
        kvb_grad,
        out_grad,
        ffn_gain_grad,
        router_out,
        sgate_grad,
        sup_grad,
        sdown_grad,
        egate_grad,
        eup_grad,
        edown_grad,
    )


def solution(mesh):
    return jax.shard_map(
        body,
        mesh=mesh,
        in_specs=(
            P(("expert", "fsdp"), None),
            P(("expert", "fsdp"), None),
            P(("expert", "fsdp"), None),
            P("expert"),
            P(("expert", "fsdp")),
            P(("expert", "fsdp"), None),
            P(("expert", "fsdp"), None),
            P(("expert", "fsdp")),
            P(("expert", "fsdp"), None),
            P(("expert", "fsdp"), None),
            P(("expert", "fsdp")),
            P(("expert", "fsdp"), None),
            P(("expert", "fsdp"), None),
            P(("expert", "fsdp"), None),
            P(("expert", "fsdp"), None),
            P("expert", "fsdp", None),
            P("expert", "fsdp", None),
            P("expert", None, "fsdp"),
        ),
        out_specs=(
            P(("expert", "fsdp"), None),
            P(("expert", "fsdp"), None),
            P(),
            P(("expert", "fsdp")),
            P(("expert", "fsdp"), None),
            P(("expert", "fsdp"), None),
            P(("expert", "fsdp")),
            P(("expert", "fsdp"), None),
            P(("expert", "fsdp"), None),
            P(("expert", "fsdp")),
            P(("expert", "fsdp"), None),
            P(("expert", "fsdp"), None),
            P(("expert", "fsdp"), None),
            P(("expert", "fsdp"), None),
            P("expert", "fsdp", None),
            P("expert", "fsdp", None),
            P("expert", None, "fsdp"),
        ),
        check_vma=False,
    )
```

```python
import functools

import jax
import jax.numpy as jnp
from jax import lax
from jax.experimental import pallas as pl
from jax.experimental.pallas import tpu as pltpu
from jax.sharding import PartitionSpec as P

D = 2048
H = 16
DN = 128
DR = 64
DV = 128
KVR = 512
TOPK = 6


epsilon = 1e-06
balance_weight = 0.001
masked_value = -1e30


def rms_norm(vector, gain_row):
    inverse = lax.rsqrt(jnp.mean(vector * vector, axis=-1, keepdims=True) + epsilon)
    return (vector * inverse * gain_row, inverse)


def norm_back(grad_in, vector, inverse, gain_row):
    scaled = grad_in * gain_row
    gain_grad = jnp.sum(grad_in * vector * inverse, axis=0)
    vector_grad = inverse * scaled - vector * inverse**3 * jnp.mean(
        scaled * vector, axis=-1, keepdims=True
    )
    return (vector_grad, gain_grad)


def rope_tables(positions):
    half_width = DR // 2
    frequency = 10000.0 ** (-jnp.arange(half_width, dtype=jnp.float32) / half_width)
    angles = positions.astype(jnp.float32)[:, None] * frequency[None, :]
    return (jnp.cos(angles), jnp.sin(angles))


def rotate(vector, cosine, sine_vals):
    half_width = vector.shape[-1] // 2
    first_half = vector[..., :half_width]
    second_half = vector[..., half_width:]
    return jnp.concatenate(
        [
            first_half * cosine - second_half * sine_vals,
            second_half * cosine + first_half * sine_vals,
        ],
        axis=-1,
    )


def rotate_back(grad_in, cosine, sine_vals):
    half_width = grad_in.shape[-1] // 2
    first_half = grad_in[..., :half_width]
    second_half = grad_in[..., half_width:]
    return jnp.concatenate(
        [
            first_half * cosine + second_half * sine_vals,
            second_half * cosine - first_half * sine_vals,
        ],
        axis=-1,
    )


def silu_slope(vector):
    sigmoid_vals = jax.nn.sigmoid(vector)
    return sigmoid_vals * (1.0 + vector * (1.0 - sigmoid_vals))


MESH_IDS = pl.DeviceIdType.MESH


class Place:
    def __init__(self, group, peers, wide):
        self.wide = wide
        self.depth = min(4, group // 2)
        self.tall = group // 2 // self.depth
        self.across = peers if wide else 1
        self.peers = peers
        self.units = self.depth * self.tall * self.across
        self.slots = 2 * self.units

    def here(self):
        e = lax.axis_index("expert")
        self.fsdp = lax.axis_index("fsdp")
        self.c = e % 2
        self.y = e // 2 % self.tall
        self.z = e // (2 * self.tall)
        self.x = self.fsdp if self.wide else 0
        return self

    def detour(self, z):
        return (self.depth - 1) * (1 - z % 2)

    def partner(self):
        return self.z + 1 - self.z % 2 * 2

    def greet_peers(self):
        barrier = pltpu.get_barrier_semaphore()
        for k in range(1, self.peers):
            pl.semaphore_signal(
                barrier,
                inc=1,
                device_id=self.device(self.z, self.y, self.c, (self.fsdp + k) % self.peers),
                device_id_type=MESH_IDS,
            )
        pl.semaphore_wait(barrier, self.peers - 1)

    def slot(self, z, y, c, x):
        return ((z * self.tall + y) * 2 + c) * self.across + x

    def device(self, z, y, c, x=None):
        return ((z * self.tall + y) * 2 + c, self.fsdp if x is None else x)

    def greet(self, swapping):
        barrier = pltpu.get_barrier_semaphore()
        partners = self.peers if swapping or self.wide else 1
        count = 1 + (self.tall - 1) + (partners - 1)

        def signal(target):
            pl.semaphore_signal(barrier, inc=1, device_id=target, device_id_type=MESH_IDS)

        signal(self.device(self.z, self.y, 1 - self.c))
        for k in range(1, self.tall):
            signal(self.device(self.z, (self.y + k) % self.tall, self.c))
        for k in range(1, partners):
            signal(self.device(self.z, self.y, self.c, (self.fsdp + k) % self.peers))

        @pl.when(self.z > 0)
        def _():
            signal(self.device(self.z - 1, self.y, self.c))

        @pl.when(self.z < self.depth - 1)
        def _():
            signal(self.device(self.z + 1, self.y, self.c))

        last = self.depth - 1
        pl.semaphore_wait(barrier, count + 2 - self.z // last - (last - self.z) // last)


def remote(src, dst, send_sem, recv_sem, target):
    return pltpu.make_async_remote_copy(
        src_ref=src,
        dst_ref=dst,
        send_sem=send_sem,
        recv_sem=recv_sem,
        device_id=target,
        device_id_type=MESH_IDS,
    )


class Swaps:
    def __init__(self, place, shifts, given, taken, send_sem, recv_sem):
        self.copies = [
            remote(
                given[i],
                taken[i],
                send_sem.at[i],
                recv_sem.at[i],
                place.device(place.z, place.y, place.c, (place.fsdp + shift) % place.peers),
            )
            for i, shift in enumerate(shifts)
        ]

    def start(self):
        for copy in self.copies:
            copy.start()

    def wait(self):
        for copy in self.copies:
            copy.wait()


def gather_kernel(place, count, shifts, *refs):
    total = count + len(shifts)
    ins, outs = refs[:count], refs[total : total + count]
    given, taken = refs[count:total], refs[total + count : 2 * total]
    near, xs, ys, cs, rc, zs, got, given_sem, taken_sem, es = refs[2 * total :]
    p = place.here()
    depth, tall, across = p.depth, p.tall, p.across
    p.greet(len(shifts) > 0)
    sibling = p.device(p.z, p.y, 1 - p.c)

    def unit(z, y, x):
        return (z * tall + y) * across + x

    def block(a, z, y, x):
        return outs[a].at[p.slot(z, y, p.c, x)]

    def to_z(a, src, z, x, way):
        return remote(
            src,
            block(a, z, p.y, x),
            zs.at[a, way, z * across + x],
            got.at[a, unit(z, p.y, x)],
            p.device(p.z + 2 * way - 1, p.y, p.c),
        )

    def to_y(a, src, z, x, k):
        return remote(
            src,
            block(a, z, p.y, x),
            ys.at[a],
            got.at[a, unit(z, p.y, x)],
            p.device(p.z, (p.y + k) % tall, p.c),
        )

    def to_sibling(a, src, z, y, x):
        return remote(src, block(a, z, y, x), cs.at[a], rc.at[a], sibling)

    def arrived(a, z, y, x):
        remote(block(a, z, y, x), block(a, z, y, x), cs.at[a], got.at[a, unit(z, y, x)], sibling).wait_recv()

    def spread(a, src, z, x, ways):
        for way in ways:

            @pl.when((p.z < depth - 1) if way else (p.z > 0))
            def _():
                to_z(a, src, z, x, way).start()

        @pl.when((p.c == 1) | (z != p.detour(p.z)))
        def _():
            for k in range(1, tall):
                to_y(a, src, z, x, k).start()

        to_sibling(a, src, z, p.y, x).start()

    def to_partner(a, z, y, x, k):
        return remote(
            block(a, z, y, x),
            block(a, z, y, x),
            es.at[a, x * max(tall - 1, 1) + k - 1],
            got.at[a, unit(z, y, x)],
            p.device(p.partner(), p.y, p.c),
        )

    def over_x(step):
        if across == 1:
            step(0)
        else:
            lax.fori_loop(0, across, lambda k, _: (step((p.x + k) % across), 0)[1], 0)

    for a in range(count):
        for k in range(1, across):
            remote(
                ins[a],
                block(a, p.z, p.y, p.x),
                xs.at[a],
                got.at[a, unit(p.z, p.y, p.x)],
                p.device(p.z, p.y, p.c, (p.x + k) % across),
            ).start()
        spread(a, ins[a], p.z, p.x, (0, 1))
        pltpu.make_async_copy(ins[a], block(a, p.z, p.y, p.x), near.at[a]).start()

    swaps = Swaps(p, shifts, given, taken, given_sem, taken_sem)
    swaps.start()
    for k in range(1, across):
        x = (p.x + k) % across
        for a in range(count):
            arrived(a, p.z, p.y, x)
            spread(a, block(a, p.z, p.y, x), p.z, x, (0, 1))

    def from_y(z):
        def step(x):
            for k in range(1, tall):
                y = (p.y + k) % tall
                for a in range(count):
                    arrived(a, z, y, x)

                    @pl.when((p.c == 0) & (z == p.detour(p.partner())))
                    def _(a=a, y=y, k=k):
                        to_partner(a, z, y, x, k).start()

                    to_sibling(a, block(a, z, y, x), z, y, x).start()

        over_x(step)

    for d in range(1, depth + 1):
        if d < depth:

            @pl.when(p.z >= d)
            def _(d=d):
                def step(x):
                    for a in range(count):
                        arrived(a, p.z - d, p.y, x)
                        spread(a, block(a, p.z - d, p.y, x), p.z - d, x, (1,))

                over_x(step)

            @pl.when(p.z + d < depth)
            def _(d=d):
                def step(x):
                    for a in range(count):
                        arrived(a, p.z + d, p.y, x)
                        spread(a, block(a, p.z + d, p.y, x), p.z + d, x, (0,))

                over_x(step)

        if d == 1:
            from_y(p.z)
        else:

            @pl.when(p.z >= d - 1)
            def _(d=d):
                from_y(p.z - d + 1)

            @pl.when(p.z + d - 1 < depth)
            def _(d=d):
                from_y(p.z + d - 1)

    for a in range(count):
        pltpu.make_async_copy(ins[a], block(a, p.z, p.y, p.x), near.at[a]).wait()

        def many(number, send, recv):
            part = outs[a].at[pl.ds(0, number)]
            return remote(part, part, send.at[a], recv.at[a], sibling)

        if across > 1:
            many(across - 1, xs, rc).wait_send()
        if tall > 1:

            @pl.when(p.c == 1)
            def _():
                many((tall - 1) * depth * across, ys, rc).wait_send()

            @pl.when(p.c == 0)
            def _(a=a):
                many((tall - 1) * (depth - 1) * across, ys, rc).wait_send()
                for x in range(across):
                    for k in range(1, tall):
                        to_partner(a, 0, p.y, x, k).wait_send()

        many(p.units, cs, rc).wait()
        for z in range(depth):
            for way in (0, 1):

                @pl.when(
                    ((p.z >= z) & (p.z < depth - 1)) if way else ((p.z <= z) & (p.z > 0))
                )
                def _(z=z, way=way, a=a):
                    for x in range(across):
                        to_z(a, block(a, z, p.y, x), z, x, way).wait_send()

    swaps.wait()


def split_swaps(swapped):
    return [w for w, _ in swapped], [shift for _, shift in swapped]


def gather(shards, wide, collective_id, swapped=()):
    group, peers = lax.axis_size("expert"), lax.axis_size("fsdp")
    place = Place(group, peers, wide)
    given, shifts = split_swaps(swapped)
    count, extra = len(shards), len(given)
    dma = pltpu.SemaphoreType.DMA
    return pl.pallas_call(
        functools.partial(gather_kernel, place, count, shifts),
        out_shape=[jax.ShapeDtypeStruct((place.slots,) + s.shape, s.dtype) for s in shards]
        + [jax.ShapeDtypeStruct(s.shape, s.dtype) for s in given],
        in_specs=[pl.BlockSpec(memory_space=pl.ANY)] * (count + extra),
        out_specs=[pl.BlockSpec(memory_space=pl.ANY)] * (count + extra),
        scratch_shapes=[dma((count,))] * 5
        + [
            dma((count, 2, place.depth * place.across)),
            dma((count, place.units)),
            dma((max(extra, 1),)),
            dma((max(extra, 1),)),
            dma((count, place.across * max(place.tall - 1, 1))),
        ],
        compiler_params=pltpu.CompilerParams(
            collective_id=collective_id, has_side_effects=True, vmem_limit_bytes=58 << 20
        ),
        name=f"gather{collective_id}",
    )(*shards, *given)


def chunk_of(left):
    return 256 if left.shape[1] % 256 == 0 else 128


class Products:
    def __init__(self, lefts, rights, results, refs):
        count = len(lefts)
        held_left, held_right, ready = refs[:count], refs[count : 2 * count], refs[2 * count : 3 * count]
        self.parts = list(zip(lefts, rights, results, held_left, held_right, ready))
        if count:
            self.in_sems, self.out_sems = refs[3 * count :]

    def copies(self, i):
        left, right, _, held_left, held_right, _ = self.parts[i]
        return (
            pltpu.make_async_copy(left, held_left, self.in_sems.at[i, 0]),
            pltpu.make_async_copy(right, held_right, self.in_sems.at[i, 1]),
        )

    def start(self):
        for i in range(len(self.parts)):
            for copy in self.copies(i):
                copy.start()

    def run(self, i):
        for copy in self.copies(i):
            copy.wait()
        _, _, result, left, right, ready = self.parts[i]
        chunk = chunk_of(left)
        steps = left.shape[1] // chunk

        def leave(j):
            return pltpu.make_async_copy(
                ready.at[j % 2],
                result.at[pl.ds(pl.multiple_of(j * chunk, chunk), chunk)],
                self.out_sems.at[i, j % 2],
            )

        def go(j, _):
            @pl.when(j >= 2)
            def _():
                leave(j - 2).wait()

            part = pl.ds(pl.multiple_of(j * chunk, chunk), chunk)
            ready[j % 2] = dot_turned(left[:, part], right[...]).astype(ready.dtype)
            leave(j).start()
            return 0

        lax.fori_loop(0, steps, go, 0)
        for j in range(max(steps - 2, 0), steps):
            leave(j).wait()


def products_room(products):
    room = [pltpu.VMEM(v[0].shape, v[0].dtype) for v in products]
    room = room + [pltpu.VMEM(v[1].shape, v[1].dtype) for v in products]
    room = room + [pltpu.VMEM((2, chunk_of(v), w.shape[1]), jnp.bfloat16) for v, w in products]
    if products:
        room = room + [pltpu.SemaphoreType.DMA((len(products), 2))] * 2
    return room


def products_shapes(products):
    return [jax.ShapeDtypeStruct((v.shape[1], w.shape[1]), jnp.bfloat16) for v, w in products]


def exchange_kernel(place, shifts, pairs, *refs):
    extra = len(shifts)
    given, refs = refs[:extra], refs[extra:]
    lefts, rights, refs = refs[:pairs], refs[pairs : 2 * pairs], refs[2 * pairs :]
    taken, results, refs = refs[:extra], refs[extra : extra + pairs], refs[extra + pairs :]
    p = place.here()
    p.greet_peers()
    swaps = Swaps(p, shifts, given, taken, *refs[:2])
    swaps.start()
    products = Products(lefts, rights, results, refs[2:])
    products.start()
    for i in range(pairs):
        products.run(i)
    swaps.wait()


def exchange(collective_id, swapped, products):
    place = Place(lax.axis_size("expert"), lax.axis_size("fsdp"), False)
    given, shifts = split_swaps(swapped)
    extra, pairs = len(given), len(products)
    lefts, rights = [v for v, _ in products], [w for _, w in products]
    return pl.pallas_call(
        functools.partial(exchange_kernel, place, shifts, pairs),
        out_shape=[jax.ShapeDtypeStruct(s.shape, s.dtype) for s in given]
        + products_shapes(products),
        in_specs=[pl.BlockSpec(memory_space=pl.ANY)] * (extra + 2 * pairs),
        out_specs=[pl.BlockSpec(memory_space=pl.ANY)] * (extra + pairs),
        scratch_shapes=[pltpu.SemaphoreType.DMA((extra,))] * 2 + products_room(products),
        compiler_params=pltpu.CompilerParams(
            collective_id=collective_id, has_side_effects=True, vmem_limit_bytes=56 << 20
        ),
        name=f"exchange{collective_id}",
    )(*given, *lefts, *rights)


def outer_kernel(count, *refs):
    for i in range(count):
        left, right, result = refs[i], refs[count + i], refs[2 * count + i]
        chunk = chunk_of(left)

        def go(j, _):
            part = pl.ds(pl.multiple_of(j * chunk, chunk), chunk)
            result[part, :] = dot_turned(left[:, part], right[...]).astype(result.dtype)
            return 0

        lax.fori_loop(0, left.shape[1] // chunk, go, 0)


def outer_products(products):
    return pl.pallas_call(
        functools.partial(outer_kernel, len(products)),
        out_shape=products_shapes(products),
        in_specs=[pl.BlockSpec(memory_space=pltpu.VMEM)] * (2 * len(products)),
        out_specs=[pl.BlockSpec(memory_space=pltpu.VMEM)] * len(products),
        compiler_params=pltpu.CompilerParams(vmem_limit_bytes=32 << 20),
        name="outer",
    )(*[v for v, _ in products], *[w for _, w in products])


def scatter_kernel(place, count, shifts, pairs, *refs):
    total = count + len(shifts)
    ins, given = refs[:count], refs[count:total]
    lefts, rights = refs[total : total + pairs], refs[total + pairs : total + 2 * pairs]
    refs = refs[total + 2 * pairs :]
    outs, taken, results = refs[:count], refs[count:total], refs[total : total + pairs]
    refs = refs[total + pairs :]
    held, side, rows_y, rows_z, rows_x, rows_e = (
        refs[i * count : (i + 1) * count] for i in range(6)
    )
    la, rc, yr, zr, zs, cs, ys, xs, xr, given_sem, taken_sem, es, er, *room = refs[6 * count :]
    p = place.here()
    depth, tall, across = p.depth, p.tall, p.across
    p.greet(len(shifts) > 0)
    sibling = p.device(p.z, p.y, 1 - p.c)
    half = max(depth // 2, 1)

    def in_order(step):
        lower = 1 - p.z // half

        def right(total, done):
            def go(j, _):
                step(depth - 1 - j // across, (p.x + 1 + j % across) % across, 1, done * across + j)
                return 0

            lax.fori_loop(0, total * across, go, 0)

        def left(total, done):
            def go(j, _):
                step(j // across, (p.x + 1 + j % across) % across, 0, done * across + j)
                return 0

            lax.fori_loop(0, total * across, go, 0)

        early = (depth - 1 - p.z) * lower
        right(early, 0)
        left(p.z, early)
        right((depth - 1 - p.z) * (1 - lower), early + p.z)

        def own(j, _):
            step(p.z, (p.x + 1 + j) % across, None, (depth - 1) * across + j)
            return 0

        lax.fori_loop(0, across, own, 0)

    def local(a, k, z, y, x):
        return pltpu.make_async_copy(ins[a].at[p.slot(z, y, p.c, x)], held[a].at[k, y], la.at[a, k])

    def begin(z, x, way, number):
        k = z * across + x
        for a in range(count):
            for y in range(tall):
                remote(
                    ins[a].at[p.slot(z, y, 1 - p.c, x)],
                    side[a].at[k, y],
                    cs.at[a],
                    rc.at[a, k],
                    sibling,
                ).start()
                local(a, k, z, y, x).start()

    def add(a, target, sources):
        rows = ins[a].shape[1]
        chunk = 16 if rows % 16 == 0 else rows

        def go(i, _):
            part = pl.ds(i * chunk, chunk)
            total = target[part].astype(jnp.float32)
            for source in sources:
                total = total + source[part].astype(jnp.float32)
            target[part] = total.astype(target.dtype)
            return 0

        lax.fori_loop(0, rows // chunk, go, 0)

    def first(z, x, way, number):
        k = z * across + x
        for a in range(count):
            pltpu.make_async_copy(held[a].at[k], held[a].at[k], la.at[a, k]).wait()
            remote(side[a].at[k], side[a].at[k], cs.at[a], rc.at[a, k], sibling).wait_recv()
            for j in range(1, tall):
                y = (p.y + j) % tall
                mine = held[a].at[k, y]

                def along_y(sources, mine=mine, j=j, y=y, a=a):
                    add(a, mine, sources)
                    remote(
                        mine,
                        rows_y[a].at[k, tall - j - 1],
                        ys.at[a],
                        yr.at[a, k],
                        p.device(p.z, y, p.c),
                    ).start()

                @pl.when((p.c == 0) & (z == p.detour(p.z)))
                def _(mine=mine, j=j, y=y, a=a):
                    add(a, mine, [side[a].at[k, y]])
                    remote(
                        mine,
                        rows_e[a].at[x, j - 1],
                        es.at[a],
                        er.at[a, x * (tall - 1) + j - 1],
                        p.device(p.partner(), p.y, p.c),
                    ).start()

                @pl.when((p.c == 0) & (z == p.detour(p.partner())))
                def _(j=j, y=y, a=a, along_y=along_y):
                    part = rows_e[a].at[x, j - 1]
                    remote(
                        part, part, cs.at[a], er.at[a, x * (tall - 1) + j - 1], sibling
                    ).wait_recv()
                    along_y([side[a].at[k, y], part])

                @pl.when((p.c == 1) | ((z != p.detour(p.z)) & (z != p.detour(p.partner()))))
                def _(y=y, a=a, along_y=along_y):
                    along_y([side[a].at[k, y]])

            add(a, held[a].at[k, p.y], [side[a].at[k, p.y]])

    products = Products(lefts, rights, results, room)
    last = depth * across - 1

    def second(z, x, way, number):
        k = z * across + x
        for i in range(pairs):
            turn = min(i, last)
            if (way is None) == (turn >= (depth - 1) * across):
                pl.when(number == turn)(functools.partial(products.run, i))
        for a in range(count):
            mine = held[a].at[k, p.y]
            if tall > 1:

                @pl.when((p.c == 1) | (z != p.detour(p.z)))
                def _(a=a, mine=mine):
                    part = rows_y[a].at[k]
                    remote(part, part, cs.at[a], yr.at[a, k], sibling).wait_recv()
                    add(a, mine, [rows_y[a].at[k, j] for j in range(tall - 1)])

            def from_z(index):
                part = rows_z[a].at[index]
                remote(part, part, cs.at[a], zr.at[a, index], sibling).wait_recv()
                add(a, mine, [part])

            def send(index, target):
                remote(mine, rows_z[a].at[index], zs.at[a, k], zr.at[a, index], target).start()

            if way is None or way == 1:
                pl.when(p.z > 0)(functools.partial(from_z, k))
            if way is None:
                pl.when(p.z < depth - 1)(functools.partial(from_z, depth * across + x))
            if way == 0:
                pl.when(p.z < depth - 1)(functools.partial(from_z, k))
            if way == 1:
                send(k, p.device(p.z + 1, p.y, p.c))
            if way == 0:
                left = p.device(p.z - 1, p.y, p.c)

                @pl.when(z == p.z - 1)
                def _():
                    send(depth * across + x, left)

                @pl.when(z < p.z - 1)
                def _():
                    send(k, left)

            if way is None and across > 1:

                @pl.when(x != p.x)
                def _():
                    remote(
                        mine,
                        rows_x[a].at[(p.x - x + across) % across - 1],
                        xs.at[a],
                        xr.at[a],
                        p.device(p.z, p.y, p.c, x),
                    ).start()

    swaps = Swaps(p, shifts, given, taken, given_sem, taken_sem)
    swaps.start()
    in_order(begin)
    products.start()
    in_order(first)
    in_order(second)
    k = p.z * across + p.x
    for a in range(count):
        mine = held[a].at[k, p.y]
        sources = []
        if across > 1:
            remote(rows_x[a], rows_x[a], xs.at[a], xr.at[a], sibling).wait()
            sources = [rows_x[a].at[j] for j in range(across - 1)]
        rows = ins[a].shape[1]
        chunk = 16 if rows % 16 == 0 else rows

        def go(i, _):
            part = pl.ds(i * chunk, chunk)
            total = mine[part].astype(jnp.float32)
            for source in sources:
                total = total + source[part].astype(jnp.float32)
            outs[a][part] = total
            return 0

        lax.fori_loop(0, rows // chunk, go, 0)
        remote(side[a], side[a], cs.at[a], rc.at[a, 0], sibling).wait_send()
        if tall > 1:

            @pl.when(p.c == 1)
            def _(a=a):
                remote(rows_y[a], rows_y[a], ys.at[a], rc.at[a, 0], sibling).wait_send()

            @pl.when(p.c == 0)
            def _(a=a):
                part = rows_y[a].at[pl.ds(0, (depth - 1) * across)]
                remote(part, part, ys.at[a], rc.at[a, 0], sibling).wait_send()
                remote(rows_e[a], rows_e[a], es.at[a], rc.at[a, 0], sibling).wait_send()

        def wait_z(k, _):
            @pl.when(k // across != p.z)
            def _():
                remote(mine, rows_z[a].at[0], zs.at[a, k], rc.at[a, 0], sibling).wait_send()

            return 0

        lax.fori_loop(0, depth * across, wait_z, 0)

    swaps.wait()


def scatter(partials, wide, collective_id, swapped=(), products=()):
    group, peers = lax.axis_size("expert"), lax.axis_size("fsdp")
    place = Place(group, peers, wide)
    given, shifts = split_swaps(swapped)
    count, extra, pairs = len(partials), len(given), len(products)
    lefts, rights = [v[0] for v in products], [v[1] for v in products]
    dma = pltpu.SemaphoreType.DMA
    items = place.depth * place.across

    def room(*lead):
        return [pltpu.VMEM(lead + s.shape[1:], s.dtype) for s in partials]

    return pl.pallas_call(
        functools.partial(scatter_kernel, place, count, shifts, pairs),
        out_shape=[jax.ShapeDtypeStruct(s.shape[1:], jnp.float32) for s in partials]
        + [jax.ShapeDtypeStruct(s.shape, s.dtype) for s in given]
        + products_shapes(products),
        in_specs=[pl.BlockSpec(memory_space=pl.ANY)] * (count + extra + 2 * pairs),
        out_specs=[pl.BlockSpec(memory_space=pltpu.VMEM)] * count
        + [pl.BlockSpec(memory_space=pl.ANY)] * extra
        + [pl.BlockSpec(memory_space=pl.ANY)] * pairs,
        scratch_shapes=room(items, place.tall)
        + room(items, place.tall)
        + room(items, max(place.tall - 1, 1))
        + room(items + place.across)
        + room(max(place.across - 1, 1))
        + room(place.across, max(place.tall - 1, 1))
        + [
            dma((count, items)),
            dma((count, items)),
            dma((count, items)),
            dma((count, items + place.across)),
            dma((count, items)),
            dma((count,)),
            dma((count,)),
            dma((count,)),
            dma((count,)),
            dma((max(extra, 1),)),
            dma((max(extra, 1),)),
            dma((count,)),
            dma((count, place.across * max(place.tall - 1, 1))),
        ]
        + products_room(products),
        compiler_params=pltpu.CompilerParams(
            collective_id=collective_id, has_side_effects=True, vmem_limit_bytes=60 << 20
        ),
        name=f"scatter{collective_id}",
    )(*partials, *given, *lefts, *rights)


def dot_plain(left, right):
    return jnp.dot(left, right, preferred_element_type=jnp.float32)


def dot_across(left, right):
    return lax.dot_general(left, right, (((1,), (1,)), ((), ())), preferred_element_type=jnp.float32)


def dot_turned(left, right):
    return lax.dot_general(left, right, (((0,), (0,)), ((), ())), preferred_element_type=jnp.float32)


def ffn_kernel(peers, sources, numbers, fill, *refs):
    hid, cot, ranks = refs[:3]
    gates, ups, downs = (refs[3 + i * peers : 3 + (i + 1) * peers] for i in range(3))
    router, shared_in, shared_out = refs[3 + 3 * peers : 6 + 3 * peers]
    refs = refs[6 + 3 * peers :]
    rows, d_out = refs[:peers], refs[peers : 2 * peers]
    out_part, back_part, act, d_g, d_u, d_log, s_act, s_grad = refs[2 * peers : 8 + 2 * peers]
    rows_here, cots_here = refs[8 + 2 * peers :]
    f32, bf16 = jnp.float32, jnp.bfloat16
    step = pl.program_id(0)
    tok_rows = hid.shape[1]
    capacity = rows_here.shape[0] // sources
    width = hid.shape[2] // peers
    eid, start, fid = numbers[0], numbers[1], numbers[2]
    scale = fill[0]

    def length(s):
        return numbers[3 + step * sources + s]

    def columns(r):
        return pl.ds(pl.multiple_of((fid + r) % peers * width, width), width)

    scales = []
    picks = []
    for s in range(sources):
        part = pl.ds(s * capacity, capacity)
        slot = lax.broadcasted_iota(jnp.int32, (capacity, tok_rows), 0).astype(f32)
        pick = jnp.where(ranks[s] == slot, 1.0, 0.0)
        lane = start + lax.broadcasted_iota(jnp.int32, (1, tok_rows), 1)
        alive = jnp.where(lane < length(s), scale, 0.0)
        scales.append(jnp.sum(pick * alive, axis=1, keepdims=True))
        pick = pick.astype(bf16)
        picks.append(pick)
        rows_here[part, :] = dot_plain(pick, hid[s]).astype(bf16)
        cots_here[part, :] = dot_plain(pick, cot[s]).astype(bf16)
    row_scale = jnp.concatenate(scales, axis=0)
    logits = dot_plain(rows_here[...], router[...])
    top = jnp.max(logits, axis=1, keepdims=True)
    powers = jnp.exp(logits - top)
    probs = powers / jnp.sum(powers, axis=1, keepdims=True)
    own = (lax.broadcasted_iota(jnp.int32, (1, probs.shape[1]), 1) == eid).astype(f32)
    gate = jnp.sum(probs * own, axis=1, keepdims=True)

    for r in range(peers):
        rows[r][...] = rows_here[:, columns(r)]

    def summed(terms):
        total = terms[0]
        for term in terms[1:]:
            total = total + term
        return total

    g = summed([dot_plain(rows[r][...], gates[r][...]) for r in range(peers)])
    u = summed([dot_plain(rows[r][...], ups[r][...]) for r in range(peers)])
    sigma = 1.0 / (1.0 + jnp.exp(-g))
    act_now = (g * sigma * u).astype(bf16)
    act[...] = act_now
    d_gate = jnp.zeros_like(gate)
    weighted = []
    for r in range(peers):
        out = dot_plain(act_now, downs[r][...]).astype(bf16).astype(f32)
        row_cot = cots_here[:, columns(r)].astype(f32)
        d_out[r][...] = ((gate * row_scale) * row_cot).astype(bf16)
        d_gate = d_gate + jnp.sum(row_cot * out, axis=1, keepdims=True)
        weighted.append((gate * out).astype(bf16))
    d_gate = d_gate * row_scale
    d_act = summed([dot_across(d_out[r][...], downs[r][...]) for r in range(peers)])
    dg_now = (d_act * u * (sigma * (1.0 + g * (1.0 - sigma)))).astype(bf16)
    du_now = (d_act * (g * sigma)).astype(bf16)
    d_g[...] = dg_now
    d_u[...] = du_now
    dl_now = (gate * d_gate * (own - probs)).astype(bf16)
    d_log[...] = dl_now
    d_rows = []
    for r in range(peers):
        total = dot_across(dg_now, gates[r][...]) + dot_across(du_now, ups[r][...])
        total = total + dot_across(dl_now, router[columns(r), :])
        d_rows.append(total.astype(bf16))
    units = shared_out.shape[0]
    total_rows = sources * tok_rows
    hid_all = hid[...].reshape(total_rows, hid.shape[2])
    cot_all = cot[...].reshape(total_rows, hid.shape[2])
    both = dot_plain(hid_all, shared_in[...])
    sg, su = both[:, :units], both[:, units:]
    s_sigma = 1.0 / (1.0 + jnp.exp(-sg))
    s_now = sg * s_sigma * su
    column = lax.broadcasted_iota(jnp.int32, (tok_rows, 1), 0) + start
    alive = jnp.concatenate(
        [jnp.where(column < length(s), scale, 0.0) for s in range(sources)], axis=0
    )
    d_s = dot_across(cot_all, shared_out[...]) * alive
    s_act[...] = (s_now * alive).astype(bf16)
    s_low = s_now.astype(bf16)
    d_sg = (d_s * su * (s_sigma * (1.0 + sg * (1.0 - s_sigma)))).astype(bf16)
    d_su = (d_s * (sg * s_sigma)).astype(bf16)
    s_grad[:, pl.ds(0, units)] = d_sg
    s_grad[:, pl.ds(units, units)] = d_su
    for s in range(sources):
        part = slice(s * capacity, (s + 1) * capacity)
        span = slice(s * tok_rows, (s + 1) * tok_rows)
        for r in range(peers):
            out_part[s, :, columns(r)] = (
                dot_turned(picks[s], weighted[r][part])
                + dot_plain(s_low[span], shared_out[:, columns(r)])
            ).astype(bf16)
            back_part[s, :, columns(r)] = (
                dot_turned(picks[s], d_rows[r][part])
                + dot_across(s_grad[span, :], shared_in[columns(r), :])
            ).astype(bf16)


def ffn(capacity, numbers, fill, hid, cot, ranks, gates, ups, downs, router, shared_in, shared_out):
    group, tok_rows, dim = hid.shape
    peers = len(gates)
    sources = max(1, min(4, 256 // capacity))
    hidden = gates[0].shape[1]
    units = shared_out.shape[0]
    rows = sources * capacity
    bf16 = jnp.bfloat16

    def whole(array):
        return pl.BlockSpec(
            array.shape, lambda i, *_: (0,) * array.ndim, pipeline_mode=pl.Buffered(1)
        )

    def tile(*shape):
        return pl.BlockSpec(shape, lambda i, *_: (i,) + (0,) * (len(shape) - 1))

    pairs = group * capacity
    weights = [*gates, *ups, *downs, router, shared_in, shared_out]
    return pl.pallas_call(
        functools.partial(ffn_kernel, peers, sources),
        out_shape=[jax.ShapeDtypeStruct((pairs, dim // peers), bf16)] * (2 * peers)
        + [
            jax.ShapeDtypeStruct((group, tok_rows, dim), bf16),
            jax.ShapeDtypeStruct((group, tok_rows, dim), bf16),
            jax.ShapeDtypeStruct((pairs, hidden), bf16),
            jax.ShapeDtypeStruct((pairs, hidden), bf16),
            jax.ShapeDtypeStruct((pairs, hidden), bf16),
            jax.ShapeDtypeStruct((pairs, router.shape[1]), bf16),
            jax.ShapeDtypeStruct((group * tok_rows, units), bf16),
            jax.ShapeDtypeStruct((group * tok_rows, 2 * units), bf16),
        ],
        grid_spec=pltpu.PrefetchScalarGridSpec(
            num_scalar_prefetch=2,
            grid=(group // sources,),
            in_specs=[
                tile(sources, tok_rows, dim),
                tile(sources, tok_rows, dim),
                tile(sources, 1, tok_rows),
            ]
            + [whole(w) for w in weights],
            out_specs=[tile(rows, dim // peers)] * (2 * peers)
            + [
                tile(sources, tok_rows, dim),
                tile(sources, tok_rows, dim),
                tile(rows, hidden),
                tile(rows, hidden),
                tile(rows, hidden),
                tile(rows, router.shape[1]),
                tile(sources * tok_rows, units),
                tile(sources * tok_rows, 2 * units),
            ],
            scratch_shapes=[pltpu.VMEM((rows, dim), bf16)] * 2,
        ),
        compiler_params=pltpu.CompilerParams(vmem_limit_bytes=62 << 20),
        cost_estimate=pl.CostEstimate(
            flops=18 * pairs * dim * hidden, bytes_accessed=60 << 20, transcendentals=1 << 22
        ),
        name="ffn",
    )(numbers, fill, hid, cot, ranks, *weights)


def both_keys(keyval, rot):
    f32 = jnp.float32
    rot = rot.astype(f32)
    first = jnp.concatenate([keyval[:, :DN].astype(f32), rot], axis=1)
    second = jnp.concatenate([keyval[:, DN + DV : 2 * DN + DV].astype(f32), rot], axis=1)
    second = pltpu.roll(second, DN + DR, 1)
    return first.astype(jnp.bfloat16), second.astype(jnp.bfloat16)


def turn(array, plain, ahead, behind):
    width = array.shape[1]
    return (
        array * plain
        + pltpu.roll(array, width - DR // 2, 1) * ahead
        + pltpu.roll(array, DR // 2, 1) * behind
    )


def attend_kernel(numbers, hidden, w_query, latent, w_expand, rot, plain, ahead, behind, *outs):
    query, keyval, probs, context = outs
    bf16 = jnp.bfloat16
    turned = turn(dot_plain(hidden[...], w_query[...]), plain[...], ahead[...], behind[...])
    query_now = turned.astype(bf16)
    query[...] = query_now
    keyval[...] = dot_plain(latent[...], w_expand[...]).astype(bf16)
    rows, keys = query.shape[0], keyval.shape[0]
    row = lax.broadcasted_iota(jnp.int32, (rows, keys), 0) + numbers[0]
    key = lax.broadcasted_iota(jnp.int32, (rows, keys), 1)
    allowed = (key <= row) & (key < numbers[1])
    for i, keys_now in enumerate(both_keys(keyval[...], rot[...])):
        scores = dot_across(query_now, keys_now) * (DN + DR) ** (-0.5)
        scores = jnp.where(allowed, scores, masked_value)
        powers = jnp.exp(scores - jnp.max(scores, axis=1, keepdims=True))
        share = powers / jnp.sum(powers, axis=1, keepdims=True)
        probs[i] = share
        value = keyval[:, pl.ds(i * (DN + DV) + DN, DV)]
        context[:, pl.ds(i * DV, DV)] = dot_plain(share.astype(bf16), value).astype(bf16)


def attend(numbers, hidden, w_query, latent, w_expand, rot, turns):
    rows, dim = hidden.shape
    keys, rank = latent.shape
    bf16 = jnp.bfloat16

    def still(array):
        return pl.BlockSpec(array.shape, lambda i, *_: (0,) * array.ndim)

    def columns(height, width):
        return pl.BlockSpec((height, width), lambda i, *_: (0, i))

    return pl.pallas_call(
        attend_kernel,
        out_shape=[
            jax.ShapeDtypeStruct((rows, H * (DN + DR)), bf16),
            jax.ShapeDtypeStruct((keys, H * (DN + DV)), bf16),
            jax.ShapeDtypeStruct((H, rows, keys), jnp.float32),
            jax.ShapeDtypeStruct((rows, H * DV), bf16),
        ],
        grid_spec=pltpu.PrefetchScalarGridSpec(
            num_scalar_prefetch=1,
            grid=(H // 2,),
            in_specs=[
                still(hidden),
                columns(dim, 2 * (DN + DR)),
                still(latent),
                columns(rank, 2 * (DN + DV)),
                still(rot),
                *[still(t) for t in turns],
            ],
            out_specs=[
                columns(rows, 2 * (DN + DR)),
                columns(keys, 2 * (DN + DV)),
                pl.BlockSpec((2, rows, keys), lambda i, *_: (i, 0, 0)),
                columns(rows, 2 * DV),
            ],
        ),
        compiler_params=pltpu.CompilerParams(vmem_limit_bytes=40 << 20),
        name="attend",
    )(numbers, hidden, w_query, latent, w_expand, rot, *turns)


def attend_back_kernel(d_res, w_output, query, keyval, probs, rot, plain, ahead, behind, *outs):
    d_query, d_keyval, d_rot = outs
    f32, bf16 = jnp.float32, jnp.bfloat16
    scale = (DN + DR) ** (-0.5)
    query_now = query[...]
    total = jnp.zeros(query.shape, f32)
    rot_total = jnp.zeros(d_rot.shape, f32)
    for i, keys_now in enumerate(both_keys(keyval[...], rot[...])):
        d_context = dot_across(d_res[...], w_output[pl.ds(i * DV, DV), :]).astype(bf16)
        share = probs[i]
        at = i * (DN + DV)
        d_value = dot_turned(share.astype(bf16), d_context)
        d_share = dot_across(d_context, keyval[:, pl.ds(at + DN, DV)])
        d_score = share * (d_share - jnp.sum(share * d_share, axis=1, keepdims=True))
        d_score = d_score.astype(bf16)
        total = total + dot_plain(d_score, keys_now) * scale
        d_key = dot_turned(d_score, query_now) * scale
        if i == 1:
            d_key = pltpu.roll(d_key, DN + DR, 1)
        d_keyval[:, pl.ds(at, DN)] = d_key[:, :DN].astype(bf16)
        d_keyval[:, pl.ds(at + DN, DV)] = d_value.astype(bf16)
        rot_total = rot_total + d_key[:, DN : 2 * DN]
    d_query[...] = turn(total, plain[...], -ahead[...], -behind[...]).astype(bf16)

    @pl.when(pl.program_id(0) == 0)
    def _():
        d_rot[...] = rot_total

    @pl.when(pl.program_id(0) != 0)
    def _():
        d_rot[...] += rot_total


def attend_back(d_res, w_output, query, keyval, probs, rot, turns):
    rows, dim = d_res.shape
    keys = keyval.shape[0]
    bf16 = jnp.bfloat16

    def still(array):
        return pl.BlockSpec(array.shape, lambda i: (0,) * array.ndim)

    def columns(height, width):
        return pl.BlockSpec((height, width), lambda i: (0, i))

    return pl.pallas_call(
        attend_back_kernel,
        out_shape=[
            jax.ShapeDtypeStruct(query.shape, bf16),
            jax.ShapeDtypeStruct(keyval.shape, bf16),
            jax.ShapeDtypeStruct((keys, DN), jnp.float32),
        ],
        grid=(H // 2,),
        in_specs=[
            still(d_res),
            pl.BlockSpec((2 * DV, dim), lambda i: (i, 0)),
            columns(rows, 2 * (DN + DR)),
            columns(keys, 2 * (DN + DV)),
            pl.BlockSpec((2, rows, keys), lambda i: (i, 0, 0)),
            still(rot),
            *[still(t) for t in turns],
        ],
        out_specs=[
            columns(rows, 2 * (DN + DR)),
            columns(keys, 2 * (DN + DV)),
            pl.BlockSpec((keys, DN), lambda i: (0, 0)),
        ],
        compiler_params=pltpu.CompilerParams(vmem_limit_bytes=40 << 20),
        name="attend_back",
    )(d_res, w_output, query, keyval, probs, rot, *turns)


def from_peers(block):
    size = lax.axis_size("fsdp")
    return [block] + [
        lax.ppermute(block, "fsdp", [(j, (j - r) % size) for j in range(size)])
        for r in range(1, size)
    ]


def sum_to_peers(term):
    size = lax.axis_size("fsdp")
    arrived = [
        lax.ppermute(term(r), "fsdp", [(j, (j + r) % size) for j in range(size)])
        for r in range(1, size)
    ]
    return arrived


def body(
    tokens,
    cotangent,
    routes,
    lengths,
    attn_gain,
    q_weight,
    kva_weight,
    kv_gain,
    kvb_weight,
    out_weight,
    ffn_gain,
    router_weight,
    shared_gate,
    shared_up,
    shared_down,
    expert_gate,
    expert_up,
    expert_down,
):
    bf16, f32 = jnp.bfloat16, jnp.float32
    tok_rows, dim = tokens.shape
    peers = lax.axis_size("fsdp")
    group = lax.axis_size("expert")
    fid, eid = lax.axis_index("fsdp"), lax.axis_index("expert")
    seq_len = tok_rows * peers
    slot_total = seq_len * group
    expert_count = router_weight.shape[1]
    capacity = max(4, 5 * tok_rows * TOPK // (4 * expert_count))
    capacity = -(-capacity // 16) * 16
    half = dim // peers
    plane_rows = group * tok_rows
    pairs = group * capacity

    positions = fid * tok_rows + jnp.arange(tok_rows, dtype=jnp.int32)
    seq_length = lengths[0]
    valid_mask = (positions < seq_length).astype(f32)
    expert_ids = jnp.arange(expert_count, dtype=jnp.int32)
    hot_sum = jnp.sum((routes[:, :, None] == expert_ids[None, None, :]).astype(f32), axis=1)
    local_counts = jnp.sum(hot_sum * valid_mask[:, None], axis=0)

    def lane_row(vector):
        return jnp.pad(vector.astype(f32), (0, tok_rows - vector.shape[0]))[None, :]

    small = jnp.concatenate(
        [routes.T.astype(f32)]
        + [lane_row(v) for v in (attn_gain, ffn_gain, kv_gain, local_counts, lengths)]
        + [jnp.zeros((16 - TOPK - 5, tok_rows), f32)],
        axis=0,
    )
    devices = group * peers
    turns = range(1, peers)
    w_query, w_compress, w_expand, w_output, w_router, small_all, *more = gather(
        [q_weight, kva_weight, kvb_weight, out_weight, router_weight, small],
        True,
        0,
        [(expert_gate[0], -r) for r in turns] + [(expert_up[0], -r) for r in turns],
    )
    gate_parts = [expert_gate[0]] + more[: peers - 1]
    up_parts = [expert_up[0]] + more[peers - 1 :]
    w_query, w_compress, w_expand, w_output, w_router = (
        w.reshape(-1, w.shape[-1]) for w in (w_query, w_compress, w_expand, w_output, w_router)
    )
    gain_attn = small_all[:, TOPK, : attn_gain.shape[0]].reshape(-1)
    gain_ffn = small_all[:, TOPK + 1, : ffn_gain.shape[0]].reshape(-1)
    gain_latent = small_all[:, TOPK + 2, : kv_gain.shape[0]].reshape(-1)
    route_counts = jnp.sum(small_all[:, TOPK + 3, :expert_count], axis=0)
    all_lengths = small_all.reshape(group, peers, 16, tok_rows)[:, 0, TOPK + 4, 0]
    valid_total = jnp.sum(all_lengths)
    fill_scale = slot_total / valid_total
    plane_small = lax.dynamic_index_in_dim(
        small_all.reshape(group, peers, 16, tok_rows), fid, axis=1, keepdims=False
    )
    units = shared_gate.shape[1] // group
    lanes_more = -units % 128
    pieces = jnp.concatenate(
        [
            jnp.pad(w.reshape(-1, group, units), ((0, 0), (0, 0), (0, lanes_more)))
            for w in (shared_gate, shared_up)
        ],
        axis=2,
    ).transpose(1, 0, 2)
    pieces = lax.all_to_all(pieces, "expert", split_axis=0, concat_axis=0, tiled=True)
    sd_weight = jnp.roll(jnp.stack(from_peers(shared_down)), fid, axis=0).reshape(units, dim)
    sd_weight = jnp.pad(sd_weight, ((0, lanes_more), (0, 0)))
    cosine, sine_vals = rope_tables(positions)
    tokens_f = tokens.astype(f32)
    cot_ready, small_all = lax.optimization_barrier((cotangent, small_all))
    cot_plane = lax.all_gather(cot_ready, "expert", axis=0, tiled=True)
    normed_one, inverse_one = rms_norm(tokens_f, gain_attn)
    hidden_one = normed_one.astype(bf16)
    compressed = jnp.dot(hidden_one, w_compress, preferred_element_type=f32)
    latent_raw = compressed[:, :KVR]
    latent_norm, inverse_kv = rms_norm(latent_raw, gain_latent)
    latent = latent_norm.astype(bf16)
    key_rot = rotate(compressed[:, KVR:], cosine, sine_vals).astype(bf16)
    latent_rot = lax.all_gather(
        jnp.concatenate([latent, key_rot], axis=1), "fsdp", axis=0, tiled=True
    )
    down_own, latent_rot = lax.optimization_barrier((expert_down[0], latent_rot))
    down_parts = from_peers(down_own)
    all_rot = jnp.pad(latent_rot[:, KVR:], ((0, 0), (0, 2 * DN - DR)))

    def spread_columns(first, second, rest):
        one = jnp.concatenate([jnp.full((tok_rows, DN), rest, f32), first, second], axis=1)
        return jnp.concatenate([one, one], axis=1)

    zero = jnp.zeros_like(cosine)
    rotations = [
        spread_columns(cosine, cosine, 1.0),
        spread_columns(-sine_vals, zero, 0.0),
        spread_columns(zero, sine_vals, 0.0),
    ]
    query_all, keyval, probs_attn, context = attend(
        jnp.stack([fid * tok_rows, seq_length]).astype(jnp.int32),
        hidden_one,
        w_query,
        latent_rot[:, :KVR],
        w_expand,
        all_rot,
        rotations,
    )
    residual = tokens_f + jnp.dot(context, w_output, preferred_element_type=f32)
    normed_two, inverse_two = rms_norm(residual, gain_ffn)
    hidden_two = normed_two.astype(bf16)
    hid3, *more = gather([hidden_two], False, 1, [(pieces, -r) for r in turns])
    gu_weight = jnp.roll(jnp.stack([pieces] + more), fid, axis=0)
    gu_weight = gu_weight.transpose(1, 0, 2, 3).reshape(dim, -1)
    hid_plane = hid3.reshape(plane_rows, dim)
    cot3 = cot_plane.reshape(group, tok_rows, dim)
    router_probs = jax.nn.softmax(jnp.dot(hidden_two, w_router, preferred_element_type=f32), axis=-1)
    local_shares = jnp.sum(router_probs * valid_mask[:, None], axis=0)
    frequency = expert_count / (TOPK * valid_total) * route_counts
    d_probs_own = balance_weight * valid_mask[:, None] * frequency[None, :] / valid_total
    dlog_own = (
        router_probs * (d_probs_own - jnp.sum(router_probs * d_probs_own, axis=-1, keepdims=True))
    ).astype(bf16)
    named = jnp.any(plane_small[:, :TOPK, :] == eid.astype(f32), axis=1)
    place = jnp.arange(tok_rows)
    before = (place[:, None] < place[None, :]).astype(bf16)
    ranks = jnp.dot(named.astype(bf16), before, preferred_element_type=f32)
    ranks = jnp.where(named, ranks, -1.0)[:, None, :]
    numbers = jnp.concatenate(
        [jnp.stack([eid, fid * tok_rows, fid]).astype(jnp.int32), all_lengths.astype(jnp.int32)]
    )
    made = ffn(
        capacity,
        numbers,
        fill_scale.reshape(1),
        hid3,
        cot3,
        ranks,
        gate_parts,
        up_parts,
        down_parts,
        w_router,
        gu_weight,
        sd_weight,
    )

    rows_in, d_out = made[:peers], made[peers : 2 * peers]
    out_part, back_part, act, d_hidden_g, d_hidden_u, dlog_rows, shared_scaled, d_gu = made[
        2 * peers :
    ]

    def outer(left, right):
        return lax.dot_general(left, right, (((0,), (0,)), ((), ())), preferred_element_type=f32)

    def back(left, weight):
        return lax.dot_general(left, weight, (((1,), (1,)), ((), ())), preferred_element_type=f32)

    def gate_term(r):
        return outer(rows_in[r], d_hidden_g)

    def up_term(r):
        return outer(rows_in[r], d_hidden_u)

    def down_term(r):
        return outer(act, d_out[r])

    def with_peers(term):
        arrived = sum_to_peers(lambda r: term(r).astype(bf16))
        total = term(0)
        for block in arrived:
            total = total + block.astype(f32)
        return total

    def plus(total, blocks):
        for block in blocks:
            total = total + block.astype(f32)
        return total

    d_hidden_two, *more = scatter(
        [back_part],
        False,
        2,
        [(gate_term(r).astype(bf16), r) for r in turns],
        [
            (hid_plane, d_gu),
            (shared_scaled, cot_plane),
            (rows_in[1], d_hidden_u),
            (act, d_out[1]),
            (rows_in[0], d_hidden_g),
        ]
        if peers == 2
        else [],
    )
    gate_blocks = more[: peers - 1]
    if peers == 2:
        d_gu_weight, d_sd, *others, gate_own = more[1:]
    else:
        d_gu_weight = outer(hid_plane, d_gu).astype(bf16)
        d_sd = outer(shared_scaled, cot_plane).astype(bf16)
        others = [up_term(r).astype(bf16) for r in turns]
        others = others + [down_term(r).astype(bf16) for r in turns]
        gate_own = gate_term(0)
    d_sd = d_sd[:units]
    out_part, d_hidden_two = lax.optimization_barrier((out_part, d_hidden_two))
    out_sum = lax.psum_scatter(
        out_part.reshape(plane_rows, dim), "expert", scatter_dimension=0, tiled=True
    )
    egate_grad = plus(gate_own.astype(f32), gate_blocks)[None]
    d_hidden_two = d_hidden_two + back(dlog_own, w_router)
    router_parts = jnp.stack([outer(rows_in[r], dlog_rows) for r in range(peers)])
    router_grad = jnp.roll(router_parts, fid, axis=0).reshape(dim, -1) + outer(hidden_two, dlog_own)
    d_gu_blocks = d_gu_weight.reshape(group, peers, dim // (group * peers), -1)
    d_sd_blocks = d_sd.reshape(peers, units // peers, dim)

    def gu_term(r):
        return lax.dynamic_index_in_dim(d_gu_blocks, (fid + r) % peers, axis=1, keepdims=False)

    def sd_term(r):
        return lax.dynamic_index_in_dim(d_sd_blocks, (fid + r) % peers, axis=0, keepdims=False)

    gu_sum = plus(gu_term(0).astype(f32), sum_to_peers(gu_term)).astype(bf16)
    sdown_grad = plus(sd_term(0).astype(f32), sum_to_peers(sd_term))
    grad_out = cotangent.astype(f32) * (valid_mask * fill_scale)[:, None]
    d_residual, d_ffn_gain = norm_back(d_hidden_two, residual, inverse_two, gain_ffn)
    d_residual = d_residual + grad_out
    d_residual_low = d_residual.astype(bf16)
    d_query, d_keyval_all, d_key_rot = attend_back(
        d_residual_low, w_output, query_all, keyval, probs_attn, all_rot, rotations
    )
    d_key_rot = d_key_rot[:, :DR]

    def own_rows(array, r):
        return lax.dynamic_slice_in_dim(array, (fid + r) % peers * tok_rows, tok_rows, axis=0)

    swapped = [(own_rows(d_keyval_all, r).astype(bf16), r) for r in turns]
    swapped = swapped + [(own_rows(d_key_rot, r).astype(bf16), r) for r in turns]
    *arrived, d_output_w, d_query_w, up_own, down_own = exchange(
        4,
        swapped,
        [
            (context, d_residual_low),
            (hidden_one, d_query),
            (rows_in[0], d_hidden_u),
            (act, d_out[0]),
        ],
    )
    own_dkeyval = plus(own_rows(d_keyval_all, 0).astype(f32), arrived[: peers - 1])
    own_dkeyrot = plus(own_rows(d_key_rot, 0), arrived[peers - 1 :])
    gu_sum, own_dkeyval = lax.optimization_barrier((gu_sum, own_dkeyval))
    gu_sum = lax.all_to_all(gu_sum, "expert", split_axis=0, concat_axis=0, tiled=True)
    d_keyval = own_dkeyval.astype(bf16)
    d_latent = back(d_keyval, w_expand)
    d_latent_raw, d_latent_gain = norm_back(d_latent, latent_raw, inverse_kv, gain_latent)
    d_compressed = jnp.concatenate(
        [d_latent_raw, rotate_back(own_dkeyrot, cosine, sine_vals)], axis=-1
    ).astype(bf16)
    d_compress_w, d_expand_w = outer_products([(hidden_one, d_compressed), (latent, d_keyval)])
    d_hidden_one = back(d_query, w_query) + back(d_compressed, w_compress)
    d_tokens, d_attn_gain = norm_back(d_hidden_one, tokens_f, inverse_one, gain_attn)
    tokens_grad = d_tokens + d_residual
    def lanes(vector):
        piece = vector.reshape(devices, -1)
        return jnp.pad(piece, ((0, 0), (0, tok_rows - piece.shape[1])))

    small_grads = jnp.stack(
        [
            lanes(d_attn_gain),
            lanes(d_latent_gain),
            lanes(d_ffn_gain),
            lanes(jnp.tile(local_shares, devices)),
        ]
        + [jnp.zeros((devices, tok_rows), f32)] * 4,
        axis=1,
    )
    dense = [
        w.astype(bf16).reshape(devices, -1, w.shape[-1])
        for w in (d_query_w, d_compress_w, d_expand_w, d_output_w, router_grad)
    ]
    q_grad, kva_grad, kvb_grad, out_grad, router_out, smalls, *blocks = scatter(
        dense + [small_grads],
        True,
        3,
        [(w, r) for w, r in zip(others, [*turns, *turns])],
    )
    gu_sum, out_sum, smalls = lax.optimization_barrier((gu_sum, out_sum, smalls))
    mixed = (residual + out_sum.astype(f32)).astype(bf16)
    gu_sum = gu_sum.astype(f32).transpose(1, 0, 2)
    sgate_grad = gu_sum[:, :, :units].reshape(shared_gate.shape)
    sup_grad = gu_sum[:, :, units + lanes_more : 2 * units + lanes_more].reshape(shared_up.shape)
    eup_grad = plus(up_own.astype(f32), blocks[: peers - 1])[None]
    edown_grad = plus(down_own.astype(f32), blocks[peers - 1 :])[None]
    attn_gain_grad = smalls[0, : attn_gain.shape[0]]
    kv_gain_grad = smalls[1, : kv_gain.shape[0]]
    ffn_gain_grad = smalls[2, : ffn_gain.shape[0]]
    balance = jnp.sum(frequency * (smalls[3, :expert_count] / valid_total))
    return (
        mixed,
        tokens_grad,
        balance,
        attn_gain_grad,
        q_grad,
        kva_grad,
        kv_gain_grad,
        kvb_grad,
        out_grad,
        ffn_gain_grad,
        router_out,
        sgate_grad,
        sup_grad,
        sdown_grad,
        egate_grad,
        eup_grad,
        edown_grad,
    )


def solution(mesh):
    return jax.shard_map(
        body,
        mesh=mesh,
        in_specs=(
            P(("expert", "fsdp"), None),
            P(("expert", "fsdp"), None),
            P(("expert", "fsdp"), None),
            P("expert"),
            P(("expert", "fsdp")),
            P(("expert", "fsdp"), None),
            P(("expert", "fsdp"), None),
            P(("expert", "fsdp")),
            P(("expert", "fsdp"), None),
            P(("expert", "fsdp"), None),
            P(("expert", "fsdp")),
            P(("expert", "fsdp"), None),
            P(("expert", "fsdp"), None),
            P(("expert", "fsdp"), None),
            P(("expert", "fsdp"), None),
            P("expert", "fsdp", None),
            P("expert", "fsdp", None),
            P("expert", None, "fsdp"),
        ),
        out_specs=(
            P(("expert", "fsdp"), None),
            P(("expert", "fsdp"), None),
            P(),
            P(("expert", "fsdp")),
            P(("expert", "fsdp"), None),
            P(("expert", "fsdp"), None),
            P(("expert", "fsdp")),
            P(("expert", "fsdp"), None),
            P(("expert", "fsdp"), None),
            P(("expert", "fsdp")),
            P(("expert", "fsdp"), None),
            P(("expert", "fsdp"), None),
            P(("expert", "fsdp"), None),
            P(("expert", "fsdp"), None),
            P("expert", "fsdp", None),
            P("expert", "fsdp", None),
            P("expert", None, "fsdp"),
        ),
        check_vma=False,
    )
```

```python
import functools

import jax
import jax.numpy as jnp
from jax import lax
from jax.experimental import pallas as pl
from jax.experimental.pallas import tpu as pltpu
from jax.sharding import PartitionSpec as P

D = 2048
H = 16
DN = 128
DR = 64
DV = 128
KVR = 512
TOPK = 6


epsilon = 1e-06
balance_weight = 0.001
masked_value = -1e30


def rms_norm(vector, gain_row):
    inverse = lax.rsqrt(jnp.mean(vector * vector, axis=-1, keepdims=True) + epsilon)
    return (vector * inverse * gain_row, inverse)


def norm_back(grad_in, vector, inverse, gain_row):
    scaled = grad_in * gain_row
    gain_grad = jnp.sum(grad_in * vector * inverse, axis=0)
    vector_grad = inverse * scaled - vector * inverse**3 * jnp.mean(
        scaled * vector, axis=-1, keepdims=True
    )
    return (vector_grad, gain_grad)


def rope_tables(positions):
    half_width = DR // 2
    frequency = 10000.0 ** (-jnp.arange(half_width, dtype=jnp.float32) / half_width)
    angles = positions.astype(jnp.float32)[:, None] * frequency[None, :]
    return (jnp.cos(angles), jnp.sin(angles))


def rotate(vector, cosine, sine_vals):
    half_width = vector.shape[-1] // 2
    first_half = vector[..., :half_width]
    second_half = vector[..., half_width:]
    return jnp.concatenate(
        [
            first_half * cosine - second_half * sine_vals,
            second_half * cosine + first_half * sine_vals,
        ],
        axis=-1,
    )


def rotate_back(grad_in, cosine, sine_vals):
    half_width = grad_in.shape[-1] // 2
    first_half = grad_in[..., :half_width]
    second_half = grad_in[..., half_width:]
    return jnp.concatenate(
        [
            first_half * cosine + second_half * sine_vals,
            second_half * cosine - first_half * sine_vals,
        ],
        axis=-1,
    )


def silu_slope(vector):
    sigmoid_vals = jax.nn.sigmoid(vector)
    return sigmoid_vals * (1.0 + vector * (1.0 - sigmoid_vals))


MESH_IDS = pl.DeviceIdType.MESH


class Place:
    def __init__(self, group, peers, wide):
        self.wide = wide
        self.depth = min(4, group // 2)
        self.tall = group // 2 // self.depth
        self.across = peers if wide else 1
        self.peers = peers
        self.units = self.depth * self.tall * self.across
        self.slots = 2 * self.units

    def here(self):
        e = lax.axis_index("expert")
        self.fsdp = lax.axis_index("fsdp")
        self.c = e % 2
        self.y = e // 2 % self.tall
        self.z = e // (2 * self.tall)
        self.x = self.fsdp if self.wide else 0
        return self

    def detour(self, z):
        return (self.depth - 1) * (1 - z % 2)

    def partner(self):
        return self.z + 1 - self.z % 2 * 2

    def greet_peers(self):
        barrier = pltpu.get_barrier_semaphore()
        for k in range(1, self.peers):
            pl.semaphore_signal(
                barrier,
                inc=1,
                device_id=self.device(self.z, self.y, self.c, (self.fsdp + k) % self.peers),
                device_id_type=MESH_IDS,
            )
        pl.semaphore_wait(barrier, self.peers - 1)

    def slot(self, z, y, c, x):
        return ((z * self.tall + y) * 2 + c) * self.across + x

    def device(self, z, y, c, x=None):
        return ((z * self.tall + y) * 2 + c, self.fsdp if x is None else x)

    def greet(self, swapping):
        barrier = pltpu.get_barrier_semaphore()
        partners = self.peers if swapping or self.wide else 1
        count = 1 + (self.tall - 1) + (partners - 1)

        def signal(target):
            pl.semaphore_signal(barrier, inc=1, device_id=target, device_id_type=MESH_IDS)

        signal(self.device(self.z, self.y, 1 - self.c))
        for k in range(1, self.tall):
            signal(self.device(self.z, (self.y + k) % self.tall, self.c))
        for k in range(1, partners):
            signal(self.device(self.z, self.y, self.c, (self.fsdp + k) % self.peers))

        @pl.when(self.z > 0)
        def _():
            signal(self.device(self.z - 1, self.y, self.c))

        @pl.when(self.z < self.depth - 1)
        def _():
            signal(self.device(self.z + 1, self.y, self.c))

        last = self.depth - 1
        pl.semaphore_wait(barrier, count + 2 - self.z // last - (last - self.z) // last)


def remote(src, dst, send_sem, recv_sem, target):
    return pltpu.make_async_remote_copy(
        src_ref=src,
        dst_ref=dst,
        send_sem=send_sem,
        recv_sem=recv_sem,
        device_id=target,
        device_id_type=MESH_IDS,
    )


class Swaps:
    def __init__(self, place, shifts, given, taken, send_sem, recv_sem):
        self.copies = [
            remote(
                given[i],
                taken[i],
                send_sem.at[i],
                recv_sem.at[i],
                place.device(place.z, place.y, place.c, (place.fsdp + shift) % place.peers),
            )
            for i, shift in enumerate(shifts)
        ]

    def start(self):
        for copy in self.copies:
            copy.start()

    def wait(self):
        for copy in self.copies:
            copy.wait()


def gather_kernel(place, count, shifts, *refs):
    total = count + len(shifts)
    ins, outs = refs[:count], refs[total : total + count]
    given, taken = refs[count:total], refs[total + count : 2 * total]
    near, xs, ys, cs, rc, zs, got, given_sem, taken_sem, es = refs[2 * total :]
    p = place.here()
    depth, tall, across = p.depth, p.tall, p.across
    p.greet(len(shifts) > 0)
    sibling = p.device(p.z, p.y, 1 - p.c)

    def unit(z, y, x):
        return (z * tall + y) * across + x

    def block(a, z, y, x):
        return outs[a].at[p.slot(z, y, p.c, x)]

    def to_z(a, src, z, x, way):
        return remote(
            src,
            block(a, z, p.y, x),
            zs.at[a, way, z * across + x],
            got.at[a, unit(z, p.y, x)],
            p.device(p.z + 2 * way - 1, p.y, p.c),
        )

    def to_y(a, src, z, x, k):
        return remote(
            src,
            block(a, z, p.y, x),
            ys.at[a],
            got.at[a, unit(z, p.y, x)],
            p.device(p.z, (p.y + k) % tall, p.c),
        )

    def to_sibling(a, src, z, y, x):
        return remote(src, block(a, z, y, x), cs.at[a], rc.at[a], sibling)

    def arrived(a, z, y, x):
        remote(block(a, z, y, x), block(a, z, y, x), cs.at[a], got.at[a, unit(z, y, x)], sibling).wait_recv()

    def spread(a, src, z, x, ways):
        for way in ways:

            @pl.when((p.z < depth - 1) if way else (p.z > 0))
            def _():
                to_z(a, src, z, x, way).start()

        @pl.when((p.c == 1) | (z != p.detour(p.z)))
        def _():
            for k in range(1, tall):
                to_y(a, src, z, x, k).start()

        to_sibling(a, src, z, p.y, x).start()

    def to_partner(a, z, y, x, k):
        return remote(
            block(a, z, y, x),
            block(a, z, y, x),
            es.at[a, x * max(tall - 1, 1) + k - 1],
            got.at[a, unit(z, y, x)],
            p.device(p.partner(), p.y, p.c),
        )

    def over_x(step):
        if across == 1:
            step(0)
        else:
            lax.fori_loop(0, across, lambda k, _: (step((p.x + k) % across), 0)[1], 0)

    for a in range(count):
        for k in range(1, across):
            remote(
                ins[a],
                block(a, p.z, p.y, p.x),
                xs.at[a],
                got.at[a, unit(p.z, p.y, p.x)],
                p.device(p.z, p.y, p.c, (p.x + k) % across),
            ).start()
        spread(a, ins[a], p.z, p.x, (0, 1))
        pltpu.make_async_copy(ins[a], block(a, p.z, p.y, p.x), near.at[a]).start()

    swaps = Swaps(p, shifts, given, taken, given_sem, taken_sem)
    swaps.start()
    for k in range(1, across):
        x = (p.x + k) % across
        for a in range(count):
            arrived(a, p.z, p.y, x)
            spread(a, block(a, p.z, p.y, x), p.z, x, (0, 1))

    def from_y(z):
        def step(x):
            for k in range(1, tall):
                y = (p.y + k) % tall
                for a in range(count):
                    arrived(a, z, y, x)

                    @pl.when((p.c == 0) & (z == p.detour(p.partner())))
                    def _(a=a, y=y, k=k):
                        to_partner(a, z, y, x, k).start()

                    to_sibling(a, block(a, z, y, x), z, y, x).start()

        over_x(step)

    for d in range(1, depth + 1):
        if d < depth:

            @pl.when(p.z >= d)
            def _(d=d):
                def step(x):
                    for a in range(count):
                        arrived(a, p.z - d, p.y, x)
                        spread(a, block(a, p.z - d, p.y, x), p.z - d, x, (1,))

                over_x(step)

            @pl.when(p.z + d < depth)
            def _(d=d):
                def step(x):
                    for a in range(count):
                        arrived(a, p.z + d, p.y, x)
                        spread(a, block(a, p.z + d, p.y, x), p.z + d, x, (0,))

                over_x(step)

        if d == 1:
            from_y(p.z)
        else:

            @pl.when(p.z >= d - 1)
            def _(d=d):
                from_y(p.z - d + 1)

            @pl.when(p.z + d - 1 < depth)
            def _(d=d):
                from_y(p.z + d - 1)

    for a in range(count):
        pltpu.make_async_copy(ins[a], block(a, p.z, p.y, p.x), near.at[a]).wait()

        def many(number, send, recv):
            part = outs[a].at[pl.ds(0, number)]
            return remote(part, part, send.at[a], recv.at[a], sibling)

        if across > 1:
            many(across - 1, xs, rc).wait_send()
        if tall > 1:

            @pl.when(p.c == 1)
            def _():
                many((tall - 1) * depth * across, ys, rc).wait_send()

            @pl.when(p.c == 0)
            def _(a=a):
                many((tall - 1) * (depth - 1) * across, ys, rc).wait_send()
                for x in range(across):
                    for k in range(1, tall):
                        to_partner(a, 0, p.y, x, k).wait_send()

        many(p.units, cs, rc).wait()
        for z in range(depth):
            for way in (0, 1):

                @pl.when(
                    ((p.z >= z) & (p.z < depth - 1)) if way else ((p.z <= z) & (p.z > 0))
                )
                def _(z=z, way=way, a=a):
                    for x in range(across):
                        to_z(a, block(a, z, p.y, x), z, x, way).wait_send()

    swaps.wait()


def split_swaps(swapped):
    return [w for w, _ in swapped], [shift for _, shift in swapped]


def gather(shards, wide, collective_id, swapped=()):
    group, peers = lax.axis_size("expert"), lax.axis_size("fsdp")
    place = Place(group, peers, wide)
    given, shifts = split_swaps(swapped)
    count, extra = len(shards), len(given)
    dma = pltpu.SemaphoreType.DMA
    return pl.pallas_call(
        functools.partial(gather_kernel, place, count, shifts),
        out_shape=[jax.ShapeDtypeStruct((place.slots,) + s.shape, s.dtype) for s in shards]
        + [jax.ShapeDtypeStruct(s.shape, s.dtype) for s in given],
        in_specs=[pl.BlockSpec(memory_space=pl.ANY)] * (count + extra),
        out_specs=[pl.BlockSpec(memory_space=pl.ANY)] * (count + extra),
        scratch_shapes=[dma((count,))] * 5
        + [
            dma((count, 2, place.depth * place.across)),
            dma((count, place.units)),
            dma((max(extra, 1),)),
            dma((max(extra, 1),)),
            dma((count, place.across * max(place.tall - 1, 1))),
        ],
        compiler_params=pltpu.CompilerParams(
            collective_id=collective_id, has_side_effects=True, vmem_limit_bytes=58 << 20
        ),
        name=f"gather{collective_id}",
    )(*shards, *given)


def chunk_of(left):
    return 256 if left.shape[1] % 256 == 0 else 128


class Pairs:
    def __init__(self, products):
        self.arrays = []
        self.uses = []
        for pair in products:
            use = []
            for array in pair:
                known = [i for i, other in enumerate(self.arrays) if other is array]
                if not known:
                    self.arrays.append(array)
                    known = [len(self.arrays) - 1]
                use.append(known[0])
            self.uses.append(tuple(use))

    def shapes(self):
        arrays = self.arrays
        return [
            jax.ShapeDtypeStruct((arrays[i].shape[1], arrays[j].shape[1]), jnp.bfloat16)
            for i, j in self.uses
        ]

    def room(self):
        if not self.uses:
            return []
        arrays = self.arrays
        held = [pltpu.VMEM(v.shape, v.dtype) for v in arrays]
        ready = [
            pltpu.VMEM((2, chunk_of(arrays[i]), arrays[j].shape[1]), jnp.bfloat16)
            for i, j in self.uses
        ]
        dma = pltpu.SemaphoreType.DMA
        return held + ready + [dma((len(arrays),)), dma((len(self.uses), 2))]


class Products:
    def __init__(self, uses, operands, results, refs):
        self.uses = uses
        if uses:
            held = refs[: len(operands)]
            self.loads = list(zip(operands, held))
            self.in_sems, self.out_sems = refs[len(operands) + len(uses) :]
            ready = refs[len(operands) : len(operands) + len(uses)]
            self.parts = [(r, held[i], held[j], v) for (i, j), r, v in zip(uses, results, ready)]

    def load(self, k):
        source, held = self.loads[k]
        return pltpu.make_async_copy(source, held, self.in_sems.at[k])

    def start(self):
        for k in range(len(self.loads) if self.uses else 0):
            self.load(k).start()

    def run(self, i):
        earlier = [k for use in self.uses[:i] for k in use]
        for k in sorted(set(self.uses[i]) - set(earlier)):
            self.load(k).wait()
        result, left, right, ready = self.parts[i]
        chunk = chunk_of(left)
        steps = left.shape[1] // chunk

        def leave(j):
            return pltpu.make_async_copy(
                ready.at[j % 2],
                result.at[pl.ds(pl.multiple_of(j * chunk, chunk), chunk)],
                self.out_sems.at[i, j % 2],
            )

        def go(j, _):
            @pl.when(j >= 2)
            def _():
                leave(j - 2).wait()

            part = pl.ds(pl.multiple_of(j * chunk, chunk), chunk)
            ready[j % 2] = dot_turned(left[:, part], right[...]).astype(ready.dtype)
            leave(j).start()
            return 0

        lax.fori_loop(0, steps, go, 0)
        for j in range(max(steps - 2, 0), steps):
            leave(j).wait()


def exchange_kernel(place, shifts, uses, operands, *refs):
    extra, pairs = len(shifts), len(uses)
    given, refs = refs[:extra], refs[extra:]
    loads, refs = refs[:operands], refs[operands:]
    left, right, refs = refs[0], refs[1], refs[2:]
    taken, results, refs = refs[:extra], refs[extra : extra + pairs], refs[extra + pairs :]
    across, held, held_sem, refs = refs[0], refs[1], refs[2], refs[3:]
    p = place.here()
    p.greet_peers()
    swaps = Swaps(p, shifts, given, taken, *refs[:2])
    swaps.start()
    products = Products(uses, loads, results, refs[2:])
    products.start()
    arrive = pltpu.make_async_copy(right, held, held_sem)
    arrive.start()
    for i in range(pairs):
        products.run(i)
    arrive.wait()
    chunk = 256

    def go(j, _):
        part = pl.ds(pl.multiple_of(j * chunk, chunk), chunk)
        across[:, part] = dot_across(left[...], held[part, :])
        return 0

    lax.fori_loop(0, held.shape[0] // chunk, go, 0)
    swaps.wait()


def exchange(collective_id, swapped, products, left, right):
    place = Place(lax.axis_size("expert"), lax.axis_size("fsdp"), False)
    given, shifts = split_swaps(swapped)
    pairs = Pairs(products)
    extra, operands = len(given), len(pairs.arrays)
    anywhere, inside = pl.BlockSpec(memory_space=pl.ANY), pl.BlockSpec(memory_space=pltpu.VMEM)
    dma = pltpu.SemaphoreType.DMA
    return pl.pallas_call(
        functools.partial(exchange_kernel, place, shifts, pairs.uses, operands),
        out_shape=[jax.ShapeDtypeStruct(s.shape, s.dtype) for s in given]
        + pairs.shapes()
        + [jax.ShapeDtypeStruct((left.shape[0], right.shape[0]), jnp.float32)],
        in_specs=[anywhere] * (extra + operands) + [inside, anywhere],
        out_specs=[anywhere] * (extra + len(products)) + [inside],
        scratch_shapes=[pltpu.VMEM(right.shape, right.dtype), dma, dma((extra,)), dma((extra,))]
        + pairs.room(),
        compiler_params=pltpu.CompilerParams(
            collective_id=collective_id, has_side_effects=True, vmem_limit_bytes=56 << 20
        ),
        name=f"exchange{collective_id}",
    )(*given, *pairs.arrays, left, right)


def outer_kernel(count, *refs):
    for i in range(count):
        left, right, result = refs[i], refs[count + i], refs[2 * count + i]
        chunk = chunk_of(left)

        def go(j, _):
            part = pl.ds(pl.multiple_of(j * chunk, chunk), chunk)
            result[part, :] = dot_turned(left[:, part], right[...]).astype(result.dtype)
            return 0

        lax.fori_loop(0, left.shape[1] // chunk, go, 0)


def outer_products(products):
    return pl.pallas_call(
        functools.partial(outer_kernel, len(products)),
        out_shape=Pairs(products).shapes(),
        in_specs=[pl.BlockSpec(memory_space=pltpu.VMEM)] * (2 * len(products)),
        out_specs=[pl.BlockSpec(memory_space=pltpu.VMEM)] * len(products),
        compiler_params=pltpu.CompilerParams(vmem_limit_bytes=32 << 20),
        name="outer",
    )(*[v for v, _ in products], *[w for _, w in products])


def scatter_kernel(place, count, shifts, uses, operands, *refs):
    total, pairs = count + len(shifts), len(uses)
    ins, given = refs[:count], refs[count:total]
    loads, refs = refs[total : total + operands], refs[total + operands :]
    outs, taken, results = refs[:count], refs[count:total], refs[total : total + pairs]
    refs = refs[total + pairs :]
    held, side, rows_y, rows_z, rows_x, rows_e = (
        refs[i * count : (i + 1) * count] for i in range(6)
    )
    la, rc, yr, zr, zs, cs, ys, xs, xr, given_sem, taken_sem, es, er, *room = refs[6 * count :]
    p = place.here()
    depth, tall, across = p.depth, p.tall, p.across
    p.greet(len(shifts) > 0)
    sibling = p.device(p.z, p.y, 1 - p.c)
    half = max(depth // 2, 1)

    def in_order(step):
        lower = 1 - p.z // half

        def right(total, done):
            def go(j, _):
                step(depth - 1 - j // across, (p.x + 1 + j % across) % across, 1, done * across + j)
                return 0

            lax.fori_loop(0, total * across, go, 0)

        def left(total, done):
            def go(j, _):
                step(j // across, (p.x + 1 + j % across) % across, 0, done * across + j)
                return 0

            lax.fori_loop(0, total * across, go, 0)

        early = (depth - 1 - p.z) * lower
        right(early, 0)
        left(p.z, early)
        right((depth - 1 - p.z) * (1 - lower), early + p.z)

        def own(j, _):
            step(p.z, (p.x + 1 + j) % across, None, (depth - 1) * across + j)
            return 0

        lax.fori_loop(0, across, own, 0)

    def local(a, k, z, y, x):
        return pltpu.make_async_copy(ins[a].at[p.slot(z, y, p.c, x)], held[a].at[k, y], la.at[a, k])

    def begin(z, x, way, number):
        k = z * across + x
        for a in range(count):
            for y in range(tall):
                remote(
                    ins[a].at[p.slot(z, y, 1 - p.c, x)],
                    side[a].at[k, y],
                    cs.at[a],
                    rc.at[a, k],
                    sibling,
                ).start()
                local(a, k, z, y, x).start()

    def add(a, target, sources):
        rows = ins[a].shape[1]
        chunk = 16 if rows % 16 == 0 else rows

        def go(i, _):
            part = pl.ds(i * chunk, chunk)
            total = target[part].astype(jnp.float32)
            for source in sources:
                total = total + source[part].astype(jnp.float32)
            target[part] = total.astype(target.dtype)
            return 0

        lax.fori_loop(0, rows // chunk, go, 0)

    def first(z, x, way, number):
        k = z * across + x
        for a in range(count):
            pltpu.make_async_copy(held[a].at[k], held[a].at[k], la.at[a, k]).wait()
            remote(side[a].at[k], side[a].at[k], cs.at[a], rc.at[a, k], sibling).wait_recv()
            for j in range(1, tall):
                y = (p.y + j) % tall
                mine = held[a].at[k, y]

                def along_y(sources, mine=mine, j=j, y=y, a=a):
                    add(a, mine, sources)
                    remote(
                        mine,
                        rows_y[a].at[k, tall - j - 1],
                        ys.at[a],
                        yr.at[a, k],
                        p.device(p.z, y, p.c),
                    ).start()

                @pl.when((p.c == 0) & (z == p.detour(p.z)))
                def _(mine=mine, j=j, y=y, a=a):
                    add(a, mine, [side[a].at[k, y]])
                    remote(
                        mine,
                        rows_e[a].at[x, j - 1],
                        es.at[a],
                        er.at[a, x * (tall - 1) + j - 1],
                        p.device(p.partner(), p.y, p.c),
                    ).start()

                @pl.when((p.c == 0) & (z == p.detour(p.partner())))
                def _(j=j, y=y, a=a, along_y=along_y):
                    part = rows_e[a].at[x, j - 1]
                    remote(
                        part, part, cs.at[a], er.at[a, x * (tall - 1) + j - 1], sibling
                    ).wait_recv()
                    along_y([side[a].at[k, y], part])

                @pl.when((p.c == 1) | ((z != p.detour(p.z)) & (z != p.detour(p.partner()))))
                def _(y=y, a=a, along_y=along_y):
                    along_y([side[a].at[k, y]])

            add(a, held[a].at[k, p.y], [side[a].at[k, p.y]])

    products = Products(uses, loads, results, room)
    items = depth * across

    def second(z, x, way, number):
        k = z * across + x
        for i in range(pairs):
            turn = i * items // pairs
            if (way is None) == (turn >= (depth - 1) * across):
                pl.when(number == turn)(functools.partial(products.run, i))
        for a in range(count):
            mine = held[a].at[k, p.y]
            if tall > 1:

                @pl.when((p.c == 1) | (z != p.detour(p.z)))
                def _(a=a, mine=mine):
                    part = rows_y[a].at[k]
                    remote(part, part, cs.at[a], yr.at[a, k], sibling).wait_recv()
                    add(a, mine, [rows_y[a].at[k, j] for j in range(tall - 1)])

            def from_z(index):
                part = rows_z[a].at[index]
                remote(part, part, cs.at[a], zr.at[a, index], sibling).wait_recv()
                add(a, mine, [part])

            def send(index, target):
                remote(mine, rows_z[a].at[index], zs.at[a, k], zr.at[a, index], target).start()

            if way is None or way == 1:
                pl.when(p.z > 0)(functools.partial(from_z, k))
            if way is None:
                pl.when(p.z < depth - 1)(functools.partial(from_z, depth * across + x))
            if way == 0:
                pl.when(p.z < depth - 1)(functools.partial(from_z, k))
            if way == 1:
                send(k, p.device(p.z + 1, p.y, p.c))
            if way == 0:
                left = p.device(p.z - 1, p.y, p.c)

                @pl.when(z == p.z - 1)
                def _():
                    send(depth * across + x, left)

                @pl.when(z < p.z - 1)
                def _():
                    send(k, left)

            if way is None and across > 1:

                @pl.when(x != p.x)
                def _():
                    remote(
                        mine,
                        rows_x[a].at[(p.x - x + across) % across - 1],
                        xs.at[a],
                        xr.at[a],
                        p.device(p.z, p.y, p.c, x),
                    ).start()

    ahead = min(across + 1 if across > 1 else 2, items)
    lower = 1 - p.z // half
    switch = lower * (depth - 1 - p.z) + (1 - lower) * p.z

    def first_at(number):
        j = number // across
        own = j // (depth - 1)
        past = (j - switch + depth) // depth
        down, up = depth - 1 - j, j
        down_late, up_late = depth - 1 - (j - switch), j - switch
        z = lower * ((1 - past) * down + past * up_late)
        z = z + (1 - lower) * ((1 - past) * up + past * down_late)
        z = own * p.z + (1 - own) * z
        first(z, (p.x + 1 + number % across) % across, None, number)

    def both(z, x, way, number):
        if way is not None:

            @pl.when(number + ahead < items)
            def _():
                first_at(number + ahead)

        second(z, x, way, number)

    swaps = Swaps(p, shifts, given, taken, given_sem, taken_sem)
    swaps.start()
    in_order(begin)
    products.start()
    lax.fori_loop(0, ahead, lambda n, _: (first_at(n), 0)[1], 0)
    in_order(both)
    k = p.z * across + p.x
    for a in range(count):
        mine = held[a].at[k, p.y]
        sources = []
        if across > 1:
            remote(rows_x[a], rows_x[a], xs.at[a], xr.at[a], sibling).wait()
            sources = [rows_x[a].at[j] for j in range(across - 1)]
        rows = ins[a].shape[1]
        chunk = 16 if rows % 16 == 0 else rows

        def go(i, _):
            part = pl.ds(i * chunk, chunk)
            total = mine[part].astype(jnp.float32)
            for source in sources:
                total = total + source[part].astype(jnp.float32)
            outs[a][part] = total
            return 0

        lax.fori_loop(0, rows // chunk, go, 0)
        remote(side[a], side[a], cs.at[a], rc.at[a, 0], sibling).wait_send()
        if tall > 1:

            @pl.when(p.c == 1)
            def _(a=a):
                remote(rows_y[a], rows_y[a], ys.at[a], rc.at[a, 0], sibling).wait_send()

            @pl.when(p.c == 0)
            def _(a=a):
                part = rows_y[a].at[pl.ds(0, (depth - 1) * across)]
                remote(part, part, ys.at[a], rc.at[a, 0], sibling).wait_send()
                remote(rows_e[a], rows_e[a], es.at[a], rc.at[a, 0], sibling).wait_send()

        def wait_z(k, _):
            @pl.when(k // across != p.z)
            def _():
                remote(mine, rows_z[a].at[0], zs.at[a, k], rc.at[a, 0], sibling).wait_send()

            return 0

        lax.fori_loop(0, depth * across, wait_z, 0)

    swaps.wait()


def scatter(partials, wide, collective_id, swapped=(), products=()):
    group, peers = lax.axis_size("expert"), lax.axis_size("fsdp")
    place = Place(group, peers, wide)
    given, shifts = split_swaps(swapped)
    pairs = Pairs(products)
    count, extra, operands = len(partials), len(given), len(pairs.arrays)
    dma = pltpu.SemaphoreType.DMA
    items = place.depth * place.across

    def room(*lead):
        return [pltpu.VMEM(lead + s.shape[1:], s.dtype) for s in partials]

    return pl.pallas_call(
        functools.partial(scatter_kernel, place, count, shifts, pairs.uses, operands),
        out_shape=[jax.ShapeDtypeStruct(s.shape[1:], jnp.float32) for s in partials]
        + [jax.ShapeDtypeStruct(s.shape, s.dtype) for s in given]
        + pairs.shapes(),
        in_specs=[pl.BlockSpec(memory_space=pl.ANY)] * (count + extra + operands),
        out_specs=[pl.BlockSpec(memory_space=pltpu.VMEM)] * count
        + [pl.BlockSpec(memory_space=pl.ANY)] * extra
        + [pl.BlockSpec(memory_space=pl.ANY)] * len(products),
        scratch_shapes=room(items, place.tall)
        + room(items, place.tall)
        + room(items, max(place.tall - 1, 1))
        + room(items + place.across)
        + room(max(place.across - 1, 1))
        + room(place.across, max(place.tall - 1, 1))
        + [
            dma((count, items)),
            dma((count, items)),
            dma((count, items)),
            dma((count, items + place.across)),
            dma((count, items)),
            dma((count,)),
            dma((count,)),
            dma((count,)),
            dma((count,)),
            dma((max(extra, 1),)),
            dma((max(extra, 1),)),
            dma((count,)),
            dma((count, place.across * max(place.tall - 1, 1))),
        ]
        + pairs.room(),
        compiler_params=pltpu.CompilerParams(
            collective_id=collective_id, has_side_effects=True, vmem_limit_bytes=60 << 20
        ),
        name=f"scatter{collective_id}",
    )(*partials, *given, *pairs.arrays)


def dot_plain(left, right):
    return jnp.dot(left, right, preferred_element_type=jnp.float32)


def dot_across(left, right):
    return lax.dot_general(left, right, (((1,), (1,)), ((), ())), preferred_element_type=jnp.float32)


def dot_turned(left, right):
    return lax.dot_general(left, right, (((0,), (0,)), ((), ())), preferred_element_type=jnp.float32)


def ffn_kernel(peers, sources, numbers, fill, *refs):
    hid, cot, ranks = refs[:3]
    gates, ups, downs = (refs[3 + i * peers : 3 + (i + 1) * peers] for i in range(3))
    router, shared_in, shared_out = refs[3 + 3 * peers : 6 + 3 * peers]
    refs = refs[6 + 3 * peers :]
    rows, d_out = refs[:peers], refs[peers : 2 * peers]
    out_part, back_part, act, d_g, d_u, d_log, s_act, s_grad = refs[2 * peers : 8 + 2 * peers]
    rows_here, cots_here = refs[8 + 2 * peers :]
    f32, bf16 = jnp.float32, jnp.bfloat16
    step = pl.program_id(0)
    tok_rows = hid.shape[1]
    capacity = rows_here.shape[0] // sources
    width = hid.shape[2] // peers
    eid, start, fid = numbers[0], numbers[1], numbers[2]
    scale = fill[0]

    def length(s):
        return numbers[3 + step * sources + s]

    def columns(r):
        return pl.ds(pl.multiple_of((fid + r) % peers * width, width), width)

    scales = []
    picks = []
    for s in range(sources):
        part = pl.ds(s * capacity, capacity)
        slot = lax.broadcasted_iota(jnp.int32, (capacity, tok_rows), 0).astype(f32)
        pick = jnp.where(ranks[s] == slot, 1.0, 0.0)
        lane = start + lax.broadcasted_iota(jnp.int32, (1, tok_rows), 1)
        alive = jnp.where(lane < length(s), scale, 0.0)
        scales.append(jnp.sum(pick * alive, axis=1, keepdims=True))
        pick = pick.astype(bf16)
        picks.append(pick)
        rows_here[part, :] = dot_plain(pick, hid[s]).astype(bf16)
        cots_here[part, :] = dot_plain(pick, cot[s]).astype(bf16)
    row_scale = jnp.concatenate(scales, axis=0)
    logits = dot_plain(rows_here[...], router[...])
    top = jnp.max(logits, axis=1, keepdims=True)
    powers = jnp.exp(logits - top)
    probs = powers / jnp.sum(powers, axis=1, keepdims=True)
    own = (lax.broadcasted_iota(jnp.int32, (1, probs.shape[1]), 1) == eid).astype(f32)
    gate = jnp.sum(probs * own, axis=1, keepdims=True)

    for r in range(peers):
        rows[r][...] = rows_here[:, columns(r)]

    def summed(terms):
        total = terms[0]
        for term in terms[1:]:
            total = total + term
        return total

    g = summed([dot_plain(rows[r][...], gates[r][...]) for r in range(peers)])
    u = summed([dot_plain(rows[r][...], ups[r][...]) for r in range(peers)])
    sigma = 1.0 / (1.0 + jnp.exp(-g))
    act_now = (g * sigma * u).astype(bf16)
    act[...] = act_now
    d_gate = jnp.zeros_like(gate)
    weighted = []
    for r in range(peers):
        out = dot_plain(act_now, downs[r][...]).astype(bf16).astype(f32)
        row_cot = cots_here[:, columns(r)].astype(f32)
        d_out[r][...] = ((gate * row_scale) * row_cot).astype(bf16)
        d_gate = d_gate + jnp.sum(row_cot * out, axis=1, keepdims=True)
        weighted.append((gate * out).astype(bf16))
    d_gate = d_gate * row_scale
    d_act = summed([dot_across(d_out[r][...], downs[r][...]) for r in range(peers)])
    dg_now = (d_act * u * (sigma * (1.0 + g * (1.0 - sigma)))).astype(bf16)
    du_now = (d_act * (g * sigma)).astype(bf16)
    d_g[...] = dg_now
    d_u[...] = du_now
    dl_now = (gate * d_gate * (own - probs)).astype(bf16)
    d_log[...] = dl_now
    d_rows = []
    for r in range(peers):
        total = dot_across(dg_now, gates[r][...]) + dot_across(du_now, ups[r][...])
        total = total + dot_across(dl_now, router[columns(r), :])
        d_rows.append(total.astype(bf16))
    units = shared_out.shape[0]
    total_rows = sources * tok_rows
    hid_all = hid[...].reshape(total_rows, hid.shape[2])
    cot_all = cot[...].reshape(total_rows, hid.shape[2])
    both = dot_plain(hid_all, shared_in[...])
    sg, su = both[:, :units], both[:, units:]
    s_sigma = 1.0 / (1.0 + jnp.exp(-sg))
    s_now = sg * s_sigma * su
    column = lax.broadcasted_iota(jnp.int32, (tok_rows, 1), 0) + start
    alive = jnp.concatenate(
        [jnp.where(column < length(s), scale, 0.0) for s in range(sources)], axis=0
    )
    d_s = dot_across(cot_all, shared_out[...]) * alive
    s_act[...] = (s_now * alive).astype(bf16)
    s_low = s_now.astype(bf16)
    d_sg = (d_s * su * (s_sigma * (1.0 + sg * (1.0 - s_sigma)))).astype(bf16)
    d_su = (d_s * (sg * s_sigma)).astype(bf16)
    s_grad[:, pl.ds(0, units)] = d_sg
    s_grad[:, pl.ds(units, units)] = d_su
    for s in range(sources):
        part = slice(s * capacity, (s + 1) * capacity)
        span = slice(s * tok_rows, (s + 1) * tok_rows)
        for r in range(peers):
            out_part[s, :, columns(r)] = (
                dot_turned(picks[s], weighted[r][part])
                + dot_plain(s_low[span], shared_out[:, columns(r)])
            ).astype(bf16)
            back_part[s, :, columns(r)] = (
                dot_turned(picks[s], d_rows[r][part])
                + dot_across(s_grad[span, :], shared_in[columns(r), :])
            ).astype(bf16)


def ffn(capacity, numbers, fill, hid, cot, ranks, gates, ups, downs, router, shared_in, shared_out):
    group, tok_rows, dim = hid.shape
    peers = len(gates)
    sources = max(1, min(4, 256 // capacity))
    hidden = gates[0].shape[1]
    units = shared_out.shape[0]
    rows = sources * capacity
    bf16 = jnp.bfloat16

    def whole(array):
        return pl.BlockSpec(
            array.shape, lambda i, *_: (0,) * array.ndim, pipeline_mode=pl.Buffered(1)
        )

    def tile(*shape):
        return pl.BlockSpec(shape, lambda i, *_: (i,) + (0,) * (len(shape) - 1))

    pairs = group * capacity
    weights = [*gates, *ups, *downs, router, shared_in, shared_out]
    return pl.pallas_call(
        functools.partial(ffn_kernel, peers, sources),
        out_shape=[jax.ShapeDtypeStruct((pairs, dim // peers), bf16)] * (2 * peers)
        + [
            jax.ShapeDtypeStruct((group, tok_rows, dim), bf16),
            jax.ShapeDtypeStruct((group, tok_rows, dim), bf16),
            jax.ShapeDtypeStruct((pairs, hidden), bf16),
            jax.ShapeDtypeStruct((pairs, hidden), bf16),
            jax.ShapeDtypeStruct((pairs, hidden), bf16),
            jax.ShapeDtypeStruct((pairs, router.shape[1]), bf16),
            jax.ShapeDtypeStruct((group * tok_rows, units), bf16),
            jax.ShapeDtypeStruct((group * tok_rows, 2 * units), bf16),
        ],
        grid_spec=pltpu.PrefetchScalarGridSpec(
            num_scalar_prefetch=2,
            grid=(group // sources,),
            in_specs=[
                tile(sources, tok_rows, dim),
                tile(sources, tok_rows, dim),
                tile(sources, 1, tok_rows),
            ]
            + [whole(w) for w in weights],
            out_specs=[tile(rows, dim // peers)] * (2 * peers)
            + [
                tile(sources, tok_rows, dim),
                tile(sources, tok_rows, dim),
                tile(rows, hidden),
                tile(rows, hidden),
                tile(rows, hidden),
                tile(rows, router.shape[1]),
                tile(sources * tok_rows, units),
                tile(sources * tok_rows, 2 * units),
            ],
            scratch_shapes=[pltpu.VMEM((rows, dim), bf16)] * 2,
        ),
        compiler_params=pltpu.CompilerParams(vmem_limit_bytes=62 << 20),
        cost_estimate=pl.CostEstimate(
            flops=18 * pairs * dim * hidden, bytes_accessed=60 << 20, transcendentals=1 << 22
        ),
        name="ffn",
    )(numbers, fill, hid, cot, ranks, *weights)


def both_keys(keyval, rot):
    f32 = jnp.float32
    rot = rot.astype(f32)
    first = jnp.concatenate([keyval[:, :DN].astype(f32), rot], axis=1)
    second = jnp.concatenate([keyval[:, DN + DV : 2 * DN + DV].astype(f32), rot], axis=1)
    second = pltpu.roll(second, DN + DR, 1)
    return first.astype(jnp.bfloat16), second.astype(jnp.bfloat16)


def turn(array, plain, ahead, behind):
    width = array.shape[1]
    return (
        array * plain
        + pltpu.roll(array, width - DR // 2, 1) * ahead
        + pltpu.roll(array, DR // 2, 1) * behind
    )


def attend_kernel(numbers, hidden, w_query, latent, w_expand, rot, plain, ahead, behind, *outs):
    query, keyval, probs, context = outs
    bf16 = jnp.bfloat16
    turned = turn(dot_plain(hidden[...], w_query[...]), plain[...], ahead[...], behind[...])
    query_now = turned.astype(bf16)
    query[...] = query_now
    keyval[...] = dot_plain(latent[...], w_expand[...]).astype(bf16)
    rows, keys = query.shape[0], keyval.shape[0]
    row = lax.broadcasted_iota(jnp.int32, (rows, keys), 0) + numbers[0]
    key = lax.broadcasted_iota(jnp.int32, (rows, keys), 1)
    allowed = (key <= row) & (key < numbers[1])
    for i, keys_now in enumerate(both_keys(keyval[...], rot[...])):
        scores = dot_across(query_now, keys_now) * (DN + DR) ** (-0.5)
        scores = jnp.where(allowed, scores, masked_value)
        powers = jnp.exp(scores - jnp.max(scores, axis=1, keepdims=True))
        share = powers / jnp.sum(powers, axis=1, keepdims=True)
        probs[i] = share
        value = keyval[:, pl.ds(i * (DN + DV) + DN, DV)]
        context[:, pl.ds(i * DV, DV)] = dot_plain(share.astype(bf16), value).astype(bf16)


def attend(numbers, hidden, w_query, latent, w_expand, rot, turns):
    rows, dim = hidden.shape
    keys, rank = latent.shape
    bf16 = jnp.bfloat16

    def still(array):
        return pl.BlockSpec(array.shape, lambda i, *_: (0,) * array.ndim)

    def columns(height, width):
        return pl.BlockSpec((height, width), lambda i, *_: (0, i))

    return pl.pallas_call(
        attend_kernel,
        out_shape=[
            jax.ShapeDtypeStruct((rows, H * (DN + DR)), bf16),
            jax.ShapeDtypeStruct((keys, H * (DN + DV)), bf16),
            jax.ShapeDtypeStruct((H, rows, keys), jnp.float32),
            jax.ShapeDtypeStruct((rows, H * DV), bf16),
        ],
        grid_spec=pltpu.PrefetchScalarGridSpec(
            num_scalar_prefetch=1,
            grid=(H // 2,),
            in_specs=[
                still(hidden),
                columns(dim, 2 * (DN + DR)),
                still(latent),
                columns(rank, 2 * (DN + DV)),
                still(rot),
                *[still(t) for t in turns],
            ],
            out_specs=[
                columns(rows, 2 * (DN + DR)),
                columns(keys, 2 * (DN + DV)),
                pl.BlockSpec((2, rows, keys), lambda i, *_: (i, 0, 0)),
                columns(rows, 2 * DV),
            ],
        ),
        compiler_params=pltpu.CompilerParams(vmem_limit_bytes=40 << 20),
        name="attend",
    )(numbers, hidden, w_query, latent, w_expand, rot, *turns)


def attend_back_kernel(d_res, w_output, query, keyval, probs, rot, plain, ahead, behind, *outs):
    d_query, d_keyval, d_rot = outs
    f32, bf16 = jnp.float32, jnp.bfloat16
    scale = (DN + DR) ** (-0.5)
    query_now = query[...]
    total = jnp.zeros(query.shape, f32)
    rot_total = jnp.zeros(d_rot.shape, f32)
    for i, keys_now in enumerate(both_keys(keyval[...], rot[...])):
        d_context = dot_across(d_res[...], w_output[pl.ds(i * DV, DV), :]).astype(bf16)
        share = probs[i]
        at = i * (DN + DV)
        d_value = dot_turned(share.astype(bf16), d_context)
        d_share = dot_across(d_context, keyval[:, pl.ds(at + DN, DV)])
        d_score = share * (d_share - jnp.sum(share * d_share, axis=1, keepdims=True))
        d_score = d_score.astype(bf16)
        total = total + dot_plain(d_score, keys_now) * scale
        d_key = dot_turned(d_score, query_now) * scale
        if i == 1:
            d_key = pltpu.roll(d_key, DN + DR, 1)
        d_keyval[:, pl.ds(at, DN)] = d_key[:, :DN].astype(bf16)
        d_keyval[:, pl.ds(at + DN, DV)] = d_value.astype(bf16)
        rot_total = rot_total + d_key[:, DN : 2 * DN]
    d_query[...] = turn(total, plain[...], -ahead[...], -behind[...]).astype(bf16)

    @pl.when(pl.program_id(0) == 0)
    def _():
        d_rot[...] = rot_total

    @pl.when(pl.program_id(0) != 0)
    def _():
        d_rot[...] += rot_total


def attend_back(d_res, w_output, query, keyval, probs, rot, turns):
    rows, dim = d_res.shape
    keys = keyval.shape[0]
    bf16 = jnp.bfloat16

    def still(array):
        return pl.BlockSpec(array.shape, lambda i: (0,) * array.ndim)

    def columns(height, width):
        return pl.BlockSpec((height, width), lambda i: (0, i))

    return pl.pallas_call(
        attend_back_kernel,
        out_shape=[
            jax.ShapeDtypeStruct(query.shape, bf16),
            jax.ShapeDtypeStruct(keyval.shape, bf16),
            jax.ShapeDtypeStruct((keys, DN), jnp.float32),
        ],
        grid=(H // 2,),
        in_specs=[
            still(d_res),
            pl.BlockSpec((2 * DV, dim), lambda i: (i, 0)),
            columns(rows, 2 * (DN + DR)),
            columns(keys, 2 * (DN + DV)),
            pl.BlockSpec((2, rows, keys), lambda i: (i, 0, 0)),
            still(rot),
            *[still(t) for t in turns],
        ],
        out_specs=[
            columns(rows, 2 * (DN + DR)),
            columns(keys, 2 * (DN + DV)),
            pl.BlockSpec((keys, DN), lambda i: (0, 0)),
        ],
        compiler_params=pltpu.CompilerParams(vmem_limit_bytes=40 << 20),
        name="attend_back",
    )(d_res, w_output, query, keyval, probs, rot, *turns)


def from_peers(block):
    size = lax.axis_size("fsdp")
    return [block] + [
        lax.ppermute(block, "fsdp", [(j, (j - r) % size) for j in range(size)])
        for r in range(1, size)
    ]


def sum_to_peers(term):
    size = lax.axis_size("fsdp")
    arrived = [
        lax.ppermute(term(r), "fsdp", [(j, (j + r) % size) for j in range(size)])
        for r in range(1, size)
    ]
    return arrived


def body(
    tokens,
    cotangent,
    routes,
    lengths,
    attn_gain,
    q_weight,
    kva_weight,
    kv_gain,
    kvb_weight,
    out_weight,
    ffn_gain,
    router_weight,
    shared_gate,
    shared_up,
    shared_down,
    expert_gate,
    expert_up,
    expert_down,
):
    bf16, f32 = jnp.bfloat16, jnp.float32
    tok_rows, dim = tokens.shape
    peers = lax.axis_size("fsdp")
    group = lax.axis_size("expert")
    fid, eid = lax.axis_index("fsdp"), lax.axis_index("expert")
    seq_len = tok_rows * peers
    slot_total = seq_len * group
    expert_count = router_weight.shape[1]
    capacity = max(4, 5 * tok_rows * TOPK // (4 * expert_count))
    capacity = -(-capacity // 16) * 16
    half = dim // peers
    plane_rows = group * tok_rows
    pairs = group * capacity

    positions = fid * tok_rows + jnp.arange(tok_rows, dtype=jnp.int32)
    seq_length = lengths[0]
    valid_mask = (positions < seq_length).astype(f32)
    expert_ids = jnp.arange(expert_count, dtype=jnp.int32)
    hot_sum = jnp.sum((routes[:, :, None] == expert_ids[None, None, :]).astype(f32), axis=1)
    local_counts = jnp.sum(hot_sum * valid_mask[:, None], axis=0)

    def lane_row(vector):
        return jnp.pad(vector.astype(f32), (0, tok_rows - vector.shape[0]))[None, :]

    small = jnp.concatenate(
        [routes.T.astype(f32)]
        + [lane_row(v) for v in (attn_gain, ffn_gain, kv_gain, local_counts, lengths)]
        + [jnp.zeros((16 - TOPK - 5, tok_rows), f32)],
        axis=0,
    )
    devices = group * peers
    turns = range(1, peers)
    w_query, w_compress, w_expand, w_output, w_router, small_all, *more = gather(
        [q_weight, kva_weight, kvb_weight, out_weight, router_weight, small],
        True,
        0,
        [(expert_gate[0], -r) for r in turns] + [(expert_up[0], -r) for r in turns],
    )
    gate_parts = [expert_gate[0]] + more[: peers - 1]
    up_parts = [expert_up[0]] + more[peers - 1 :]
    w_query, w_compress, w_expand, w_output, w_router = (
        w.reshape(-1, w.shape[-1]) for w in (w_query, w_compress, w_expand, w_output, w_router)
    )
    gain_attn = small_all[:, TOPK, : attn_gain.shape[0]].reshape(-1)
    gain_ffn = small_all[:, TOPK + 1, : ffn_gain.shape[0]].reshape(-1)
    gain_latent = small_all[:, TOPK + 2, : kv_gain.shape[0]].reshape(-1)
    route_counts = jnp.sum(small_all[:, TOPK + 3, :expert_count], axis=0)
    all_lengths = small_all.reshape(group, peers, 16, tok_rows)[:, 0, TOPK + 4, 0]
    valid_total = jnp.sum(all_lengths)
    fill_scale = slot_total / valid_total
    plane_small = lax.dynamic_index_in_dim(
        small_all.reshape(group, peers, 16, tok_rows), fid, axis=1, keepdims=False
    )
    units = shared_gate.shape[1] // group
    lanes_more = -units % 128
    pieces = jnp.concatenate(
        [
            jnp.pad(w.reshape(-1, group, units), ((0, 0), (0, 0), (0, lanes_more)))
            for w in (shared_gate, shared_up)
        ],
        axis=2,
    ).transpose(1, 0, 2)
    pieces = lax.all_to_all(pieces, "expert", split_axis=0, concat_axis=0, tiled=True)
    sd_weight = jnp.roll(jnp.stack(from_peers(shared_down)), fid, axis=0).reshape(units, dim)
    sd_weight = jnp.pad(sd_weight, ((0, lanes_more), (0, 0)))
    cosine, sine_vals = rope_tables(positions)
    tokens_f = tokens.astype(f32)
    cot_ready, small_all = lax.optimization_barrier((cotangent, small_all))
    cot_plane = lax.all_gather(cot_ready, "expert", axis=0, tiled=True)
    normed_one, inverse_one = rms_norm(tokens_f, gain_attn)
    hidden_one = normed_one.astype(bf16)
    compressed = jnp.dot(hidden_one, w_compress, preferred_element_type=f32)
    latent_raw = compressed[:, :KVR]
    latent_norm, inverse_kv = rms_norm(latent_raw, gain_latent)
    latent = latent_norm.astype(bf16)
    key_rot = rotate(compressed[:, KVR:], cosine, sine_vals).astype(bf16)
    latent_rot = lax.all_gather(
        jnp.concatenate([latent, key_rot], axis=1), "fsdp", axis=0, tiled=True
    )
    down_own, latent_rot = lax.optimization_barrier((expert_down[0], latent_rot))
    down_parts = from_peers(down_own)
    all_rot = jnp.pad(latent_rot[:, KVR:], ((0, 0), (0, 2 * DN - DR)))

    def spread_columns(first, second, rest):
        one = jnp.concatenate([jnp.full((tok_rows, DN), rest, f32), first, second], axis=1)
        return jnp.concatenate([one, one], axis=1)

    zero = jnp.zeros_like(cosine)
    rotations = [
        spread_columns(cosine, cosine, 1.0),
        spread_columns(-sine_vals, zero, 0.0),
        spread_columns(zero, sine_vals, 0.0),
    ]
    query_all, keyval, probs_attn, context = attend(
        jnp.stack([fid * tok_rows, seq_length]).astype(jnp.int32),
        hidden_one,
        w_query,
        latent_rot[:, :KVR],
        w_expand,
        all_rot,
        rotations,
    )
    residual = tokens_f + jnp.dot(context, w_output, preferred_element_type=f32)
    normed_two, inverse_two = rms_norm(residual, gain_ffn)
    hidden_two = normed_two.astype(bf16)
    hid3, *more = gather([hidden_two], False, 1, [(pieces, -r) for r in turns])
    gu_weight = jnp.roll(jnp.stack([pieces] + more), fid, axis=0)
    gu_weight = gu_weight.transpose(1, 0, 2, 3).reshape(dim, -1)
    hid_plane = hid3.reshape(plane_rows, dim)
    cot3 = cot_plane.reshape(group, tok_rows, dim)
    router_probs = jax.nn.softmax(jnp.dot(hidden_two, w_router, preferred_element_type=f32), axis=-1)
    local_shares = jnp.sum(router_probs * valid_mask[:, None], axis=0)
    frequency = expert_count / (TOPK * valid_total) * route_counts
    d_probs_own = balance_weight * valid_mask[:, None] * frequency[None, :] / valid_total
    dlog_own = (
        router_probs * (d_probs_own - jnp.sum(router_probs * d_probs_own, axis=-1, keepdims=True))
    ).astype(bf16)
    named = jnp.any(plane_small[:, :TOPK, :] == eid.astype(f32), axis=1)
    place = jnp.arange(tok_rows)
    before = (place[:, None] < place[None, :]).astype(bf16)
    ranks = jnp.dot(named.astype(bf16), before, preferred_element_type=f32)
    ranks = jnp.where(named, ranks, -1.0)[:, None, :]
    numbers = jnp.concatenate(
        [jnp.stack([eid, fid * tok_rows, fid]).astype(jnp.int32), all_lengths.astype(jnp.int32)]
    )
    made = ffn(
        capacity,
        numbers,
        fill_scale.reshape(1),
        hid3,
        cot3,
        ranks,
        gate_parts,
        up_parts,
        down_parts,
        w_router,
        gu_weight,
        sd_weight,
    )

    rows_in, d_out = made[:peers], made[peers : 2 * peers]
    out_part, back_part, act, d_hidden_g, d_hidden_u, dlog_rows, shared_scaled, d_gu = made[
        2 * peers :
    ]

    def outer(left, right):
        return lax.dot_general(left, right, (((0,), (0,)), ((), ())), preferred_element_type=f32)

    def back(left, weight):
        return lax.dot_general(left, weight, (((1,), (1,)), ((), ())), preferred_element_type=f32)

    def gate_term(r):
        return outer(rows_in[r], d_hidden_g)

    def up_term(r):
        return outer(rows_in[r], d_hidden_u)

    def down_term(r):
        return outer(act, d_out[r])

    def with_peers(term):
        arrived = sum_to_peers(lambda r: term(r).astype(bf16))
        total = term(0)
        for block in arrived:
            total = total + block.astype(f32)
        return total

    def plus(total, blocks):
        for block in blocks:
            total = total + block.astype(f32)
        return total

    d_hidden_two, *more = scatter(
        [back_part],
        False,
        2,
        [(gate_term(r).astype(bf16), r) for r in turns],
        [
            (hid_plane, d_gu),
            (shared_scaled, cot_plane),
            (rows_in[1], d_hidden_u),
            (act, d_out[1]),
            (rows_in[0], d_hidden_g),
            (rows_in[0], d_hidden_u),
            (act, d_out[0]),
        ]
        if peers == 2
        else [],
    )
    gate_blocks = more[: peers - 1]
    if peers == 2:
        d_gu_weight, d_sd, *others, gate_own, up_own, down_own = more[1:]
    else:
        d_gu_weight = outer(hid_plane, d_gu).astype(bf16)
        d_sd = outer(shared_scaled, cot_plane).astype(bf16)
        others = [up_term(r).astype(bf16) for r in turns]
        others = others + [down_term(r).astype(bf16) for r in turns]
        gate_own, up_own, down_own = gate_term(0), up_term(0), down_term(0)
    d_sd = d_sd[:units]
    out_part, d_hidden_two = lax.optimization_barrier((out_part, d_hidden_two))
    out_sum = lax.psum_scatter(
        out_part.reshape(plane_rows, dim), "expert", scatter_dimension=0, tiled=True
    )
    egate_grad = plus(gate_own.astype(f32), gate_blocks)[None]
    d_hidden_two = d_hidden_two + back(dlog_own, w_router)
    router_parts = jnp.stack([outer(rows_in[r], dlog_rows) for r in range(peers)])
    router_grad = jnp.roll(router_parts, fid, axis=0).reshape(dim, -1) + outer(hidden_two, dlog_own)
    d_gu_blocks = d_gu_weight.reshape(group, peers, dim // (group * peers), -1)
    d_sd_blocks = d_sd.reshape(peers, units // peers, dim)

    def gu_term(r):
        return lax.dynamic_index_in_dim(d_gu_blocks, (fid + r) % peers, axis=1, keepdims=False)

    def sd_term(r):
        return lax.dynamic_index_in_dim(d_sd_blocks, (fid + r) % peers, axis=0, keepdims=False)

    gu_sum = plus(gu_term(0).astype(f32), sum_to_peers(gu_term)).astype(bf16)
    sdown_grad = plus(sd_term(0).astype(f32), sum_to_peers(sd_term))
    grad_out = cotangent.astype(f32) * (valid_mask * fill_scale)[:, None]
    d_residual, d_ffn_gain = norm_back(d_hidden_two, residual, inverse_two, gain_ffn)
    d_residual = d_residual + grad_out
    d_residual_low = d_residual.astype(bf16)
    d_query, d_keyval_all, d_key_rot = attend_back(
        d_residual_low, w_output, query_all, keyval, probs_attn, all_rot, rotations
    )
    d_key_rot = d_key_rot[:, :DR]

    def own_rows(array, r):
        return lax.dynamic_slice_in_dim(array, (fid + r) % peers * tok_rows, tok_rows, axis=0)

    swapped = [(own_rows(d_keyval_all, r).astype(bf16), r) for r in turns]
    swapped = swapped + [(own_rows(d_key_rot, r).astype(bf16), r) for r in turns]
    *arrived, d_output_w, d_query_w, d_hidden_one = exchange(
        4,
        swapped,
        [(context, d_residual_low), (hidden_one, d_query)],
        d_query,
        w_query,
    )
    up_others, arrived[0] = lax.optimization_barrier((others[: peers - 1], arrived[0]))
    size = peers
    up_blocks = [
        lax.ppermute(w, "fsdp", [(j, (j + r) % size) for j in range(size)])
        for w, r in zip(up_others, turns)
    ]
    own_dkeyval = plus(own_rows(d_keyval_all, 0).astype(f32), arrived[: peers - 1])
    own_dkeyrot = plus(own_rows(d_key_rot, 0), arrived[peers - 1 :])
    gu_sum, own_dkeyval = lax.optimization_barrier((gu_sum, own_dkeyval))
    gu_sum = lax.all_to_all(gu_sum, "expert", split_axis=0, concat_axis=0, tiled=True)
    d_keyval = own_dkeyval.astype(bf16)
    d_latent = back(d_keyval, w_expand)
    d_latent_raw, d_latent_gain = norm_back(d_latent, latent_raw, inverse_kv, gain_latent)
    d_compressed = jnp.concatenate(
        [d_latent_raw, rotate_back(own_dkeyrot, cosine, sine_vals)], axis=-1
    ).astype(bf16)
    d_compress_w, d_expand_w = outer_products([(hidden_one, d_compressed), (latent, d_keyval)])
    d_hidden_one = d_hidden_one + back(d_compressed, w_compress)
    d_tokens, d_attn_gain = norm_back(d_hidden_one, tokens_f, inverse_one, gain_attn)
    tokens_grad = d_tokens + d_residual
    def lanes(vector):
        piece = vector.reshape(devices, -1)
        return jnp.pad(piece, ((0, 0), (0, tok_rows - piece.shape[1])))

    small_grads = jnp.stack(
        [
            lanes(d_attn_gain),
            lanes(d_latent_gain),
            lanes(d_ffn_gain),
            lanes(jnp.tile(local_shares, devices)),
        ]
        + [jnp.zeros((devices, tok_rows), f32)] * 4,
        axis=1,
    )
    dense = [
        w.astype(bf16).reshape(devices, -1, w.shape[-1])
        for w in (d_query_w, d_compress_w, d_expand_w, d_output_w, router_grad)
    ]
    q_grad, kva_grad, kvb_grad, out_grad, router_out, smalls, *blocks = scatter(
        dense + [small_grads],
        True,
        3,
        [(w, r) for w, r in zip(others[peers - 1 :], turns)],
    )
    gu_sum, out_sum, smalls = lax.optimization_barrier((gu_sum, out_sum, smalls))
    mixed = (residual + out_sum.astype(f32)).astype(bf16)
    gu_sum = gu_sum.astype(f32).transpose(1, 0, 2)
    sgate_grad = gu_sum[:, :, :units].reshape(shared_gate.shape)
    sup_grad = gu_sum[:, :, units + lanes_more : 2 * units + lanes_more].reshape(shared_up.shape)
    eup_grad = plus(up_own.astype(f32), up_blocks)[None]
    edown_grad = plus(down_own.astype(f32), blocks)[None]
    attn_gain_grad = smalls[0, : attn_gain.shape[0]]
    kv_gain_grad = smalls[1, : kv_gain.shape[0]]
    ffn_gain_grad = smalls[2, : ffn_gain.shape[0]]
    balance = jnp.sum(frequency * (smalls[3, :expert_count] / valid_total))
    return (
        mixed,
        tokens_grad,
        balance,
        attn_gain_grad,
        q_grad,
        kva_grad,
        kv_gain_grad,
        kvb_grad,
        out_grad,
        ffn_gain_grad,
        router_out,
        sgate_grad,
        sup_grad,
        sdown_grad,
        egate_grad,
        eup_grad,
        edown_grad,
    )


def solution(mesh):
    return jax.shard_map(
        body,
        mesh=mesh,
        in_specs=(
            P(("expert", "fsdp"), None),
            P(("expert", "fsdp"), None),
            P(("expert", "fsdp"), None),
            P("expert"),
            P(("expert", "fsdp")),
            P(("expert", "fsdp"), None),
            P(("expert", "fsdp"), None),
            P(("expert", "fsdp")),
            P(("expert", "fsdp"), None),
            P(("expert", "fsdp"), None),
            P(("expert", "fsdp")),
            P(("expert", "fsdp"), None),
            P(("expert", "fsdp"), None),
            P(("expert", "fsdp"), None),
            P(("expert", "fsdp"), None),
            P("expert", "fsdp", None),
            P("expert", "fsdp", None),
            P("expert", None, "fsdp"),
        ),
        out_specs=(
            P(("expert", "fsdp"), None),
            P(("expert", "fsdp"), None),
            P(),
            P(("expert", "fsdp")),
            P(("expert", "fsdp"), None),
            P(("expert", "fsdp"), None),
            P(("expert", "fsdp")),
            P(("expert", "fsdp"), None),
            P(("expert", "fsdp"), None),
            P(("expert", "fsdp")),
            P(("expert", "fsdp"), None),
            P(("expert", "fsdp"), None),
            P(("expert", "fsdp"), None),
            P(("expert", "fsdp"), None),
            P("expert", "fsdp", None),
            P("expert", "fsdp", None),
            P("expert", None, "fsdp"),
        ),
        check_vma=False,
    )
```

```python
import functools

import jax
import jax.numpy as jnp
from jax import lax
from jax.experimental import pallas as pl
from jax.experimental.pallas import tpu as pltpu
from jax.sharding import PartitionSpec as P

D = 2048
H = 16
DN = 128
DR = 64
DV = 128
KVR = 512
TOPK = 6


epsilon = 1e-06
balance_weight = 0.001
masked_value = -1e30


def rms_norm(vector, gain_row):
    inverse = lax.rsqrt(jnp.mean(vector * vector, axis=-1, keepdims=True) + epsilon)
    return (vector * inverse * gain_row, inverse)


def norm_back(grad_in, vector, inverse, gain_row):
    scaled = grad_in * gain_row
    gain_grad = jnp.sum(grad_in * vector * inverse, axis=0)
    vector_grad = inverse * scaled - vector * inverse**3 * jnp.mean(
        scaled * vector, axis=-1, keepdims=True
    )
    return (vector_grad, gain_grad)


def rope_tables(positions):
    half_width = DR // 2
    frequency = 10000.0 ** (-jnp.arange(half_width, dtype=jnp.float32) / half_width)
    angles = positions.astype(jnp.float32)[:, None] * frequency[None, :]
    return (jnp.cos(angles), jnp.sin(angles))


def rotate(vector, cosine, sine_vals):
    half_width = vector.shape[-1] // 2
    first_half = vector[..., :half_width]
    second_half = vector[..., half_width:]
    return jnp.concatenate(
        [
            first_half * cosine - second_half * sine_vals,
            second_half * cosine + first_half * sine_vals,
        ],
        axis=-1,
    )


def rotate_back(grad_in, cosine, sine_vals):
    half_width = grad_in.shape[-1] // 2
    first_half = grad_in[..., :half_width]
    second_half = grad_in[..., half_width:]
    return jnp.concatenate(
        [
            first_half * cosine + second_half * sine_vals,
            second_half * cosine - first_half * sine_vals,
        ],
        axis=-1,
    )


def silu_slope(vector):
    sigmoid_vals = jax.nn.sigmoid(vector)
    return sigmoid_vals * (1.0 + vector * (1.0 - sigmoid_vals))


MESH_IDS = pl.DeviceIdType.MESH


class Place:
    def __init__(self, group, peers, wide):
        self.wide = wide
        self.depth = min(4, group // 2)
        self.tall = group // 2 // self.depth
        self.across = peers if wide else 1
        self.peers = peers
        self.units = self.depth * self.tall * self.across
        self.slots = 2 * self.units

    def here(self):
        e = lax.axis_index("expert")
        self.fsdp = lax.axis_index("fsdp")
        self.c = e % 2
        self.y = e // 2 % self.tall
        self.z = e // (2 * self.tall)
        self.x = self.fsdp if self.wide else 0
        return self

    def detour(self, z):
        return (self.depth - 1) * (1 - z % 2)

    def partner(self):
        return self.z + 1 - self.z % 2 * 2

    def greet_peers(self):
        barrier = pltpu.get_barrier_semaphore()
        for k in range(1, self.peers):
            pl.semaphore_signal(
                barrier,
                inc=1,
                device_id=self.device(self.z, self.y, self.c, (self.fsdp + k) % self.peers),
                device_id_type=MESH_IDS,
            )
        pl.semaphore_wait(barrier, self.peers - 1)

    def slot(self, z, y, c, x):
        return ((z * self.tall + y) * 2 + c) * self.across + x

    def device(self, z, y, c, x=None):
        return ((z * self.tall + y) * 2 + c, self.fsdp if x is None else x)

    def greet(self, swapping):
        barrier = pltpu.get_barrier_semaphore()
        partners = self.peers if swapping or self.wide else 1
        count = 1 + (self.tall - 1) + (partners - 1)

        def signal(target):
            pl.semaphore_signal(barrier, inc=1, device_id=target, device_id_type=MESH_IDS)

        signal(self.device(self.z, self.y, 1 - self.c))
        for k in range(1, self.tall):
            signal(self.device(self.z, (self.y + k) % self.tall, self.c))
        for k in range(1, partners):
            signal(self.device(self.z, self.y, self.c, (self.fsdp + k) % self.peers))

        @pl.when(self.z > 0)
        def _():
            signal(self.device(self.z - 1, self.y, self.c))

        @pl.when(self.z < self.depth - 1)
        def _():
            signal(self.device(self.z + 1, self.y, self.c))

        last = self.depth - 1
        pl.semaphore_wait(barrier, count + 2 - self.z // last - (last - self.z) // last)


def remote(src, dst, send_sem, recv_sem, target):
    return pltpu.make_async_remote_copy(
        src_ref=src,
        dst_ref=dst,
        send_sem=send_sem,
        recv_sem=recv_sem,
        device_id=target,
        device_id_type=MESH_IDS,
    )


class Swaps:
    def __init__(self, place, shifts, given, taken, send_sem, recv_sem):
        self.copies = [
            remote(
                given[i],
                taken[i],
                send_sem.at[i],
                recv_sem.at[i],
                place.device(place.z, place.y, place.c, (place.fsdp + shift) % place.peers),
            )
            for i, shift in enumerate(shifts)
        ]

    def start(self):
        for copy in self.copies:
            copy.start()

    def wait(self):
        for copy in self.copies:
            copy.wait()


def gather_kernel(place, count, shifts, spans, into, *refs):
    total = count + len(shifts)
    ins, given = refs[:count], refs[count:total]
    refs = refs[:total] + refs[total + into :]
    outs, taken = refs[total : total + count], refs[total + count : 2 * total]
    given = [w if at is None else w.at[pl.ds(*at)] for w, at in zip(given, spans)]
    taken = [w if at is None else w.at[pl.ds(*at)] for w, at in zip(taken, spans)]
    near, xs, ys, cs, rc, zs, got, given_sem, taken_sem, es = refs[2 * total :]
    p = place.here()
    depth, tall, across = p.depth, p.tall, p.across
    p.greet(len(shifts) > 0)
    sibling = p.device(p.z, p.y, 1 - p.c)

    def unit(z, y, x):
        return (z * tall + y) * across + x

    def block(a, z, y, x):
        return outs[a].at[p.slot(z, y, p.c, x)]

    def to_z(a, src, z, x, way):
        return remote(
            src,
            block(a, z, p.y, x),
            zs.at[a, way, z * across + x],
            got.at[a, unit(z, p.y, x)],
            p.device(p.z + 2 * way - 1, p.y, p.c),
        )

    def to_y(a, src, z, x, k):
        return remote(
            src,
            block(a, z, p.y, x),
            ys.at[a],
            got.at[a, unit(z, p.y, x)],
            p.device(p.z, (p.y + k) % tall, p.c),
        )

    def to_sibling(a, src, z, y, x):
        return remote(src, block(a, z, y, x), cs.at[a], rc.at[a], sibling)

    def arrived(a, z, y, x):
        remote(block(a, z, y, x), block(a, z, y, x), cs.at[a], got.at[a, unit(z, y, x)], sibling).wait_recv()

    def spread(a, src, z, x, ways):
        for way in ways:

            @pl.when((p.z < depth - 1) if way else (p.z > 0))
            def _():
                to_z(a, src, z, x, way).start()

        @pl.when((p.c == 1) | (z != p.detour(p.z)))
        def _():
            for k in range(1, tall):
                to_y(a, src, z, x, k).start()

        to_sibling(a, src, z, p.y, x).start()

    def to_partner(a, z, y, x, k):
        return remote(
            block(a, z, y, x),
            block(a, z, y, x),
            es.at[a, x * max(tall - 1, 1) + k - 1],
            got.at[a, unit(z, y, x)],
            p.device(p.partner(), p.y, p.c),
        )

    def over_x(step):
        if across == 1:
            step(0)
        else:
            lax.fori_loop(0, across, lambda k, _: (step((p.x + k) % across), 0)[1], 0)

    for a in range(count):
        for k in range(1, across):
            remote(
                ins[a],
                block(a, p.z, p.y, p.x),
                xs.at[a],
                got.at[a, unit(p.z, p.y, p.x)],
                p.device(p.z, p.y, p.c, (p.x + k) % across),
            ).start()
        spread(a, ins[a], p.z, p.x, (0, 1))
        pltpu.make_async_copy(ins[a], block(a, p.z, p.y, p.x), near.at[a]).start()

    swaps = Swaps(p, shifts, given, taken, given_sem, taken_sem)
    swaps.start()
    for k in range(1, across):
        x = (p.x + k) % across
        for a in range(count):
            arrived(a, p.z, p.y, x)
            spread(a, block(a, p.z, p.y, x), p.z, x, (0, 1))

    def from_y(z):
        def step(x):
            for k in range(1, tall):
                y = (p.y + k) % tall
                for a in range(count):
                    arrived(a, z, y, x)

                    @pl.when((p.c == 0) & (z == p.detour(p.partner())))
                    def _(a=a, y=y, k=k):
                        to_partner(a, z, y, x, k).start()

                    to_sibling(a, block(a, z, y, x), z, y, x).start()

        over_x(step)

    for d in range(1, depth + 1):
        if d < depth:

            @pl.when(p.z >= d)
            def _(d=d):
                def step(x):
                    for a in range(count):
                        arrived(a, p.z - d, p.y, x)
                        spread(a, block(a, p.z - d, p.y, x), p.z - d, x, (1,))

                over_x(step)

            @pl.when(p.z + d < depth)
            def _(d=d):
                def step(x):
                    for a in range(count):
                        arrived(a, p.z + d, p.y, x)
                        spread(a, block(a, p.z + d, p.y, x), p.z + d, x, (0,))

                over_x(step)

        if d == 1:
            from_y(p.z)
        else:

            @pl.when(p.z >= d - 1)
            def _(d=d):
                from_y(p.z - d + 1)

            @pl.when(p.z + d - 1 < depth)
            def _(d=d):
                from_y(p.z + d - 1)

    for a in range(count):
        pltpu.make_async_copy(ins[a], block(a, p.z, p.y, p.x), near.at[a]).wait()

        def many(number, send, recv):
            part = outs[a].at[pl.ds(0, number)]
            return remote(part, part, send.at[a], recv.at[a], sibling)

        if across > 1:
            many(across - 1, xs, rc).wait_send()
        if tall > 1:

            @pl.when(p.c == 1)
            def _():
                many((tall - 1) * depth * across, ys, rc).wait_send()

            @pl.when(p.c == 0)
            def _(a=a):
                many((tall - 1) * (depth - 1) * across, ys, rc).wait_send()
                for x in range(across):
                    for k in range(1, tall):
                        to_partner(a, 0, p.y, x, k).wait_send()

        many(p.units, cs, rc).wait()
        for z in range(depth):
            for way in (0, 1):

                @pl.when(
                    ((p.z >= z) & (p.z < depth - 1)) if way else ((p.z <= z) & (p.z > 0))
                )
                def _(z=z, way=way, a=a):
                    for x in range(across):
                        to_z(a, block(a, z, p.y, x), z, x, way).wait_send()

    swaps.wait()


def split_swaps(swapped):
    return [w for w, _ in swapped], [shift for _, shift in swapped]


def gather(shards, wide, collective_id, swapped=()):
    group, peers = lax.axis_size("expert"), lax.axis_size("fsdp")
    place = Place(group, peers, wide)
    given, shifts = split_swaps([w[:2] for w in swapped])
    spans = [w[2] if len(w) > 2 else None for w in swapped]
    into = {i: w[3] for i, w in enumerate(swapped) if len(w) > 3}
    count, extra = len(shards), len(given)
    aliases = {count + extra + j: count + i for j, i in enumerate(into)}
    dma = pltpu.SemaphoreType.DMA
    return pl.pallas_call(
        functools.partial(gather_kernel, place, count, shifts, spans, len(into)),
        out_shape=[jax.ShapeDtypeStruct((place.slots,) + s.shape, s.dtype) for s in shards]
        + [jax.ShapeDtypeStruct(s.shape, s.dtype) for s in given],
        in_specs=[pl.BlockSpec(memory_space=pl.ANY)] * (count + extra + len(into)),
        out_specs=[pl.BlockSpec(memory_space=pl.ANY)] * (count + extra),
        input_output_aliases=aliases,
        scratch_shapes=[dma((count,))] * 5
        + [
            dma((count, 2, place.depth * place.across)),
            dma((count, place.units)),
            dma((max(extra, 1),)),
            dma((max(extra, 1),)),
            dma((count, place.across * max(place.tall - 1, 1))),
        ],
        compiler_params=pltpu.CompilerParams(
            collective_id=collective_id, has_side_effects=True, vmem_limit_bytes=58 << 20
        ),
        name=f"gather{collective_id}",
    )(*shards, *given, *into.values())


def chunk_of(left):
    return 256 if left.shape[1] % 256 == 0 else 128


class Pairs:
    def __init__(self, products):
        self.arrays = []
        self.uses = []
        for pair in products:
            use = []
            for array in pair:
                known = [i for i, other in enumerate(self.arrays) if other is array]
                if not known:
                    self.arrays.append(array)
                    known = [len(self.arrays) - 1]
                use.append(known[0])
            self.uses.append(tuple(use))

    def shapes(self):
        arrays = self.arrays
        return [
            jax.ShapeDtypeStruct((arrays[i].shape[1], arrays[j].shape[1]), jnp.bfloat16)
            for i, j in self.uses
        ]

    def room(self):
        if not self.uses:
            return []
        arrays = self.arrays
        held = [pltpu.VMEM(v.shape, v.dtype) for v in arrays]
        ready = [
            pltpu.VMEM((2, chunk_of(arrays[i]), arrays[j].shape[1]), jnp.bfloat16)
            for i, j in self.uses
        ]
        dma = pltpu.SemaphoreType.DMA
        return held + ready + [dma((len(arrays),)), dma((len(self.uses), 2))]


class Products:
    def __init__(self, uses, operands, results, refs):
        self.uses = uses
        if uses:
            held = refs[: len(operands)]
            self.loads = list(zip(operands, held))
            self.in_sems, self.out_sems = refs[len(operands) + len(uses) :]
            ready = refs[len(operands) : len(operands) + len(uses)]
            self.parts = [(r, held[i], held[j], v) for (i, j), r, v in zip(uses, results, ready)]

    def load(self, k):
        source, held = self.loads[k]
        return pltpu.make_async_copy(source, held, self.in_sems.at[k])

    def start(self):
        for k in range(len(self.loads) if self.uses else 0):
            self.load(k).start()

    def run(self, i):
        earlier = [k for use in self.uses[:i] for k in use]
        for k in sorted(set(self.uses[i]) - set(earlier)):
            self.load(k).wait()
        result, left, right, ready = self.parts[i]
        chunk = chunk_of(left)
        steps = left.shape[1] // chunk

        def leave(j):
            return pltpu.make_async_copy(
                ready.at[j % 2],
                result.at[pl.ds(pl.multiple_of(j * chunk, chunk), chunk)],
                self.out_sems.at[i, j % 2],
            )

        def go(j, _):
            @pl.when(j >= 2)
            def _():
                leave(j - 2).wait()

            part = pl.ds(pl.multiple_of(j * chunk, chunk), chunk)
            ready[j % 2] = dot_turned(left[:, part], right[...]).astype(ready.dtype)
            leave(j).start()
            return 0

        lax.fori_loop(0, steps, go, 0)
        for j in range(max(steps - 2, 0), steps):
            leave(j).wait()


def exchange_kernel(place, shifts, uses, operands, *refs):
    extra, pairs = len(shifts), len(uses)
    given, refs = refs[:extra], refs[extra:]
    loads, refs = refs[:operands], refs[operands:]
    left, right, refs = refs[0], refs[1], refs[2:]
    taken, results, refs = refs[:extra], refs[extra : extra + pairs], refs[extra + pairs :]
    across, held, held_sem, refs = refs[0], refs[1], refs[2], refs[3:]
    p = place.here()
    p.greet_peers()
    swaps = Swaps(p, shifts, given, taken, *refs[:2])
    swaps.start()
    products = Products(uses, loads, results, refs[2:])
    products.start()
    arrive = pltpu.make_async_copy(right, held, held_sem)
    arrive.start()
    for i in range(pairs):
        products.run(i)
    arrive.wait()
    chunk = 256

    def go(j, _):
        part = pl.ds(pl.multiple_of(j * chunk, chunk), chunk)
        across[:, part] = dot_across(left[...], held[part, :])
        return 0

    lax.fori_loop(0, held.shape[0] // chunk, go, 0)
    swaps.wait()


def exchange(collective_id, swapped, products, left, right):
    place = Place(lax.axis_size("expert"), lax.axis_size("fsdp"), False)
    given, shifts = split_swaps(swapped)
    pairs = Pairs(products)
    extra, operands = len(given), len(pairs.arrays)
    anywhere, inside = pl.BlockSpec(memory_space=pl.ANY), pl.BlockSpec(memory_space=pltpu.VMEM)
    dma = pltpu.SemaphoreType.DMA
    return pl.pallas_call(
        functools.partial(exchange_kernel, place, shifts, pairs.uses, operands),
        out_shape=[jax.ShapeDtypeStruct(s.shape, s.dtype) for s in given]
        + pairs.shapes()
        + [jax.ShapeDtypeStruct((left.shape[0], right.shape[0]), jnp.float32)],
        in_specs=[anywhere] * (extra + operands) + [inside, anywhere],
        out_specs=[anywhere] * (extra + len(products)) + [inside],
        scratch_shapes=[pltpu.VMEM(right.shape, right.dtype), dma, dma((extra,)), dma((extra,))]
        + pairs.room(),
        compiler_params=pltpu.CompilerParams(
            collective_id=collective_id, has_side_effects=True, vmem_limit_bytes=56 << 20
        ),
        name=f"exchange{collective_id}",
    )(*given, *pairs.arrays, left, right)


def outer_kernel(count, *refs):
    for i in range(count):
        left, right, result = refs[i], refs[count + i], refs[2 * count + i]
        chunk = chunk_of(left)

        def go(j, _):
            part = pl.ds(pl.multiple_of(j * chunk, chunk), chunk)
            result[part, :] = dot_turned(left[:, part], right[...]).astype(result.dtype)
            return 0

        lax.fori_loop(0, left.shape[1] // chunk, go, 0)


def outer_products(products):
    return pl.pallas_call(
        functools.partial(outer_kernel, len(products)),
        out_shape=Pairs(products).shapes(),
        in_specs=[pl.BlockSpec(memory_space=pltpu.VMEM)] * (2 * len(products)),
        out_specs=[pl.BlockSpec(memory_space=pltpu.VMEM)] * len(products),
        compiler_params=pltpu.CompilerParams(vmem_limit_bytes=32 << 20),
        name="outer",
    )(*[v for v, _ in products], *[w for _, w in products])


def scatter_kernel(place, count, shifts, uses, operands, *refs):
    total, pairs = count + len(shifts), len(uses)
    ins, given = refs[:count], refs[count:total]
    loads, refs = refs[total : total + operands], refs[total + operands :]
    outs, taken, results = refs[:count], refs[count:total], refs[total : total + pairs]
    refs = refs[total + pairs :]
    held, side, rows_y, rows_z, rows_x, rows_e = (
        refs[i * count : (i + 1) * count] for i in range(6)
    )
    la, rc, yr, zr, zs, cs, ys, xs, xr, given_sem, taken_sem, es, er, *room = refs[6 * count :]
    p = place.here()
    depth, tall, across = p.depth, p.tall, p.across
    p.greet(len(shifts) > 0)
    sibling = p.device(p.z, p.y, 1 - p.c)
    half = max(depth // 2, 1)

    def in_order(step):
        lower = 1 - p.z // half

        def right(total, done):
            def go(j, _):
                step(depth - 1 - j // across, (p.x + 1 + j % across) % across, 1, done * across + j)
                return 0

            lax.fori_loop(0, total * across, go, 0)

        def left(total, done):
            def go(j, _):
                step(j // across, (p.x + 1 + j % across) % across, 0, done * across + j)
                return 0

            lax.fori_loop(0, total * across, go, 0)

        early = (depth - 1 - p.z) * lower
        right(early, 0)
        left(p.z, early)
        right((depth - 1 - p.z) * (1 - lower), early + p.z)

        def own(j, _):
            step(p.z, (p.x + 1 + j) % across, None, (depth - 1) * across + j)
            return 0

        lax.fori_loop(0, across, own, 0)

    def local(a, k, z, y, x):
        return pltpu.make_async_copy(ins[a].at[p.slot(z, y, p.c, x)], held[a].at[k, y], la.at[a, k])

    def begin(z, x, way, number):
        k = z * across + x
        for a in range(count):
            for y in range(tall):
                remote(
                    ins[a].at[p.slot(z, y, 1 - p.c, x)],
                    side[a].at[k, y],
                    cs.at[a],
                    rc.at[a, k],
                    sibling,
                ).start()
                local(a, k, z, y, x).start()

    def add(a, target, sources):
        rows = ins[a].shape[1]
        chunk = 16 if rows % 16 == 0 else rows

        def go(i, _):
            part = pl.ds(i * chunk, chunk)
            total = target[part].astype(jnp.float32)
            for source in sources:
                total = total + source[part].astype(jnp.float32)
            target[part] = total.astype(target.dtype)
            return 0

        lax.fori_loop(0, rows // chunk, go, 0)

    def first(z, x, way, number):
        k = z * across + x
        for a in range(count):
            pltpu.make_async_copy(held[a].at[k], held[a].at[k], la.at[a, k]).wait()
            remote(side[a].at[k], side[a].at[k], cs.at[a], rc.at[a, k], sibling).wait_recv()
            for j in range(1, tall):
                y = (p.y + j) % tall
                mine = held[a].at[k, y]

                def along_y(sources, mine=mine, j=j, y=y, a=a):
                    add(a, mine, sources)
                    remote(
                        mine,
                        rows_y[a].at[k, tall - j - 1],
                        ys.at[a],
                        yr.at[a, k],
                        p.device(p.z, y, p.c),
                    ).start()

                @pl.when((p.c == 0) & (z == p.detour(p.z)))
                def _(mine=mine, j=j, y=y, a=a):
                    add(a, mine, [side[a].at[k, y]])
                    remote(
                        mine,
                        rows_e[a].at[x, j - 1],
                        es.at[a],
                        er.at[a, x * (tall - 1) + j - 1],
                        p.device(p.partner(), p.y, p.c),
                    ).start()

                @pl.when((p.c == 0) & (z == p.detour(p.partner())))
                def _(j=j, y=y, a=a, along_y=along_y):
                    part = rows_e[a].at[x, j - 1]
                    remote(
                        part, part, cs.at[a], er.at[a, x * (tall - 1) + j - 1], sibling
                    ).wait_recv()
                    along_y([side[a].at[k, y], part])

                @pl.when((p.c == 1) | ((z != p.detour(p.z)) & (z != p.detour(p.partner()))))
                def _(y=y, a=a, along_y=along_y):
                    along_y([side[a].at[k, y]])

            add(a, held[a].at[k, p.y], [side[a].at[k, p.y]])

    products = Products(uses, loads, results, room)
    items = depth * across

    def second(z, x, way, number):
        k = z * across + x
        for i in range(pairs):
            turn = i * items // pairs
            if (way is None) == (turn >= (depth - 1) * across):
                pl.when(number == turn)(functools.partial(products.run, i))
        for a in range(count):
            mine = held[a].at[k, p.y]
            if tall > 1:

                @pl.when((p.c == 1) | (z != p.detour(p.z)))
                def _(a=a, mine=mine):
                    part = rows_y[a].at[k]
                    remote(part, part, cs.at[a], yr.at[a, k], sibling).wait_recv()
                    add(a, mine, [rows_y[a].at[k, j] for j in range(tall - 1)])

            def from_z(index):
                part = rows_z[a].at[index]
                remote(part, part, cs.at[a], zr.at[a, index], sibling).wait_recv()
                add(a, mine, [part])

            def send(index, target):
                remote(mine, rows_z[a].at[index], zs.at[a, k], zr.at[a, index], target).start()

            if way is None or way == 1:
                pl.when(p.z > 0)(functools.partial(from_z, k))
            if way is None:
                pl.when(p.z < depth - 1)(functools.partial(from_z, depth * across + x))
            if way == 0:
                pl.when(p.z < depth - 1)(functools.partial(from_z, k))
            if way == 1:
                send(k, p.device(p.z + 1, p.y, p.c))
            if way == 0:
                left = p.device(p.z - 1, p.y, p.c)

                @pl.when(z == p.z - 1)
                def _():
                    send(depth * across + x, left)

                @pl.when(z < p.z - 1)
                def _():
                    send(k, left)

            if way is None and across > 1:

                @pl.when(x != p.x)
                def _():
                    remote(
                        mine,
                        rows_x[a].at[(p.x - x + across) % across - 1],
                        xs.at[a],
                        xr.at[a],
                        p.device(p.z, p.y, p.c, x),
                    ).start()

    ahead = min(across + 1 if across > 1 else 2, items)
    lower = 1 - p.z // half
    switch = lower * (depth - 1 - p.z) + (1 - lower) * p.z

    def first_at(number):
        j = number // across
        own = j // (depth - 1)
        past = (j - switch + depth) // depth
        down, up = depth - 1 - j, j
        down_late, up_late = depth - 1 - (j - switch), j - switch
        z = lower * ((1 - past) * down + past * up_late)
        z = z + (1 - lower) * ((1 - past) * up + past * down_late)
        z = own * p.z + (1 - own) * z
        first(z, (p.x + 1 + number % across) % across, None, number)

    def both(z, x, way, number):
        if way is not None:

            @pl.when(number + ahead < items)
            def _():
                first_at(number + ahead)

        second(z, x, way, number)

    swaps = Swaps(p, shifts, given, taken, given_sem, taken_sem)
    swaps.start()
    in_order(begin)
    products.start()
    lax.fori_loop(0, ahead, lambda n, _: (first_at(n), 0)[1], 0)
    in_order(both)
    k = p.z * across + p.x
    for a in range(count):
        mine = held[a].at[k, p.y]
        sources = []
        if across > 1:
            remote(rows_x[a], rows_x[a], xs.at[a], xr.at[a], sibling).wait()
            sources = [rows_x[a].at[j] for j in range(across - 1)]
        rows = ins[a].shape[1]
        chunk = 16 if rows % 16 == 0 else rows

        def go(i, _):
            part = pl.ds(i * chunk, chunk)
            total = mine[part].astype(jnp.float32)
            for source in sources:
                total = total + source[part].astype(jnp.float32)
            outs[a][part] = total
            return 0

        lax.fori_loop(0, rows // chunk, go, 0)
        remote(side[a], side[a], cs.at[a], rc.at[a, 0], sibling).wait_send()
        if tall > 1:

            @pl.when(p.c == 1)
            def _(a=a):
                remote(rows_y[a], rows_y[a], ys.at[a], rc.at[a, 0], sibling).wait_send()

            @pl.when(p.c == 0)
            def _(a=a):
                part = rows_y[a].at[pl.ds(0, (depth - 1) * across)]
                remote(part, part, ys.at[a], rc.at[a, 0], sibling).wait_send()
                remote(rows_e[a], rows_e[a], es.at[a], rc.at[a, 0], sibling).wait_send()

        def wait_z(k, _):
            @pl.when(k // across != p.z)
            def _():
                remote(mine, rows_z[a].at[0], zs.at[a, k], rc.at[a, 0], sibling).wait_send()

            return 0

        lax.fori_loop(0, depth * across, wait_z, 0)

    swaps.wait()


def scatter(partials, wide, collective_id, swapped=(), products=()):
    group, peers = lax.axis_size("expert"), lax.axis_size("fsdp")
    place = Place(group, peers, wide)
    given, shifts = split_swaps(swapped)
    pairs = Pairs(products)
    count, extra, operands = len(partials), len(given), len(pairs.arrays)
    dma = pltpu.SemaphoreType.DMA
    items = place.depth * place.across

    def room(*lead):
        return [pltpu.VMEM(lead + s.shape[1:], s.dtype) for s in partials]

    return pl.pallas_call(
        functools.partial(scatter_kernel, place, count, shifts, pairs.uses, operands),
        out_shape=[jax.ShapeDtypeStruct(s.shape[1:], jnp.float32) for s in partials]
        + [jax.ShapeDtypeStruct(s.shape, s.dtype) for s in given]
        + pairs.shapes(),
        in_specs=[pl.BlockSpec(memory_space=pl.ANY)] * (count + extra + operands),
        out_specs=[pl.BlockSpec(memory_space=pltpu.VMEM)] * count
        + [pl.BlockSpec(memory_space=pl.ANY)] * extra
        + [pl.BlockSpec(memory_space=pl.ANY)] * len(products),
        scratch_shapes=room(items, place.tall)
        + room(items, place.tall)
        + room(items, max(place.tall - 1, 1))
        + room(items + place.across)
        + room(max(place.across - 1, 1))
        + room(place.across, max(place.tall - 1, 1))
        + [
            dma((count, items)),
            dma((count, items)),
            dma((count, items)),
            dma((count, items + place.across)),
            dma((count, items)),
            dma((count,)),
            dma((count,)),
            dma((count,)),
            dma((count,)),
            dma((max(extra, 1),)),
            dma((max(extra, 1),)),
            dma((count,)),
            dma((count, place.across * max(place.tall - 1, 1))),
        ]
        + pairs.room(),
        compiler_params=pltpu.CompilerParams(
            collective_id=collective_id, has_side_effects=True, vmem_limit_bytes=60 << 20
        ),
        name=f"scatter{collective_id}",
    )(*partials, *given, *pairs.arrays)


def dot_plain(left, right):
    return jnp.dot(left, right, preferred_element_type=jnp.float32)


def dot_across(left, right):
    return lax.dot_general(left, right, (((1,), (1,)), ((), ())), preferred_element_type=jnp.float32)


def dot_turned(left, right):
    return lax.dot_general(left, right, (((0,), (0,)), ((), ())), preferred_element_type=jnp.float32)


def ffn_kernel(peers, sources, numbers, fill, *refs):
    hid, cot, ranks = refs[:3]
    gates, ups, downs = (refs[3 + i * peers : 3 + (i + 1) * peers] for i in range(3))
    router, shared_in, shared_out = refs[3 + 3 * peers : 6 + 3 * peers]
    refs = refs[6 + 3 * peers :]
    rows, d_out = refs[:peers], refs[peers : 2 * peers]
    out_part, back_part, act, d_g, d_u, d_log, s_act, s_grad = refs[2 * peers : 8 + 2 * peers]
    rows_here, cots_here = refs[8 + 2 * peers :]
    f32, bf16 = jnp.float32, jnp.bfloat16
    step = pl.program_id(0)
    tok_rows = hid.shape[1]
    capacity = rows_here.shape[0] // sources
    width = hid.shape[2] // peers
    eid, start, fid = numbers[0], numbers[1], numbers[2]
    scale = fill[0]

    def length(s):
        return numbers[3 + step * sources + s]

    def columns(r):
        return pl.ds(pl.multiple_of((fid + r) % peers * width, width), width)

    scales = []
    picks = []
    for s in range(sources):
        part = pl.ds(s * capacity, capacity)
        slot = lax.broadcasted_iota(jnp.int32, (capacity, tok_rows), 0).astype(f32)
        pick = jnp.where(ranks[s] == slot, 1.0, 0.0)
        lane = start + lax.broadcasted_iota(jnp.int32, (1, tok_rows), 1)
        alive = jnp.where(lane < length(s), scale, 0.0)
        scales.append(jnp.sum(pick * alive, axis=1, keepdims=True))
        pick = pick.astype(bf16)
        picks.append(pick)
        rows_here[part, :] = dot_plain(pick, hid[s]).astype(bf16)
        cots_here[part, :] = dot_plain(pick, cot[s]).astype(bf16)
    row_scale = jnp.concatenate(scales, axis=0)
    logits = dot_plain(rows_here[...], router[...])
    top = jnp.max(logits, axis=1, keepdims=True)
    powers = jnp.exp(logits - top)
    probs = powers / jnp.sum(powers, axis=1, keepdims=True)
    own = (lax.broadcasted_iota(jnp.int32, (1, probs.shape[1]), 1) == eid).astype(f32)
    gate = jnp.sum(probs * own, axis=1, keepdims=True)

    for r in range(peers):
        rows[r][...] = rows_here[:, columns(r)]

    def summed(terms):
        total = terms[0]
        for term in terms[1:]:
            total = total + term
        return total

    g = summed([dot_plain(rows[r][...], gates[r][...]) for r in range(peers)])
    u = summed([dot_plain(rows[r][...], ups[r][...]) for r in range(peers)])
    sigma = 1.0 / (1.0 + jnp.exp(-g))
    act_now = (g * sigma * u).astype(bf16)
    act[...] = act_now
    d_gate = jnp.zeros_like(gate)
    weighted = []
    for r in range(peers):
        out = dot_plain(act_now, downs[r][...]).astype(bf16).astype(f32)
        row_cot = cots_here[:, columns(r)].astype(f32)
        d_out[r][...] = ((gate * row_scale) * row_cot).astype(bf16)
        d_gate = d_gate + jnp.sum(row_cot * out, axis=1, keepdims=True)
        weighted.append((gate * out).astype(bf16))
    d_gate = d_gate * row_scale
    d_act = summed([dot_across(d_out[r][...], downs[r][...]) for r in range(peers)])
    dg_now = (d_act * u * (sigma * (1.0 + g * (1.0 - sigma)))).astype(bf16)
    du_now = (d_act * (g * sigma)).astype(bf16)
    d_g[...] = dg_now
    d_u[...] = du_now
    dl_now = (gate * d_gate * (own - probs)).astype(bf16)
    d_log[...] = dl_now
    d_rows = []
    for r in range(peers):
        total = dot_across(dg_now, gates[r][...]) + dot_across(du_now, ups[r][...])
        total = total + dot_across(dl_now, router[columns(r), :])
        d_rows.append(total.astype(bf16))
    units = shared_out.shape[0]
    total_rows = sources * tok_rows
    hid_all = hid[...].reshape(total_rows, hid.shape[2])
    cot_all = cot[...].reshape(total_rows, hid.shape[2])
    both = dot_plain(hid_all, shared_in[...])
    sg, su = both[:, :units], both[:, units:]
    s_sigma = 1.0 / (1.0 + jnp.exp(-sg))
    s_now = sg * s_sigma * su
    column = lax.broadcasted_iota(jnp.int32, (tok_rows, 1), 0) + start
    alive = jnp.concatenate(
        [jnp.where(column < length(s), scale, 0.0) for s in range(sources)], axis=0
    )
    d_s = dot_across(cot_all, shared_out[...]) * alive
    s_act[...] = (s_now * alive).astype(bf16)
    s_low = s_now.astype(bf16)
    d_sg = (d_s * su * (s_sigma * (1.0 + sg * (1.0 - s_sigma)))).astype(bf16)
    d_su = (d_s * (sg * s_sigma)).astype(bf16)
    s_grad[:, pl.ds(0, units)] = d_sg
    s_grad[:, pl.ds(units, units)] = d_su
    for r in range(peers):
        for n in range(0, width, 256):
            at = pl.ds(pl.multiple_of((fid + r) % peers * width + n, 256), 256)
            s_out = dot_plain(s_low, shared_out[:, at])
            s_back = dot_across(s_grad[...], shared_in[at, :])
            for s in range(sources):
                part = slice(s * capacity, (s + 1) * capacity)
                span = slice(s * tok_rows, (s + 1) * tok_rows)
                out_part[s, :, at] = (
                    dot_turned(picks[s], weighted[r][part, n : n + 256]) + s_out[span]
                ).astype(bf16)
                back_part[s, :, at] = (
                    dot_turned(picks[s], d_rows[r][part, n : n + 256]) + s_back[span]
                ).astype(bf16)


def ffn(capacity, numbers, fill, hid, cot, ranks, gates, ups, downs, router, shared_in, shared_out):
    group, tok_rows, dim = hid.shape
    peers = len(gates)
    sources = max(1, min(4, 256 // capacity))
    hidden = gates[0].shape[1]
    units = shared_out.shape[0]
    rows = sources * capacity
    bf16 = jnp.bfloat16

    def whole(array):
        return pl.BlockSpec(
            array.shape, lambda i, *_: (0,) * array.ndim, pipeline_mode=pl.Buffered(1)
        )

    def tile(*shape):
        return pl.BlockSpec(shape, lambda i, *_: (i,) + (0,) * (len(shape) - 1))

    pairs = group * capacity
    weights = [*gates, *ups, *downs, router, shared_in, shared_out]
    return pl.pallas_call(
        functools.partial(ffn_kernel, peers, sources),
        out_shape=[jax.ShapeDtypeStruct((pairs, dim // peers), bf16)] * (2 * peers)
        + [
            jax.ShapeDtypeStruct((group, tok_rows, dim), bf16),
            jax.ShapeDtypeStruct((group, tok_rows, dim), bf16),
            jax.ShapeDtypeStruct((pairs, hidden), bf16),
            jax.ShapeDtypeStruct((pairs, hidden), bf16),
            jax.ShapeDtypeStruct((pairs, hidden), bf16),
            jax.ShapeDtypeStruct((pairs, router.shape[1]), bf16),
            jax.ShapeDtypeStruct((group * tok_rows, units), bf16),
            jax.ShapeDtypeStruct((group * tok_rows, 2 * units), bf16),
        ],
        grid_spec=pltpu.PrefetchScalarGridSpec(
            num_scalar_prefetch=2,
            grid=(group // sources,),
            in_specs=[
                tile(sources, tok_rows, dim),
                tile(sources, tok_rows, dim),
                tile(sources, 1, tok_rows),
            ]
            + [whole(w) for w in weights],
            out_specs=[tile(rows, dim // peers)] * (2 * peers)
            + [
                tile(sources, tok_rows, dim),
                tile(sources, tok_rows, dim),
                tile(rows, hidden),
                tile(rows, hidden),
                tile(rows, hidden),
                tile(rows, router.shape[1]),
                tile(sources * tok_rows, units),
                tile(sources * tok_rows, 2 * units),
            ],
            scratch_shapes=[pltpu.VMEM((rows, dim), bf16)] * 2,
        ),
        compiler_params=pltpu.CompilerParams(vmem_limit_bytes=62 << 20),
        cost_estimate=pl.CostEstimate(
            flops=18 * pairs * dim * hidden, bytes_accessed=60 << 20, transcendentals=1 << 22
        ),
        name="ffn",
    )(numbers, fill, hid, cot, ranks, *weights)


def both_keys(keyval, rot):
    f32 = jnp.float32
    rot = rot.astype(f32)
    first = jnp.concatenate([keyval[:, :DN].astype(f32), rot], axis=1)
    second = jnp.concatenate([keyval[:, DN + DV : 2 * DN + DV].astype(f32), rot], axis=1)
    second = pltpu.roll(second, DN + DR, 1)
    return first.astype(jnp.bfloat16), second.astype(jnp.bfloat16)


def turn(array, plain, ahead, behind):
    width = array.shape[1]
    return (
        array * plain
        + pltpu.roll(array, width - DR // 2, 1) * ahead
        + pltpu.roll(array, DR // 2, 1) * behind
    )


def attend_kernel(numbers, hidden, w_query, latent, w_expand, rot, plain, ahead, behind, *outs):
    query, keyval, probs, context = outs
    bf16 = jnp.bfloat16
    turned = turn(dot_plain(hidden[...], w_query[...]), plain[...], ahead[...], behind[...])
    query_now = turned.astype(bf16)
    query[...] = query_now
    keyval[...] = dot_plain(latent[...], w_expand[...]).astype(bf16)
    rows, keys = query.shape[0], keyval.shape[0]
    row = lax.broadcasted_iota(jnp.int32, (rows, keys), 0) + numbers[0]
    key = lax.broadcasted_iota(jnp.int32, (rows, keys), 1)
    allowed = (key <= row) & (key < numbers[1])
    for i, keys_now in enumerate(both_keys(keyval[...], rot[...])):
        scores = dot_across(query_now, keys_now) * (DN + DR) ** (-0.5)
        scores = jnp.where(allowed, scores, masked_value)
        powers = jnp.exp(scores - jnp.max(scores, axis=1, keepdims=True))
        share = powers / jnp.sum(powers, axis=1, keepdims=True)
        probs[i] = share
        value = keyval[:, pl.ds(i * (DN + DV) + DN, DV)]
        context[:, pl.ds(i * DV, DV)] = dot_plain(share.astype(bf16), value).astype(bf16)


def attend(numbers, hidden, w_query, latent, w_expand, rot, turns):
    rows, dim = hidden.shape
    keys, rank = latent.shape
    bf16 = jnp.bfloat16

    def still(array):
        return pl.BlockSpec(array.shape, lambda i, *_: (0,) * array.ndim)

    def columns(height, width):
        return pl.BlockSpec((height, width), lambda i, *_: (0, i))

    return pl.pallas_call(
        attend_kernel,
        out_shape=[
            jax.ShapeDtypeStruct((rows, H * (DN + DR)), bf16),
            jax.ShapeDtypeStruct((keys, H * (DN + DV)), bf16),
            jax.ShapeDtypeStruct((H, rows, keys), jnp.float32),
            jax.ShapeDtypeStruct((rows, H * DV), bf16),
        ],
        grid_spec=pltpu.PrefetchScalarGridSpec(
            num_scalar_prefetch=1,
            grid=(H // 2,),
            in_specs=[
                still(hidden),
                columns(dim, 2 * (DN + DR)),
                still(latent),
                columns(rank, 2 * (DN + DV)),
                still(rot),
                *[still(t) for t in turns],
            ],
            out_specs=[
                columns(rows, 2 * (DN + DR)),
                columns(keys, 2 * (DN + DV)),
                pl.BlockSpec((2, rows, keys), lambda i, *_: (i, 0, 0)),
                columns(rows, 2 * DV),
            ],
        ),
        compiler_params=pltpu.CompilerParams(vmem_limit_bytes=40 << 20),
        name="attend",
    )(numbers, hidden, w_query, latent, w_expand, rot, *turns)


def attend_back_kernel(d_res, w_output, query, keyval, probs, rot, plain, ahead, behind, *outs):
    d_query, d_keyval, d_rot = outs
    f32, bf16 = jnp.float32, jnp.bfloat16
    scale = (DN + DR) ** (-0.5)
    query_now = query[...]
    total = jnp.zeros(query.shape, f32)
    rot_total = jnp.zeros(d_rot.shape, f32)
    for i, keys_now in enumerate(both_keys(keyval[...], rot[...])):
        d_context = dot_across(d_res[...], w_output[pl.ds(i * DV, DV), :]).astype(bf16)
        share = probs[i]
        at = i * (DN + DV)
        d_value = dot_turned(share.astype(bf16), d_context)
        d_share = dot_across(d_context, keyval[:, pl.ds(at + DN, DV)])
        d_score = share * (d_share - jnp.sum(share * d_share, axis=1, keepdims=True))
        d_score = d_score.astype(bf16)
        total = total + dot_plain(d_score, keys_now) * scale
        d_key = dot_turned(d_score, query_now) * scale
        if i == 1:
            d_key = pltpu.roll(d_key, DN + DR, 1)
        d_keyval[:, pl.ds(at, DN)] = d_key[:, :DN].astype(bf16)
        d_keyval[:, pl.ds(at + DN, DV)] = d_value.astype(bf16)
        rot_total = rot_total + d_key[:, DN : 2 * DN]
    d_query[...] = turn(total, plain[...], -ahead[...], -behind[...]).astype(bf16)

    @pl.when(pl.program_id(0) == 0)
    def _():
        d_rot[...] = rot_total

    @pl.when(pl.program_id(0) != 0)
    def _():
        d_rot[...] += rot_total


def attend_back(d_res, w_output, query, keyval, probs, rot, turns):
    rows, dim = d_res.shape
    keys = keyval.shape[0]
    bf16 = jnp.bfloat16

    def still(array):
        return pl.BlockSpec(array.shape, lambda i: (0,) * array.ndim)

    def columns(height, width):
        return pl.BlockSpec((height, width), lambda i: (0, i))

    return pl.pallas_call(
        attend_back_kernel,
        out_shape=[
            jax.ShapeDtypeStruct(query.shape, bf16),
            jax.ShapeDtypeStruct(keyval.shape, bf16),
            jax.ShapeDtypeStruct((keys, DN), jnp.float32),
        ],
        grid=(H // 2,),
        in_specs=[
            still(d_res),
            pl.BlockSpec((2 * DV, dim), lambda i: (i, 0)),
            columns(rows, 2 * (DN + DR)),
            columns(keys, 2 * (DN + DV)),
            pl.BlockSpec((2, rows, keys), lambda i: (i, 0, 0)),
            still(rot),
            *[still(t) for t in turns],
        ],
        out_specs=[
            columns(rows, 2 * (DN + DR)),
            columns(keys, 2 * (DN + DV)),
            pl.BlockSpec((keys, DN), lambda i: (0, 0)),
        ],
        compiler_params=pltpu.CompilerParams(vmem_limit_bytes=40 << 20),
        name="attend_back",
    )(d_res, w_output, query, keyval, probs, rot, *turns)


def from_peers(block):
    size = lax.axis_size("fsdp")
    return [block] + [
        lax.ppermute(block, "fsdp", [(j, (j - r) % size) for j in range(size)])
        for r in range(1, size)
    ]


def sum_to_peers(term):
    size = lax.axis_size("fsdp")
    arrived = [
        lax.ppermute(term(r), "fsdp", [(j, (j + r) % size) for j in range(size)])
        for r in range(1, size)
    ]
    return arrived


def body(
    tokens,
    cotangent,
    routes,
    lengths,
    attn_gain,
    q_weight,
    kva_weight,
    kv_gain,
    kvb_weight,
    out_weight,
    ffn_gain,
    router_weight,
    shared_gate,
    shared_up,
    shared_down,
    expert_gate,
    expert_up,
    expert_down,
):
    bf16, f32 = jnp.bfloat16, jnp.float32
    tok_rows, dim = tokens.shape
    peers = lax.axis_size("fsdp")
    group = lax.axis_size("expert")
    fid, eid = lax.axis_index("fsdp"), lax.axis_index("expert")
    seq_len = tok_rows * peers
    slot_total = seq_len * group
    expert_count = router_weight.shape[1]
    capacity = max(4, 5 * tok_rows * TOPK // (4 * expert_count))
    capacity = -(-capacity // 16) * 16
    half = dim // peers
    plane_rows = group * tok_rows
    pairs = group * capacity

    positions = fid * tok_rows + jnp.arange(tok_rows, dtype=jnp.int32)
    seq_length = lengths[0]
    valid_mask = (positions < seq_length).astype(f32)
    expert_ids = jnp.arange(expert_count, dtype=jnp.int32)
    hot_sum = jnp.sum((routes[:, :, None] == expert_ids[None, None, :]).astype(f32), axis=1)
    local_counts = jnp.sum(hot_sum * valid_mask[:, None], axis=0)

    def lane_row(vector):
        return jnp.pad(vector.astype(f32), (0, tok_rows - vector.shape[0]))[None, :]

    small = jnp.concatenate(
        [routes.T.astype(f32)]
        + [lane_row(v) for v in (attn_gain, ffn_gain, kv_gain, local_counts, lengths)]
        + [jnp.zeros((16 - TOPK - 5, tok_rows), f32)],
        axis=0,
    )
    devices = group * peers
    turns = range(1, peers)
    w_query, w_compress, w_expand, w_output, w_router, small_all, *more = gather(
        [q_weight, kva_weight, kvb_weight, out_weight, router_weight, small],
        True,
        0,
        [(expert_gate[0], -r) for r in turns] + [(expert_up[0], -r, (0, half // 2)) for r in turns],
    )
    gate_parts = [expert_gate[0]] + more[: peers - 1]
    up_begun = more[peers - 1 :]
    w_query, w_compress, w_expand, w_output, w_router = (
        w.reshape(-1, w.shape[-1]) for w in (w_query, w_compress, w_expand, w_output, w_router)
    )
    gain_attn = small_all[:, TOPK, : attn_gain.shape[0]].reshape(-1)
    gain_ffn = small_all[:, TOPK + 1, : ffn_gain.shape[0]].reshape(-1)
    gain_latent = small_all[:, TOPK + 2, : kv_gain.shape[0]].reshape(-1)
    route_counts = jnp.sum(small_all[:, TOPK + 3, :expert_count], axis=0)
    all_lengths = small_all.reshape(group, peers, 16, tok_rows)[:, 0, TOPK + 4, 0]
    valid_total = jnp.sum(all_lengths)
    fill_scale = slot_total / valid_total
    plane_small = lax.dynamic_index_in_dim(
        small_all.reshape(group, peers, 16, tok_rows), fid, axis=1, keepdims=False
    )
    units = shared_gate.shape[1] // group
    lanes_more = -units % 128
    pieces = jnp.concatenate(
        [
            jnp.pad(w.reshape(-1, group, units), ((0, 0), (0, 0), (0, lanes_more)))
            for w in (shared_gate, shared_up)
        ],
        axis=2,
    ).transpose(1, 0, 2)
    pieces = lax.all_to_all(pieces, "expert", split_axis=0, concat_axis=0, tiled=True)
    sd_weight = jnp.roll(jnp.stack(from_peers(shared_down)), fid, axis=0).reshape(units, dim)
    sd_weight = jnp.pad(sd_weight, ((0, lanes_more), (0, 0)))
    cosine, sine_vals = rope_tables(positions)
    tokens_f = tokens.astype(f32)
    cot_ready, small_all = lax.optimization_barrier((cotangent, small_all))
    cot_plane = lax.all_gather(cot_ready, "expert", axis=0, tiled=True)
    normed_one, inverse_one = rms_norm(tokens_f, gain_attn)
    hidden_one = normed_one.astype(bf16)
    compressed = jnp.dot(hidden_one, w_compress, preferred_element_type=f32)
    latent_raw = compressed[:, :KVR]
    latent_norm, inverse_kv = rms_norm(latent_raw, gain_latent)
    latent = latent_norm.astype(bf16)
    key_rot = rotate(compressed[:, KVR:], cosine, sine_vals).astype(bf16)
    latent_rot = lax.all_gather(
        jnp.concatenate([latent, key_rot], axis=1), "fsdp", axis=0, tiled=True
    )
    down_own, latent_rot = lax.optimization_barrier((expert_down[0], latent_rot))
    down_parts = from_peers(down_own)
    all_rot = jnp.pad(latent_rot[:, KVR:], ((0, 0), (0, 2 * DN - DR)))

    def spread_columns(first, second, rest):
        one = jnp.concatenate([jnp.full((tok_rows, DN), rest, f32), first, second], axis=1)
        return jnp.concatenate([one, one], axis=1)

    zero = jnp.zeros_like(cosine)
    rotations = [
        spread_columns(cosine, cosine, 1.0),
        spread_columns(-sine_vals, zero, 0.0),
        spread_columns(zero, sine_vals, 0.0),
    ]
    query_all, keyval, probs_attn, context = attend(
        jnp.stack([fid * tok_rows, seq_length]).astype(jnp.int32),
        hidden_one,
        w_query,
        latent_rot[:, :KVR],
        w_expand,
        all_rot,
        rotations,
    )
    residual = tokens_f + jnp.dot(context, w_output, preferred_element_type=f32)
    normed_two, inverse_two = rms_norm(residual, gain_ffn)
    hidden_two = normed_two.astype(bf16)
    rest = (half // 2, half // 2)
    hid3, *more = gather(
        [hidden_two],
        False,
        1,
        [(pieces, -r) for r in turns]
        + [(expert_up[0], -r, rest, w) for r, w in zip(turns, up_begun)],
    )
    up_parts = [expert_up[0]] + more[peers - 1 :]
    gu_weight = jnp.roll(jnp.stack([pieces] + more[: peers - 1]), fid, axis=0)
    gu_weight = gu_weight.transpose(1, 0, 2, 3).reshape(dim, -1)
    hid_plane = hid3.reshape(plane_rows, dim)
    cot3 = cot_plane.reshape(group, tok_rows, dim)
    router_probs = jax.nn.softmax(jnp.dot(hidden_two, w_router, preferred_element_type=f32), axis=-1)
    local_shares = jnp.sum(router_probs * valid_mask[:, None], axis=0)
    frequency = expert_count / (TOPK * valid_total) * route_counts
    d_probs_own = balance_weight * valid_mask[:, None] * frequency[None, :] / valid_total
    dlog_own = (
        router_probs * (d_probs_own - jnp.sum(router_probs * d_probs_own, axis=-1, keepdims=True))
    ).astype(bf16)
    named = jnp.any(plane_small[:, :TOPK, :] == eid.astype(f32), axis=1)
    place = jnp.arange(tok_rows)
    before = (place[:, None] < place[None, :]).astype(bf16)
    ranks = jnp.dot(named.astype(bf16), before, preferred_element_type=f32)
    ranks = jnp.where(named, ranks, -1.0)[:, None, :]
    numbers = jnp.concatenate(
        [jnp.stack([eid, fid * tok_rows, fid]).astype(jnp.int32), all_lengths.astype(jnp.int32)]
    )
    made = ffn(
        capacity,
        numbers,
        fill_scale.reshape(1),
        hid3,
        cot3,
        ranks,
        gate_parts,
        up_parts,
        down_parts,
        w_router,
        gu_weight,
        sd_weight,
    )

    rows_in, d_out = made[:peers], made[peers : 2 * peers]
    out_part, back_part, act, d_hidden_g, d_hidden_u, dlog_rows, shared_scaled, d_gu = made[
        2 * peers :
    ]

    def outer(left, right):
        return lax.dot_general(left, right, (((0,), (0,)), ((), ())), preferred_element_type=f32)

    def back(left, weight):
        return lax.dot_general(left, weight, (((1,), (1,)), ((), ())), preferred_element_type=f32)

    def gate_term(r):
        return outer(rows_in[r], d_hidden_g)

    def up_term(r):
        return outer(rows_in[r], d_hidden_u)

    def down_term(r):
        return outer(act, d_out[r])

    def with_peers(term):
        arrived = sum_to_peers(lambda r: term(r).astype(bf16))
        total = term(0)
        for block in arrived:
            total = total + block.astype(f32)
        return total

    def plus(total, blocks):
        for block in blocks:
            total = total + block.astype(f32)
        return total

    d_hidden_two, *more = scatter(
        [back_part],
        False,
        2,
        [(gate_term(r).astype(bf16), r) for r in turns],
        [
            (hid_plane, d_gu),
            (shared_scaled, cot_plane),
            (rows_in[1], d_hidden_u),
            (act, d_out[1]),
            (rows_in[0], d_hidden_g),
            (rows_in[0], d_hidden_u),
            (act, d_out[0]),
        ]
        if peers == 2
        else [],
    )
    gate_blocks = more[: peers - 1]
    if peers == 2:
        d_gu_weight, d_sd, *others, gate_own, up_own, down_own = more[1:]
    else:
        d_gu_weight = outer(hid_plane, d_gu).astype(bf16)
        d_sd = outer(shared_scaled, cot_plane).astype(bf16)
        others = [up_term(r).astype(bf16) for r in turns]
        others = others + [down_term(r).astype(bf16) for r in turns]
        gate_own, up_own, down_own = gate_term(0), up_term(0), down_term(0)
    d_sd = d_sd[:units]
    out_part, d_hidden_two = lax.optimization_barrier((out_part, d_hidden_two))
    out_sum = lax.psum_scatter(
        out_part.reshape(plane_rows, dim), "expert", scatter_dimension=0, tiled=True
    )
    egate_grad = plus(gate_own.astype(f32), gate_blocks)[None]
    d_hidden_two = d_hidden_two + back(dlog_own, w_router)
    router_parts = jnp.stack([outer(rows_in[r], dlog_rows) for r in range(peers)])
    router_grad = jnp.roll(router_parts, fid, axis=0).reshape(dim, -1) + outer(hidden_two, dlog_own)
    d_gu_blocks = d_gu_weight.reshape(group, peers, dim // (group * peers), -1)
    d_sd_blocks = d_sd.reshape(peers, units // peers, dim)

    def gu_term(r):
        return lax.dynamic_index_in_dim(d_gu_blocks, (fid + r) % peers, axis=1, keepdims=False)

    def sd_term(r):
        return lax.dynamic_index_in_dim(d_sd_blocks, (fid + r) % peers, axis=0, keepdims=False)

    gu_sum = plus(gu_term(0).astype(f32), sum_to_peers(gu_term)).astype(bf16)
    sdown_grad = plus(sd_term(0).astype(f32), sum_to_peers(sd_term))
    grad_out = cotangent.astype(f32) * (valid_mask * fill_scale)[:, None]
    d_residual, d_ffn_gain = norm_back(d_hidden_two, residual, inverse_two, gain_ffn)
    d_residual = d_residual + grad_out
    d_residual_low = d_residual.astype(bf16)
    d_query, d_keyval_all, d_key_rot = attend_back(
        d_residual_low, w_output, query_all, keyval, probs_attn, all_rot, rotations
    )
    d_key_rot = d_key_rot[:, :DR]

    def own_rows(array, r):
        return lax.dynamic_slice_in_dim(array, (fid + r) % peers * tok_rows, tok_rows, axis=0)

    swapped = [(own_rows(d_keyval_all, r).astype(bf16), r) for r in turns]
    swapped = swapped + [(own_rows(d_key_rot, r).astype(bf16), r) for r in turns]
    *arrived, d_output_w, d_query_w, d_hidden_one = exchange(
        4,
        swapped,
        [(context, d_residual_low), (hidden_one, d_query)],
        d_query,
        w_query,
    )
    up_others, arrived[0] = lax.optimization_barrier((others[: peers - 1], arrived[0]))
    size = peers
    up_blocks = [
        lax.ppermute(w, "fsdp", [(j, (j + r) % size) for j in range(size)])
        for w, r in zip(up_others, turns)
    ]
    own_dkeyval = plus(own_rows(d_keyval_all, 0).astype(f32), arrived[: peers - 1])
    own_dkeyrot = plus(own_rows(d_key_rot, 0), arrived[peers - 1 :])
    gu_sum, own_dkeyval = lax.optimization_barrier((gu_sum, own_dkeyval))
    gu_sum = lax.all_to_all(gu_sum, "expert", split_axis=0, concat_axis=0, tiled=True)
    d_keyval = own_dkeyval.astype(bf16)
    d_latent = back(d_keyval, w_expand)
    d_latent_raw, d_latent_gain = norm_back(d_latent, latent_raw, inverse_kv, gain_latent)
    d_compressed = jnp.concatenate(
        [d_latent_raw, rotate_back(own_dkeyrot, cosine, sine_vals)], axis=-1
    ).astype(bf16)
    d_compress_w, d_expand_w = outer_products([(hidden_one, d_compressed), (latent, d_keyval)])
    d_hidden_one = d_hidden_one + back(d_compressed, w_compress)
    d_tokens, d_attn_gain = norm_back(d_hidden_one, tokens_f, inverse_one, gain_attn)
    tokens_grad = d_tokens + d_residual
    def lanes(vector):
        piece = vector.reshape(devices, -1)
        return jnp.pad(piece, ((0, 0), (0, tok_rows - piece.shape[1])))

    small_grads = jnp.stack(
        [
            lanes(d_attn_gain),
            lanes(d_latent_gain),
            lanes(d_ffn_gain),
            lanes(jnp.tile(local_shares, devices)),
        ]
        + [jnp.zeros((devices, tok_rows), f32)] * 4,
        axis=1,
    )
    dense = [
        w.astype(bf16).reshape(devices, -1, w.shape[-1])
        for w in (d_query_w, d_compress_w, d_expand_w, d_output_w, router_grad)
    ]
    q_grad, kva_grad, kvb_grad, out_grad, router_out, smalls, *blocks = scatter(
        dense + [small_grads],
        True,
        3,
        [(w, r) for w, r in zip(others[peers - 1 :], turns)],
    )
    gu_sum, out_sum, smalls = lax.optimization_barrier((gu_sum, out_sum, smalls))
    mixed = (residual + out_sum.astype(f32)).astype(bf16)
    gu_sum = gu_sum.astype(f32).transpose(1, 0, 2)
    sgate_grad = gu_sum[:, :, :units].reshape(shared_gate.shape)
    sup_grad = gu_sum[:, :, units + lanes_more : 2 * units + lanes_more].reshape(shared_up.shape)
    eup_grad = plus(up_own.astype(f32), up_blocks)[None]
    edown_grad = plus(down_own.astype(f32), blocks)[None]
    attn_gain_grad = smalls[0, : attn_gain.shape[0]]
    kv_gain_grad = smalls[1, : kv_gain.shape[0]]
    ffn_gain_grad = smalls[2, : ffn_gain.shape[0]]
    balance = jnp.sum(frequency * (smalls[3, :expert_count] / valid_total))
    return (
        mixed,
        tokens_grad,
        balance,
        attn_gain_grad,
        q_grad,
        kva_grad,
        kv_gain_grad,
        kvb_grad,
        out_grad,
        ffn_gain_grad,
        router_out,
        sgate_grad,
        sup_grad,
        sdown_grad,
        egate_grad,
        eup_grad,
        edown_grad,
    )


def solution(mesh):
    return jax.shard_map(
        body,
        mesh=mesh,
        in_specs=(
            P(("expert", "fsdp"), None),
            P(("expert", "fsdp"), None),
            P(("expert", "fsdp"), None),
            P("expert"),
            P(("expert", "fsdp")),
            P(("expert", "fsdp"), None),
            P(("expert", "fsdp"), None),
            P(("expert", "fsdp")),
            P(("expert", "fsdp"), None),
            P(("expert", "fsdp"), None),
            P(("expert", "fsdp")),
            P(("expert", "fsdp"), None),
            P(("expert", "fsdp"), None),
            P(("expert", "fsdp"), None),
            P(("expert", "fsdp"), None),
            P("expert", "fsdp", None),
            P("expert", "fsdp", None),
            P("expert", None, "fsdp"),
        ),
        out_specs=(
            P(("expert", "fsdp"), None),
            P(("expert", "fsdp"), None),
            P(),
            P(("expert", "fsdp")),
            P(("expert", "fsdp"), None),
            P(("expert", "fsdp"), None),
            P(("expert", "fsdp")),
            P(("expert", "fsdp"), None),
            P(("expert", "fsdp"), None),
            P(("expert", "fsdp")),
            P(("expert", "fsdp"), None),
            P(("expert", "fsdp"), None),
            P(("expert", "fsdp"), None),
            P(("expert", "fsdp"), None),
            P("expert", "fsdp", None),
            P("expert", "fsdp", None),
            P("expert", None, "fsdp"),
        ),
        check_vma=False,
    )
```

```python
import functools

import jax
import jax.numpy as jnp
from jax import lax
from jax.experimental import pallas as pl
from jax.experimental.pallas import tpu as pltpu
from jax.sharding import PartitionSpec as P

D = 2048
H = 16
DN = 128
DR = 64
DV = 128
KVR = 512
TOPK = 6


epsilon = 1e-06
balance_weight = 0.001
masked_value = -1e30


def rms_norm(vector, gain_row):
    inverse = lax.rsqrt(jnp.mean(vector * vector, axis=-1, keepdims=True) + epsilon)
    return (vector * inverse * gain_row, inverse)


def norm_back(grad_in, vector, inverse, gain_row):
    scaled = grad_in * gain_row
    gain_grad = jnp.sum(grad_in * vector * inverse, axis=0)
    vector_grad = inverse * scaled - vector * inverse**3 * jnp.mean(
        scaled * vector, axis=-1, keepdims=True
    )
    return (vector_grad, gain_grad)


def rope_tables(positions):
    half_width = DR // 2
    frequency = 10000.0 ** (-jnp.arange(half_width, dtype=jnp.float32) / half_width)
    angles = positions.astype(jnp.float32)[:, None] * frequency[None, :]
    return (jnp.cos(angles), jnp.sin(angles))


def rotate(vector, cosine, sine_vals):
    half_width = vector.shape[-1] // 2
    first_half = vector[..., :half_width]
    second_half = vector[..., half_width:]
    return jnp.concatenate(
        [
            first_half * cosine - second_half * sine_vals,
            second_half * cosine + first_half * sine_vals,
        ],
        axis=-1,
    )


def rotate_back(grad_in, cosine, sine_vals):
    half_width = grad_in.shape[-1] // 2
    first_half = grad_in[..., :half_width]
    second_half = grad_in[..., half_width:]
    return jnp.concatenate(
        [
            first_half * cosine + second_half * sine_vals,
            second_half * cosine - first_half * sine_vals,
        ],
        axis=-1,
    )


def silu_slope(vector):
    sigmoid_vals = jax.nn.sigmoid(vector)
    return sigmoid_vals * (1.0 + vector * (1.0 - sigmoid_vals))


MESH_IDS = pl.DeviceIdType.MESH


class Place:
    def __init__(self, group, peers, wide):
        self.wide = wide
        self.depth = min(4, group // 2)
        self.tall = group // 2 // self.depth
        self.across = peers if wide else 1
        self.peers = peers
        self.units = self.depth * self.tall * self.across
        self.slots = 2 * self.units

    def here(self):
        e = lax.axis_index("expert")
        self.fsdp = lax.axis_index("fsdp")
        self.c = e % 2
        self.y = e // 2 % self.tall
        self.z = e // (2 * self.tall)
        self.x = self.fsdp if self.wide else 0
        return self

    def detour(self, z):
        return (self.depth - 1) * (1 - z % 2)

    def partner(self):
        return self.z + 1 - self.z % 2 * 2

    def greet_peers(self):
        barrier = pltpu.get_barrier_semaphore()
        for k in range(1, self.peers):
            pl.semaphore_signal(
                barrier,
                inc=1,
                device_id=self.device(self.z, self.y, self.c, (self.fsdp + k) % self.peers),
                device_id_type=MESH_IDS,
            )
        pl.semaphore_wait(barrier, self.peers - 1)

    def slot(self, z, y, c, x):
        return ((z * self.tall + y) * 2 + c) * self.across + x

    def device(self, z, y, c, x=None):
        return ((z * self.tall + y) * 2 + c, self.fsdp if x is None else x)

    def greet(self, swapping):
        barrier = pltpu.get_barrier_semaphore()
        partners = self.peers if swapping or self.wide else 1
        count = 1 + (self.tall - 1) + (partners - 1)

        def signal(target):
            pl.semaphore_signal(barrier, inc=1, device_id=target, device_id_type=MESH_IDS)

        signal(self.device(self.z, self.y, 1 - self.c))
        for k in range(1, self.tall):
            signal(self.device(self.z, (self.y + k) % self.tall, self.c))
        for k in range(1, partners):
            signal(self.device(self.z, self.y, self.c, (self.fsdp + k) % self.peers))

        @pl.when(self.z > 0)
        def _():
            signal(self.device(self.z - 1, self.y, self.c))

        @pl.when(self.z < self.depth - 1)
        def _():
            signal(self.device(self.z + 1, self.y, self.c))

        last = self.depth - 1
        pl.semaphore_wait(barrier, count + 2 - self.z // last - (last - self.z) // last)


def remote(src, dst, send_sem, recv_sem, target):
    return pltpu.make_async_remote_copy(
        src_ref=src,
        dst_ref=dst,
        send_sem=send_sem,
        recv_sem=recv_sem,
        device_id=target,
        device_id_type=MESH_IDS,
    )


class Swaps:
    def __init__(self, place, shifts, given, taken, send_sem, recv_sem):
        self.copies = [
            remote(
                given[i],
                taken[i],
                send_sem.at[i],
                recv_sem.at[i],
                place.device(place.z, place.y, place.c, (place.fsdp + shift) % place.peers),
            )
            for i, shift in enumerate(shifts)
        ]

    def start(self):
        for copy in self.copies:
            copy.start()

    def wait(self):
        for copy in self.copies:
            copy.wait()


def gather_kernel(place, count, shifts, spans, into, *refs):
    total = count + len(shifts)
    ins, given = refs[:count], refs[count:total]
    refs = refs[:total] + refs[total + into :]
    outs, taken = refs[total : total + count], refs[total + count : 2 * total]
    given = [w if at is None else w.at[pl.ds(*at)] for w, at in zip(given, spans)]
    taken = [w if at is None else w.at[pl.ds(*at)] for w, at in zip(taken, spans)]
    near, xs, ys, cs, rc, zs, got, given_sem, taken_sem, es = refs[2 * total :]
    p = place.here()
    depth, tall, across = p.depth, p.tall, p.across
    p.greet(len(shifts) > 0)
    sibling = p.device(p.z, p.y, 1 - p.c)

    def unit(z, y, x):
        return (z * tall + y) * across + x

    def block(a, z, y, x):
        return outs[a].at[p.slot(z, y, p.c, x)]

    def to_z(a, src, z, x, way):
        return remote(
            src,
            block(a, z, p.y, x),
            zs.at[a, way, z * across + x],
            got.at[a, unit(z, p.y, x)],
            p.device(p.z + 2 * way - 1, p.y, p.c),
        )

    def to_y(a, src, z, x, k):
        return remote(
            src,
            block(a, z, p.y, x),
            ys.at[a],
            got.at[a, unit(z, p.y, x)],
            p.device(p.z, (p.y + k) % tall, p.c),
        )

    def to_sibling(a, src, z, y, x):
        return remote(src, block(a, z, y, x), cs.at[a], rc.at[a], sibling)

    def arrived(a, z, y, x):
        remote(block(a, z, y, x), block(a, z, y, x), cs.at[a], got.at[a, unit(z, y, x)], sibling).wait_recv()

    def spread(a, src, z, x, ways):
        for way in ways:

            @pl.when((p.z < depth - 1) if way else (p.z > 0))
            def _():
                to_z(a, src, z, x, way).start()

        @pl.when((p.c == 1) | (z != p.detour(p.z)))
        def _():
            for k in range(1, tall):
                to_y(a, src, z, x, k).start()

        to_sibling(a, src, z, p.y, x).start()

    def to_partner(a, z, y, x, k):
        return remote(
            block(a, z, y, x),
            block(a, z, y, x),
            es.at[a, x * max(tall - 1, 1) + k - 1],
            got.at[a, unit(z, y, x)],
            p.device(p.partner(), p.y, p.c),
        )

    def over_x(step):
        if across == 1:
            step(0)
        else:
            lax.fori_loop(0, across, lambda k, _: (step((p.x + k) % across), 0)[1], 0)

    for a in range(count):
        for k in range(1, across):
            remote(
                ins[a],
                block(a, p.z, p.y, p.x),
                xs.at[a],
                got.at[a, unit(p.z, p.y, p.x)],
                p.device(p.z, p.y, p.c, (p.x + k) % across),
            ).start()
        spread(a, ins[a], p.z, p.x, (0, 1))
        pltpu.make_async_copy(ins[a], block(a, p.z, p.y, p.x), near.at[a]).start()

    swaps = Swaps(p, shifts, given, taken, given_sem, taken_sem)
    swaps.start()
    for k in range(1, across):
        x = (p.x + k) % across
        for a in range(count):
            arrived(a, p.z, p.y, x)
            spread(a, block(a, p.z, p.y, x), p.z, x, (0, 1))

    def from_y(z):
        def step(x):
            for k in range(1, tall):
                y = (p.y + k) % tall
                for a in range(count):
                    arrived(a, z, y, x)

                    @pl.when((p.c == 0) & (z == p.detour(p.partner())))
                    def _(a=a, y=y, k=k):
                        to_partner(a, z, y, x, k).start()

                    to_sibling(a, block(a, z, y, x), z, y, x).start()

        over_x(step)

    for d in range(1, depth + 1):
        if d < depth:

            @pl.when(p.z >= d)
            def _(d=d):
                def step(x):
                    for a in range(count):
                        arrived(a, p.z - d, p.y, x)
                        spread(a, block(a, p.z - d, p.y, x), p.z - d, x, (1,))

                over_x(step)

            @pl.when(p.z + d < depth)
            def _(d=d):
                def step(x):
                    for a in range(count):
                        arrived(a, p.z + d, p.y, x)
                        spread(a, block(a, p.z + d, p.y, x), p.z + d, x, (0,))

                over_x(step)

        if d == 1:
            from_y(p.z)
        else:

            @pl.when(p.z >= d - 1)
            def _(d=d):
                from_y(p.z - d + 1)

            @pl.when(p.z + d - 1 < depth)
            def _(d=d):
                from_y(p.z + d - 1)

    for a in range(count):
        pltpu.make_async_copy(ins[a], block(a, p.z, p.y, p.x), near.at[a]).wait()

        def many(number, send, recv):
            part = outs[a].at[pl.ds(0, number)]
            return remote(part, part, send.at[a], recv.at[a], sibling)

        if across > 1:
            many(across - 1, xs, rc).wait_send()
        if tall > 1:

            @pl.when(p.c == 1)
            def _():
                many((tall - 1) * depth * across, ys, rc).wait_send()

            @pl.when(p.c == 0)
            def _(a=a):
                many((tall - 1) * (depth - 1) * across, ys, rc).wait_send()
                for x in range(across):
                    for k in range(1, tall):
                        to_partner(a, 0, p.y, x, k).wait_send()

        many(p.units, cs, rc).wait()
        for z in range(depth):
            for way in (0, 1):

                @pl.when(
                    ((p.z >= z) & (p.z < depth - 1)) if way else ((p.z <= z) & (p.z > 0))
                )
                def _(z=z, way=way, a=a):
                    for x in range(across):
                        to_z(a, block(a, z, p.y, x), z, x, way).wait_send()

    swaps.wait()


def split_swaps(swapped):
    return [w for w, _ in swapped], [shift for _, shift in swapped]


def gather(shards, wide, collective_id, swapped=()):
    group, peers = lax.axis_size("expert"), lax.axis_size("fsdp")
    place = Place(group, peers, wide)
    given, shifts = split_swaps([w[:2] for w in swapped])
    spans = [w[2] if len(w) > 2 else None for w in swapped]
    into = {i: w[3] for i, w in enumerate(swapped) if len(w) > 3}
    count, extra = len(shards), len(given)
    aliases = {count + extra + j: count + i for j, i in enumerate(into)}
    dma = pltpu.SemaphoreType.DMA
    return pl.pallas_call(
        functools.partial(gather_kernel, place, count, shifts, spans, len(into)),
        out_shape=[jax.ShapeDtypeStruct((place.slots,) + s.shape, s.dtype) for s in shards]
        + [jax.ShapeDtypeStruct(s.shape, s.dtype) for s in given],
        in_specs=[pl.BlockSpec(memory_space=pl.ANY)] * (count + extra + len(into)),
        out_specs=[pl.BlockSpec(memory_space=pl.ANY)] * (count + extra),
        input_output_aliases=aliases,
        scratch_shapes=[dma((count,))] * 5
        + [
            dma((count, 2, place.depth * place.across)),
            dma((count, place.units)),
            dma((max(extra, 1),)),
            dma((max(extra, 1),)),
            dma((count, place.across * max(place.tall - 1, 1))),
        ],
        compiler_params=pltpu.CompilerParams(
            collective_id=collective_id, has_side_effects=True, vmem_limit_bytes=58 << 20
        ),
        name=f"gather{collective_id}",
    )(*shards, *given, *into.values())


def chunk_of(left):
    return 256 if left.shape[1] % 256 == 0 else 128


class Pairs:
    def __init__(self, products):
        self.arrays = []
        self.uses = []
        for pair in products:
            use = []
            for array in pair:
                known = [i for i, other in enumerate(self.arrays) if other is array]
                if not known:
                    self.arrays.append(array)
                    known = [len(self.arrays) - 1]
                use.append(known[0])
            self.uses.append(tuple(use))

    def shapes(self):
        arrays = self.arrays
        return [
            jax.ShapeDtypeStruct((arrays[i].shape[1], arrays[j].shape[1]), jnp.bfloat16)
            for i, j in self.uses
        ]

    def room(self):
        if not self.uses:
            return []
        arrays = self.arrays
        held = [pltpu.VMEM(v.shape, v.dtype) for v in arrays]
        ready = [
            pltpu.VMEM((2, chunk_of(arrays[i]), arrays[j].shape[1]), jnp.bfloat16)
            for i, j in self.uses
        ]
        dma = pltpu.SemaphoreType.DMA
        return held + ready + [dma((len(arrays),)), dma((len(self.uses), 2))]


class Products:
    def __init__(self, uses, operands, results, refs):
        self.uses = uses
        if uses:
            held = refs[: len(operands)]
            self.loads = list(zip(operands, held))
            self.in_sems, self.out_sems = refs[len(operands) + len(uses) :]
            ready = refs[len(operands) : len(operands) + len(uses)]
            self.parts = [(r, held[i], held[j], v) for (i, j), r, v in zip(uses, results, ready)]

    def load(self, k):
        source, held = self.loads[k]
        return pltpu.make_async_copy(source, held, self.in_sems.at[k])

    def start(self):
        for k in range(len(self.loads) if self.uses else 0):
            self.load(k).start()

    def run(self, i):
        earlier = [k for use in self.uses[:i] for k in use]
        for k in sorted(set(self.uses[i]) - set(earlier)):
            self.load(k).wait()
        result, left, right, ready = self.parts[i]
        chunk = chunk_of(left)
        steps = left.shape[1] // chunk

        def leave(j):
            return pltpu.make_async_copy(
                ready.at[j % 2],
                result.at[pl.ds(pl.multiple_of(j * chunk, chunk), chunk)],
                self.out_sems.at[i, j % 2],
            )

        def go(j, _):
            @pl.when(j >= 2)
            def _():
                leave(j - 2).wait()

            part = pl.ds(pl.multiple_of(j * chunk, chunk), chunk)
            ready[j % 2] = dot_turned(left[:, part], right[...]).astype(ready.dtype)
            leave(j).start()
            return 0

        lax.fori_loop(0, steps, go, 0)
        for j in range(max(steps - 2, 0), steps):
            leave(j).wait()


def exchange_kernel(place, shifts, uses, operands, *refs):
    extra, pairs = len(shifts), len(uses)
    given, refs = refs[:extra], refs[extra:]
    loads, refs = refs[:operands], refs[operands:]
    left, right, refs = refs[0], refs[1], refs[2:]
    taken, results, refs = refs[:extra], refs[extra : extra + pairs], refs[extra + pairs :]
    across, held, held_sem, refs = refs[0], refs[1], refs[2], refs[3:]
    p = place.here()
    p.greet_peers()
    swaps = Swaps(p, shifts, given, taken, *refs[:2])
    swaps.start()
    products = Products(uses, loads, results, refs[2:])
    products.start()
    arrive = pltpu.make_async_copy(right, held, held_sem)
    arrive.start()
    for i in range(pairs):
        products.run(i)
    arrive.wait()
    chunk = 256

    def go(j, _):
        part = pl.ds(pl.multiple_of(j * chunk, chunk), chunk)
        across[:, part] = dot_across(left[...], held[part, :])
        return 0

    lax.fori_loop(0, held.shape[0] // chunk, go, 0)
    swaps.wait()


def exchange(collective_id, swapped, products, left, right):
    place = Place(lax.axis_size("expert"), lax.axis_size("fsdp"), False)
    given, shifts = split_swaps(swapped)
    pairs = Pairs(products)
    extra, operands = len(given), len(pairs.arrays)
    anywhere, inside = pl.BlockSpec(memory_space=pl.ANY), pl.BlockSpec(memory_space=pltpu.VMEM)
    dma = pltpu.SemaphoreType.DMA
    return pl.pallas_call(
        functools.partial(exchange_kernel, place, shifts, pairs.uses, operands),
        out_shape=[jax.ShapeDtypeStruct(s.shape, s.dtype) for s in given]
        + pairs.shapes()
        + [jax.ShapeDtypeStruct((left.shape[0], right.shape[0]), jnp.float32)],
        in_specs=[anywhere] * (extra + operands) + [inside, anywhere],
        out_specs=[anywhere] * (extra + len(products)) + [inside],
        scratch_shapes=[pltpu.VMEM(right.shape, right.dtype), dma, dma((extra,)), dma((extra,))]
        + pairs.room(),
        compiler_params=pltpu.CompilerParams(
            collective_id=collective_id, has_side_effects=True, vmem_limit_bytes=56 << 20
        ),
        name=f"exchange{collective_id}",
    )(*given, *pairs.arrays, left, right)


def outer_kernel(count, *refs):
    for i in range(count):
        left, right, result = refs[i], refs[count + i], refs[2 * count + i]
        chunk = chunk_of(left)

        def go(j, _):
            part = pl.ds(pl.multiple_of(j * chunk, chunk), chunk)
            result[part, :] = dot_turned(left[:, part], right[...]).astype(result.dtype)
            return 0

        lax.fori_loop(0, left.shape[1] // chunk, go, 0)


def outer_products(products):
    return pl.pallas_call(
        functools.partial(outer_kernel, len(products)),
        out_shape=Pairs(products).shapes(),
        in_specs=[pl.BlockSpec(memory_space=pltpu.VMEM)] * (2 * len(products)),
        out_specs=[pl.BlockSpec(memory_space=pltpu.VMEM)] * len(products),
        compiler_params=pltpu.CompilerParams(vmem_limit_bytes=32 << 20),
        name="outer",
    )(*[v for v, _ in products], *[w for _, w in products])


def scatter_kernel(place, count, shifts, uses, operands, *refs):
    total, pairs = count + len(shifts), len(uses)
    ins, given = refs[:count], refs[count:total]
    loads, refs = refs[total : total + operands], refs[total + operands :]
    outs, taken, results = refs[:count], refs[count:total], refs[total : total + pairs]
    refs = refs[total + pairs :]
    held, side, rows_y, rows_z, rows_x, rows_e = (
        refs[i * count : (i + 1) * count] for i in range(6)
    )
    la, rc, yr, zr, zs, cs, ys, xs, xr, given_sem, taken_sem, es, er, *room = refs[6 * count :]
    p = place.here()
    depth, tall, across = p.depth, p.tall, p.across
    p.greet(len(shifts) > 0)
    sibling = p.device(p.z, p.y, 1 - p.c)
    half = max(depth // 2, 1)

    def in_order(step):
        lower = 1 - p.z // half

        def right(total, done):
            def go(j, _):
                step(depth - 1 - j // across, (p.x + 1 + j % across) % across, 1, done * across + j)
                return 0

            lax.fori_loop(0, total * across, go, 0)

        def left(total, done):
            def go(j, _):
                step(j // across, (p.x + 1 + j % across) % across, 0, done * across + j)
                return 0

            lax.fori_loop(0, total * across, go, 0)

        early = (depth - 1 - p.z) * lower
        right(early, 0)
        left(p.z, early)
        right((depth - 1 - p.z) * (1 - lower), early + p.z)

        def own(j, _):
            step(p.z, (p.x + 1 + j) % across, None, (depth - 1) * across + j)
            return 0

        lax.fori_loop(0, across, own, 0)

    def local(a, k, z, y, x):
        return pltpu.make_async_copy(ins[a].at[p.slot(z, y, p.c, x)], held[a].at[k, y], la.at[a, k])

    def begin(z, x, way, number):
        k = z * across + x
        for a in range(count):
            for y in range(tall):
                remote(
                    ins[a].at[p.slot(z, y, 1 - p.c, x)],
                    side[a].at[k, y],
                    cs.at[a],
                    rc.at[a, k],
                    sibling,
                ).start()
                local(a, k, z, y, x).start()

    def add(a, target, sources):
        rows = ins[a].shape[1]
        chunk = 16 if rows % 16 == 0 else rows

        def go(i, _):
            part = pl.ds(i * chunk, chunk)
            total = target[part].astype(jnp.float32)
            for source in sources:
                total = total + source[part].astype(jnp.float32)
            target[part] = total.astype(target.dtype)
            return 0

        lax.fori_loop(0, rows // chunk, go, 0)

    def first(z, x, way, number):
        k = z * across + x
        for a in range(count):
            pltpu.make_async_copy(held[a].at[k], held[a].at[k], la.at[a, k]).wait()
            remote(side[a].at[k], side[a].at[k], cs.at[a], rc.at[a, k], sibling).wait_recv()
            for j in range(1, tall):
                y = (p.y + j) % tall
                mine = held[a].at[k, y]

                def along_y(sources, mine=mine, j=j, y=y, a=a):
                    add(a, mine, sources)
                    remote(
                        mine,
                        rows_y[a].at[k, tall - j - 1],
                        ys.at[a],
                        yr.at[a, k],
                        p.device(p.z, y, p.c),
                    ).start()

                @pl.when((p.c == 0) & (z == p.detour(p.z)))
                def _(mine=mine, j=j, y=y, a=a):
                    add(a, mine, [side[a].at[k, y]])
                    remote(
                        mine,
                        rows_e[a].at[x, j - 1],
                        es.at[a],
                        er.at[a, x * (tall - 1) + j - 1],
                        p.device(p.partner(), p.y, p.c),
                    ).start()

                @pl.when((p.c == 0) & (z == p.detour(p.partner())))
                def _(j=j, y=y, a=a, along_y=along_y):
                    part = rows_e[a].at[x, j - 1]
                    remote(
                        part, part, cs.at[a], er.at[a, x * (tall - 1) + j - 1], sibling
                    ).wait_recv()
                    along_y([side[a].at[k, y], part])

                @pl.when((p.c == 1) | ((z != p.detour(p.z)) & (z != p.detour(p.partner()))))
                def _(y=y, a=a, along_y=along_y):
                    along_y([side[a].at[k, y]])

            add(a, held[a].at[k, p.y], [side[a].at[k, p.y]])

    products = Products(uses, loads, results, room)
    items = depth * across

    def second(z, x, way, number):
        k = z * across + x
        for i in range(pairs):
            turn = i * items // pairs
            if (way is None) == (turn >= (depth - 1) * across):
                pl.when(number == turn)(functools.partial(products.run, i))
        for a in range(count):
            mine = held[a].at[k, p.y]
            if tall > 1:

                @pl.when((p.c == 1) | (z != p.detour(p.z)))
                def _(a=a, mine=mine):
                    part = rows_y[a].at[k]
                    remote(part, part, cs.at[a], yr.at[a, k], sibling).wait_recv()
                    add(a, mine, [rows_y[a].at[k, j] for j in range(tall - 1)])

            def from_z(index):
                part = rows_z[a].at[index]
                remote(part, part, cs.at[a], zr.at[a, index], sibling).wait_recv()
                add(a, mine, [part])

            def send(index, target):
                remote(mine, rows_z[a].at[index], zs.at[a, k], zr.at[a, index], target).start()

            if way is None or way == 1:
                pl.when(p.z > 0)(functools.partial(from_z, k))
            if way is None:
                pl.when(p.z < depth - 1)(functools.partial(from_z, depth * across + x))
            if way == 0:
                pl.when(p.z < depth - 1)(functools.partial(from_z, k))
            if way == 1:
                send(k, p.device(p.z + 1, p.y, p.c))
            if way == 0:
                left = p.device(p.z - 1, p.y, p.c)

                @pl.when(z == p.z - 1)
                def _():
                    send(depth * across + x, left)

                @pl.when(z < p.z - 1)
                def _():
                    send(k, left)

            if way is None and across > 1:

                @pl.when(x != p.x)
                def _():
                    remote(
                        mine,
                        rows_x[a].at[(p.x - x + across) % across - 1],
                        xs.at[a],
                        xr.at[a],
                        p.device(p.z, p.y, p.c, x),
                    ).start()

    ahead = min(across + 1 if across > 1 else 2, items)
    lower = 1 - p.z // half
    switch = lower * (depth - 1 - p.z) + (1 - lower) * p.z

    def first_at(number):
        j = number // across
        own = j // (depth - 1)
        past = (j - switch + depth) // depth
        down, up = depth - 1 - j, j
        down_late, up_late = depth - 1 - (j - switch), j - switch
        z = lower * ((1 - past) * down + past * up_late)
        z = z + (1 - lower) * ((1 - past) * up + past * down_late)
        z = own * p.z + (1 - own) * z
        first(z, (p.x + 1 + number % across) % across, None, number)

    def both(z, x, way, number):
        if way is not None:

            @pl.when(number + ahead < items)
            def _():
                first_at(number + ahead)

        second(z, x, way, number)

    swaps = Swaps(p, shifts, given, taken, given_sem, taken_sem)
    swaps.start()
    in_order(begin)
    products.start()
    lax.fori_loop(0, ahead, lambda n, _: (first_at(n), 0)[1], 0)
    in_order(both)
    k = p.z * across + p.x
    for a in range(count):
        mine = held[a].at[k, p.y]
        sources = []
        if across > 1:
            remote(rows_x[a], rows_x[a], xs.at[a], xr.at[a], sibling).wait()
            sources = [rows_x[a].at[j] for j in range(across - 1)]
        rows = ins[a].shape[1]
        chunk = 16 if rows % 16 == 0 else rows

        def go(i, _):
            part = pl.ds(i * chunk, chunk)
            total = mine[part].astype(jnp.float32)
            for source in sources:
                total = total + source[part].astype(jnp.float32)
            outs[a][part] = total
            return 0

        lax.fori_loop(0, rows // chunk, go, 0)
        remote(side[a], side[a], cs.at[a], rc.at[a, 0], sibling).wait_send()
        if tall > 1:

            @pl.when(p.c == 1)
            def _(a=a):
                remote(rows_y[a], rows_y[a], ys.at[a], rc.at[a, 0], sibling).wait_send()

            @pl.when(p.c == 0)
            def _(a=a):
                part = rows_y[a].at[pl.ds(0, (depth - 1) * across)]
                remote(part, part, ys.at[a], rc.at[a, 0], sibling).wait_send()
                remote(rows_e[a], rows_e[a], es.at[a], rc.at[a, 0], sibling).wait_send()

        def wait_z(k, _):
            @pl.when(k // across != p.z)
            def _():
                remote(mine, rows_z[a].at[0], zs.at[a, k], rc.at[a, 0], sibling).wait_send()

            return 0

        lax.fori_loop(0, depth * across, wait_z, 0)

    swaps.wait()


def scatter(partials, wide, collective_id, swapped=(), products=()):
    group, peers = lax.axis_size("expert"), lax.axis_size("fsdp")
    place = Place(group, peers, wide)
    given, shifts = split_swaps(swapped)
    pairs = Pairs(products)
    count, extra, operands = len(partials), len(given), len(pairs.arrays)
    dma = pltpu.SemaphoreType.DMA
    items = place.depth * place.across

    def room(*lead):
        return [pltpu.VMEM(lead + s.shape[1:], s.dtype) for s in partials]

    return pl.pallas_call(
        functools.partial(scatter_kernel, place, count, shifts, pairs.uses, operands),
        out_shape=[jax.ShapeDtypeStruct(s.shape[1:], jnp.float32) for s in partials]
        + [jax.ShapeDtypeStruct(s.shape, s.dtype) for s in given]
        + pairs.shapes(),
        in_specs=[pl.BlockSpec(memory_space=pl.ANY)] * (count + extra + operands),
        out_specs=[pl.BlockSpec(memory_space=pltpu.VMEM)] * count
        + [pl.BlockSpec(memory_space=pl.ANY)] * extra
        + [pl.BlockSpec(memory_space=pl.ANY)] * len(products),
        scratch_shapes=room(items, place.tall)
        + room(items, place.tall)
        + room(items, max(place.tall - 1, 1))
        + room(items + place.across)
        + room(max(place.across - 1, 1))
        + room(place.across, max(place.tall - 1, 1))
        + [
            dma((count, items)),
            dma((count, items)),
            dma((count, items)),
            dma((count, items + place.across)),
            dma((count, items)),
            dma((count,)),
            dma((count,)),
            dma((count,)),
            dma((count,)),
            dma((max(extra, 1),)),
            dma((max(extra, 1),)),
            dma((count,)),
            dma((count, place.across * max(place.tall - 1, 1))),
        ]
        + pairs.room(),
        compiler_params=pltpu.CompilerParams(
            collective_id=collective_id, has_side_effects=True, vmem_limit_bytes=60 << 20
        ),
        name=f"scatter{collective_id}",
    )(*partials, *given, *pairs.arrays)


def dot_plain(left, right):
    return jnp.dot(left, right, preferred_element_type=jnp.float32)


def dot_across(left, right):
    return lax.dot_general(left, right, (((1,), (1,)), ((), ())), preferred_element_type=jnp.float32)


def dot_turned(left, right):
    return lax.dot_general(left, right, (((0,), (0,)), ((), ())), preferred_element_type=jnp.float32)


def ffn_kernel(peers, sources, numbers, fill, *refs):
    hid, cot, ranks = refs[:3]
    gates, ups, downs = (refs[3 + i * peers : 3 + (i + 1) * peers] for i in range(3))
    router, shared_in, shared_out = refs[3 + 3 * peers : 6 + 3 * peers]
    refs = refs[6 + 3 * peers :]
    rows, d_out = refs[:peers], refs[peers : 2 * peers]
    out_part, back_part, act, d_g, d_u, d_log, s_act, s_grad = refs[2 * peers : 8 + 2 * peers]
    rows_here, cots_here = refs[8 + 2 * peers :]
    f32, bf16 = jnp.float32, jnp.bfloat16
    step = pl.program_id(0)
    tok_rows = hid.shape[1]
    capacity = rows_here.shape[0] // sources
    width = hid.shape[2] // peers
    eid, start, fid = numbers[0], numbers[1], numbers[2]
    scale = fill[0]

    def length(s):
        return numbers[3 + step * sources + s]

    def columns(r):
        return pl.ds(pl.multiple_of((fid + r) % peers * width, width), width)

    scales = []
    picks = []
    for s in range(sources):
        part = pl.ds(s * capacity, capacity)
        slot = lax.broadcasted_iota(jnp.int32, (capacity, tok_rows), 0).astype(f32)
        pick = jnp.where(ranks[s] == slot, 1.0, 0.0)
        lane = start + lax.broadcasted_iota(jnp.int32, (1, tok_rows), 1)
        alive = jnp.where(lane < length(s), scale, 0.0)
        scales.append(jnp.sum(pick * alive, axis=1, keepdims=True))
        pick = pick.astype(bf16)
        picks.append(pick)
        rows_here[part, :] = dot_plain(pick, hid[s]).astype(bf16)
        cots_here[part, :] = dot_plain(pick, cot[s]).astype(bf16)
    row_scale = jnp.concatenate(scales, axis=0)
    logits = dot_plain(rows_here[...], router[...])
    top = jnp.max(logits, axis=1, keepdims=True)
    powers = jnp.exp(logits - top)
    probs = powers / jnp.sum(powers, axis=1, keepdims=True)
    own = (lax.broadcasted_iota(jnp.int32, (1, probs.shape[1]), 1) == eid).astype(f32)
    gate = jnp.sum(probs * own, axis=1, keepdims=True)

    for r in range(peers):
        rows[r][...] = rows_here[:, columns(r)]

    def summed(terms):
        total = terms[0]
        for term in terms[1:]:
            total = total + term
        return total

    g = summed([dot_plain(rows[r][...], gates[r][...]) for r in range(peers)])
    u = summed([dot_plain(rows[r][...], ups[r][...]) for r in range(peers)])
    sigma = 1.0 / (1.0 + jnp.exp(-g))
    act_now = (g * sigma * u).astype(bf16)
    act[...] = act_now
    d_gate = jnp.zeros_like(gate)
    weighted = []
    for r in range(peers):
        out = dot_plain(act_now, downs[r][...]).astype(bf16).astype(f32)
        row_cot = cots_here[:, columns(r)].astype(f32)
        d_out[r][...] = ((gate * row_scale) * row_cot).astype(bf16)
        d_gate = d_gate + jnp.sum(row_cot * out, axis=1, keepdims=True)
        weighted.append((gate * out).astype(bf16))
    d_gate = d_gate * row_scale
    d_act = summed([dot_across(d_out[r][...], downs[r][...]) for r in range(peers)])
    dg_now = (d_act * u * (sigma * (1.0 + g * (1.0 - sigma)))).astype(bf16)
    du_now = (d_act * (g * sigma)).astype(bf16)
    d_g[...] = dg_now
    d_u[...] = du_now
    dl_now = (gate * d_gate * (own - probs)).astype(bf16)
    d_log[...] = dl_now
    d_rows = []
    for r in range(peers):
        total = dot_across(dg_now, gates[r][...]) + dot_across(du_now, ups[r][...])
        total = total + dot_across(dl_now, router[columns(r), :])
        d_rows.append(total.astype(bf16))
    units = shared_out.shape[0]
    total_rows = sources * tok_rows
    hid_all = hid[...].reshape(total_rows, hid.shape[2])
    cot_all = cot[...].reshape(total_rows, hid.shape[2])
    both = dot_plain(hid_all, shared_in[...])
    sg, su = both[:, :units], both[:, units:]
    s_sigma = 1.0 / (1.0 + jnp.exp(-sg))
    s_now = sg * s_sigma * su
    column = lax.broadcasted_iota(jnp.int32, (tok_rows, 1), 0) + start
    alive = jnp.concatenate(
        [jnp.where(column < length(s), scale, 0.0) for s in range(sources)], axis=0
    )
    d_s = dot_across(cot_all, shared_out[...]) * alive
    s_act[...] = (s_now * alive).astype(bf16)
    s_low = s_now.astype(bf16)
    d_sg = (d_s * su * (s_sigma * (1.0 + sg * (1.0 - s_sigma)))).astype(bf16)
    d_su = (d_s * (sg * s_sigma)).astype(bf16)
    s_grad[:, pl.ds(0, units)] = d_sg
    s_grad[:, pl.ds(units, units)] = d_su
    for r in range(peers):
        for n in range(0, width, 256):
            at = pl.ds(pl.multiple_of((fid + r) % peers * width + n, 256), 256)
            s_out = dot_plain(s_low, shared_out[:, at])
            s_back = dot_across(s_grad[...], shared_in[at, :])
            for s in range(sources):
                part = slice(s * capacity, (s + 1) * capacity)
                span = slice(s * tok_rows, (s + 1) * tok_rows)
                out_part[s, :, at] = (
                    dot_turned(picks[s], weighted[r][part, n : n + 256]) + s_out[span]
                ).astype(bf16)
                back_part[s, :, at] = (
                    dot_turned(picks[s], d_rows[r][part, n : n + 256]) + s_back[span]
                ).astype(bf16)


def ffn(capacity, numbers, fill, hid, cot, ranks, gates, ups, downs, router, shared_in, shared_out):
    group, tok_rows, dim = hid.shape
    peers = len(gates)
    sources = max(1, min(4, 256 // capacity))
    hidden = gates[0].shape[1]
    units = shared_out.shape[0]
    rows = sources * capacity
    bf16 = jnp.bfloat16

    def whole(array):
        return pl.BlockSpec(
            array.shape, lambda i, *_: (0,) * array.ndim, pipeline_mode=pl.Buffered(1)
        )

    def tile(*shape):
        return pl.BlockSpec(shape, lambda i, *_: (i,) + (0,) * (len(shape) - 1))

    pairs = group * capacity
    weights = [*gates, *ups, *downs, router, shared_in, shared_out]
    return pl.pallas_call(
        functools.partial(ffn_kernel, peers, sources),
        out_shape=[jax.ShapeDtypeStruct((pairs, dim // peers), bf16)] * (2 * peers)
        + [
            jax.ShapeDtypeStruct((group, tok_rows, dim), bf16),
            jax.ShapeDtypeStruct((group, tok_rows, dim), bf16),
            jax.ShapeDtypeStruct((pairs, hidden), bf16),
            jax.ShapeDtypeStruct((pairs, hidden), bf16),
            jax.ShapeDtypeStruct((pairs, hidden), bf16),
            jax.ShapeDtypeStruct((pairs, router.shape[1]), bf16),
            jax.ShapeDtypeStruct((group * tok_rows, units), bf16),
            jax.ShapeDtypeStruct((group * tok_rows, 2 * units), bf16),
        ],
        grid_spec=pltpu.PrefetchScalarGridSpec(
            num_scalar_prefetch=2,
            grid=(group // sources,),
            in_specs=[
                tile(sources, tok_rows, dim),
                tile(sources, tok_rows, dim),
                tile(sources, 1, tok_rows),
            ]
            + [whole(w) for w in weights],
            out_specs=[tile(rows, dim // peers)] * (2 * peers)
            + [
                tile(sources, tok_rows, dim),
                tile(sources, tok_rows, dim),
                tile(rows, hidden),
                tile(rows, hidden),
                tile(rows, hidden),
                tile(rows, router.shape[1]),
                tile(sources * tok_rows, units),
                tile(sources * tok_rows, 2 * units),
            ],
            scratch_shapes=[pltpu.VMEM((rows, dim), bf16)] * 2,
        ),
        compiler_params=pltpu.CompilerParams(vmem_limit_bytes=62 << 20),
        cost_estimate=pl.CostEstimate(
            flops=18 * pairs * dim * hidden, bytes_accessed=60 << 20, transcendentals=1 << 22
        ),
        name="ffn",
    )(numbers, fill, hid, cot, ranks, *weights)


def both_keys(keyval, rot):
    f32 = jnp.float32
    rot = rot.astype(f32)
    first = jnp.concatenate([keyval[:, :DN].astype(f32), rot], axis=1)
    second = jnp.concatenate([keyval[:, DN + DV : 2 * DN + DV].astype(f32), rot], axis=1)
    second = pltpu.roll(second, DN + DR, 1)
    return first.astype(jnp.bfloat16), second.astype(jnp.bfloat16)


def turn(array, plain, ahead, behind):
    width = array.shape[1]
    return (
        array * plain
        + pltpu.roll(array, width - DR // 2, 1) * ahead
        + pltpu.roll(array, DR // 2, 1) * behind
    )


def attend_kernel(numbers, hidden, w_query, latent, w_expand, rot, plain, ahead, behind, *outs):
    query, keyval, probs, context = outs
    bf16 = jnp.bfloat16
    turned = turn(dot_plain(hidden[...], w_query[...]), plain[...], ahead[...], behind[...])
    query_now = turned.astype(bf16)
    query[...] = query_now
    keyval[...] = dot_plain(latent[...], w_expand[...]).astype(bf16)
    rows, keys = query.shape[0], keyval.shape[0]
    row = lax.broadcasted_iota(jnp.int32, (rows, keys), 0) + numbers[0]
    key = lax.broadcasted_iota(jnp.int32, (rows, keys), 1)
    allowed = (key <= row) & (key < numbers[1])
    for i, keys_now in enumerate(both_keys(keyval[...], rot[...])):
        scores = dot_across(query_now, keys_now) * (DN + DR) ** (-0.5)
        scores = jnp.where(allowed, scores, masked_value)
        powers = jnp.exp(scores - jnp.max(scores, axis=1, keepdims=True))
        share = powers / jnp.sum(powers, axis=1, keepdims=True)
        probs[i] = share
        value = keyval[:, pl.ds(i * (DN + DV) + DN, DV)]
        context[:, pl.ds(i * DV, DV)] = dot_plain(share.astype(bf16), value).astype(bf16)


def attend(numbers, hidden, w_query, latent, w_expand, rot, turns):
    rows, dim = hidden.shape
    keys, rank = latent.shape
    bf16 = jnp.bfloat16

    def still(array):
        return pl.BlockSpec(array.shape, lambda i, *_: (0,) * array.ndim)

    def columns(height, width):
        return pl.BlockSpec((height, width), lambda i, *_: (0, i))

    return pl.pallas_call(
        attend_kernel,
        out_shape=[
            jax.ShapeDtypeStruct((rows, H * (DN + DR)), bf16),
            jax.ShapeDtypeStruct((keys, H * (DN + DV)), bf16),
            jax.ShapeDtypeStruct((H, rows, keys), jnp.float32),
            jax.ShapeDtypeStruct((rows, H * DV), bf16),
        ],
        grid_spec=pltpu.PrefetchScalarGridSpec(
            num_scalar_prefetch=1,
            grid=(H // 2,),
            in_specs=[
                still(hidden),
                columns(dim, 2 * (DN + DR)),
                still(latent),
                columns(rank, 2 * (DN + DV)),
                still(rot),
                *[still(t) for t in turns],
            ],
            out_specs=[
                columns(rows, 2 * (DN + DR)),
                columns(keys, 2 * (DN + DV)),
                pl.BlockSpec((2, rows, keys), lambda i, *_: (i, 0, 0)),
                columns(rows, 2 * DV),
            ],
        ),
        compiler_params=pltpu.CompilerParams(vmem_limit_bytes=40 << 20),
        name="attend",
    )(numbers, hidden, w_query, latent, w_expand, rot, *turns)


def attend_back_kernel(d_res, w_output, query, keyval, probs, rot, plain, ahead, behind, *outs):
    d_query, d_keyval, d_rot = outs
    f32, bf16 = jnp.float32, jnp.bfloat16
    scale = (DN + DR) ** (-0.5)
    query_now = query[...]
    total = jnp.zeros(query.shape, f32)
    rot_total = jnp.zeros(d_rot.shape, f32)
    for i, keys_now in enumerate(both_keys(keyval[...], rot[...])):
        d_context = dot_across(d_res[...], w_output[pl.ds(i * DV, DV), :]).astype(bf16)
        share = probs[i]
        at = i * (DN + DV)
        d_value = dot_turned(share.astype(bf16), d_context)
        d_share = dot_across(d_context, keyval[:, pl.ds(at + DN, DV)])
        d_score = share * (d_share - jnp.sum(share * d_share, axis=1, keepdims=True))
        d_score = d_score.astype(bf16)
        total = total + dot_plain(d_score, keys_now) * scale
        d_key = dot_turned(d_score, query_now) * scale
        if i == 1:
            d_key = pltpu.roll(d_key, DN + DR, 1)
        d_keyval[:, pl.ds(at, DN)] = d_key[:, :DN].astype(bf16)
        d_keyval[:, pl.ds(at + DN, DV)] = d_value.astype(bf16)
        rot_total = rot_total + d_key[:, DN : 2 * DN]
    d_query[...] = turn(total, plain[...], -ahead[...], -behind[...]).astype(bf16)

    @pl.when(pl.program_id(0) == 0)
    def _():
        d_rot[...] = rot_total

    @pl.when(pl.program_id(0) != 0)
    def _():
        d_rot[...] += rot_total


def attend_back(d_res, w_output, query, keyval, probs, rot, turns):
    rows, dim = d_res.shape
    keys = keyval.shape[0]
    bf16 = jnp.bfloat16

    def still(array):
        return pl.BlockSpec(array.shape, lambda i: (0,) * array.ndim)

    def columns(height, width):
        return pl.BlockSpec((height, width), lambda i: (0, i))

    return pl.pallas_call(
        attend_back_kernel,
        out_shape=[
            jax.ShapeDtypeStruct(query.shape, bf16),
            jax.ShapeDtypeStruct(keyval.shape, bf16),
            jax.ShapeDtypeStruct((keys, DN), jnp.float32),
        ],
        grid=(H // 2,),
        in_specs=[
            still(d_res),
            pl.BlockSpec((2 * DV, dim), lambda i: (i, 0)),
            columns(rows, 2 * (DN + DR)),
            columns(keys, 2 * (DN + DV)),
            pl.BlockSpec((2, rows, keys), lambda i: (i, 0, 0)),
            still(rot),
            *[still(t) for t in turns],
        ],
        out_specs=[
            columns(rows, 2 * (DN + DR)),
            columns(keys, 2 * (DN + DV)),
            pl.BlockSpec((keys, DN), lambda i: (0, 0)),
        ],
        compiler_params=pltpu.CompilerParams(vmem_limit_bytes=40 << 20),
        name="attend_back",
    )(d_res, w_output, query, keyval, probs, rot, *turns)


def from_peers(block):
    size = lax.axis_size("fsdp")
    return [block] + [
        lax.ppermute(block, "fsdp", [(j, (j - r) % size) for j in range(size)])
        for r in range(1, size)
    ]


def sum_to_peers(term):
    size = lax.axis_size("fsdp")
    arrived = [
        lax.ppermute(term(r), "fsdp", [(j, (j + r) % size) for j in range(size)])
        for r in range(1, size)
    ]
    return arrived


def body(
    tokens,
    cotangent,
    routes,
    lengths,
    attn_gain,
    q_weight,
    kva_weight,
    kv_gain,
    kvb_weight,
    out_weight,
    ffn_gain,
    router_weight,
    shared_gate,
    shared_up,
    shared_down,
    expert_gate,
    expert_up,
    expert_down,
):
    bf16, f32 = jnp.bfloat16, jnp.float32
    tok_rows, dim = tokens.shape
    peers = lax.axis_size("fsdp")
    group = lax.axis_size("expert")
    fid, eid = lax.axis_index("fsdp"), lax.axis_index("expert")
    seq_len = tok_rows * peers
    slot_total = seq_len * group
    expert_count = router_weight.shape[1]
    capacity = max(4, 5 * tok_rows * TOPK // (4 * expert_count))
    capacity = -(-capacity // 16) * 16
    half = dim // peers
    plane_rows = group * tok_rows
    pairs = group * capacity

    positions = fid * tok_rows + jnp.arange(tok_rows, dtype=jnp.int32)
    seq_length = lengths[0]
    valid_mask = (positions < seq_length).astype(f32)
    expert_ids = jnp.arange(expert_count, dtype=jnp.int32)
    hot_sum = jnp.sum((routes[:, :, None] == expert_ids[None, None, :]).astype(f32), axis=1)
    local_counts = jnp.sum(hot_sum * valid_mask[:, None], axis=0)

    def lane_row(vector):
        return jnp.pad(vector.astype(f32), (0, tok_rows - vector.shape[0]))[None, :]

    small = jnp.concatenate(
        [routes.T.astype(f32)]
        + [lane_row(v) for v in (attn_gain, ffn_gain, kv_gain, local_counts, lengths)]
        + [jnp.zeros((16 - TOPK - 5, tok_rows), f32)],
        axis=0,
    )
    devices = group * peers
    turns = range(1, peers)
    w_query, w_compress, w_expand, w_output, w_router, small_all, *more = gather(
        [q_weight, kva_weight, kvb_weight, out_weight, router_weight, small],
        True,
        0,
        [(expert_gate[0], -r) for r in turns] + [(expert_up[0], -r, (0, half // 2)) for r in turns],
    )
    gate_parts = [expert_gate[0]] + more[: peers - 1]
    up_begun = more[peers - 1 :]
    w_query, w_compress, w_expand, w_output, w_router = (
        w.reshape(-1, w.shape[-1]) for w in (w_query, w_compress, w_expand, w_output, w_router)
    )
    gain_attn = small_all[:, TOPK, : attn_gain.shape[0]].reshape(-1)
    gain_ffn = small_all[:, TOPK + 1, : ffn_gain.shape[0]].reshape(-1)
    gain_latent = small_all[:, TOPK + 2, : kv_gain.shape[0]].reshape(-1)
    route_counts = jnp.sum(small_all[:, TOPK + 3, :expert_count], axis=0)
    all_lengths = small_all.reshape(group, peers, 16, tok_rows)[:, 0, TOPK + 4, 0]
    valid_total = jnp.sum(all_lengths)
    fill_scale = slot_total / valid_total
    plane_small = lax.dynamic_index_in_dim(
        small_all.reshape(group, peers, 16, tok_rows), fid, axis=1, keepdims=False
    )
    units = shared_gate.shape[1] // group
    lanes_more = -units % 128
    pieces = jnp.concatenate(
        [
            jnp.pad(w.reshape(-1, group, units), ((0, 0), (0, 0), (0, lanes_more)))
            for w in (shared_gate, shared_up)
        ],
        axis=2,
    ).transpose(1, 0, 2)
    pieces = lax.all_to_all(pieces, "expert", split_axis=0, concat_axis=0, tiled=True)
    sd_weight = jnp.roll(jnp.stack(from_peers(shared_down)), fid, axis=0).reshape(units, dim)
    sd_weight = jnp.pad(sd_weight, ((0, lanes_more), (0, 0)))
    cosine, sine_vals = rope_tables(positions)
    tokens_f = tokens.astype(f32)
    cot_ready, small_all = lax.optimization_barrier((cotangent, small_all))
    cot_plane = lax.all_gather(cot_ready, "expert", axis=0, tiled=True)
    normed_one, inverse_one = rms_norm(tokens_f, gain_attn)
    hidden_one = normed_one.astype(bf16)
    compressed = jnp.dot(hidden_one, w_compress, preferred_element_type=f32)
    latent_raw = compressed[:, :KVR]
    latent_norm, inverse_kv = rms_norm(latent_raw, gain_latent)
    latent = latent_norm.astype(bf16)
    key_rot = rotate(compressed[:, KVR:], cosine, sine_vals).astype(bf16)
    latent_rot = lax.all_gather(
        jnp.concatenate([latent, key_rot], axis=1), "fsdp", axis=0, tiled=True
    )
    down_own, latent_rot = lax.optimization_barrier((expert_down[0], latent_rot))
    down_parts = from_peers(down_own)
    all_rot = jnp.pad(latent_rot[:, KVR:], ((0, 0), (0, 2 * DN - DR)))

    def spread_columns(first, second, rest):
        one = jnp.concatenate([jnp.full((tok_rows, DN), rest, f32), first, second], axis=1)
        return jnp.concatenate([one, one], axis=1)

    zero = jnp.zeros_like(cosine)
    rotations = [
        spread_columns(cosine, cosine, 1.0),
        spread_columns(-sine_vals, zero, 0.0),
        spread_columns(zero, sine_vals, 0.0),
    ]
    query_all, keyval, probs_attn, context = attend(
        jnp.stack([fid * tok_rows, seq_length]).astype(jnp.int32),
        hidden_one,
        w_query,
        latent_rot[:, :KVR],
        w_expand,
        all_rot,
        rotations,
    )
    residual = tokens_f + jnp.dot(context, w_output, preferred_element_type=f32)
    normed_two, inverse_two = rms_norm(residual, gain_ffn)
    hidden_two = normed_two.astype(bf16)
    rest = (half // 2, half // 2)
    hid3, *more = gather(
        [hidden_two],
        False,
        1,
        [(pieces, -r) for r in turns]
        + [(expert_up[0], -r, rest, w) for r, w in zip(turns, up_begun)],
    )
    up_parts = [expert_up[0]] + more[peers - 1 :]
    gu_weight = jnp.roll(jnp.stack([pieces] + more[: peers - 1]), fid, axis=0)
    gu_weight = gu_weight.transpose(1, 0, 2, 3).reshape(dim, -1)
    hid_plane = hid3.reshape(plane_rows, dim)
    cot3 = cot_plane.reshape(group, tok_rows, dim)
    router_probs = jax.nn.softmax(jnp.dot(hidden_two, w_router, preferred_element_type=f32), axis=-1)
    local_shares = jnp.sum(router_probs * valid_mask[:, None], axis=0)
    frequency = expert_count / (TOPK * valid_total) * route_counts
    d_probs_own = balance_weight * valid_mask[:, None] * frequency[None, :] / valid_total
    dlog_own = (
        router_probs * (d_probs_own - jnp.sum(router_probs * d_probs_own, axis=-1, keepdims=True))
    ).astype(bf16)
    named = jnp.any(plane_small[:, :TOPK, :] == eid.astype(f32), axis=1)
    place = jnp.arange(tok_rows)
    before = (place[:, None] < place[None, :]).astype(bf16)
    ranks = jnp.dot(named.astype(bf16), before, preferred_element_type=f32)
    ranks = jnp.where(named, ranks, -1.0)[:, None, :]
    numbers = jnp.concatenate(
        [jnp.stack([eid, fid * tok_rows, fid]).astype(jnp.int32), all_lengths.astype(jnp.int32)]
    )
    made = ffn(
        capacity,
        numbers,
        fill_scale.reshape(1),
        hid3,
        cot3,
        ranks,
        gate_parts,
        up_parts,
        down_parts,
        w_router,
        gu_weight,
        sd_weight,
    )

    rows_in, d_out = made[:peers], made[peers : 2 * peers]
    out_part, back_part, act, d_hidden_g, d_hidden_u, dlog_rows, shared_scaled, d_gu = made[
        2 * peers :
    ]

    def outer(left, right):
        return lax.dot_general(left, right, (((0,), (0,)), ((), ())), preferred_element_type=f32)

    def back(left, weight):
        return lax.dot_general(left, weight, (((1,), (1,)), ((), ())), preferred_element_type=f32)

    def gate_term(r):
        return outer(rows_in[r], d_hidden_g)

    def up_term(r):
        return outer(rows_in[r], d_hidden_u)

    def down_term(r):
        return outer(act, d_out[r])

    def with_peers(term):
        arrived = sum_to_peers(lambda r: term(r).astype(bf16))
        total = term(0)
        for block in arrived:
            total = total + block.astype(f32)
        return total

    def plus(total, blocks):
        for block in blocks:
            total = total + block.astype(f32)
        return total

    dlog_wide = jnp.pad(dlog_rows, ((0, 0), (0, -expert_count % 128)))
    d_hidden_two, *more = scatter(
        [back_part],
        False,
        2,
        [(gate_term(r).astype(bf16), r) for r in turns],
        [
            (hid_plane, d_gu),
            (shared_scaled, cot_plane),
            (rows_in[1], d_hidden_u),
            (act, d_out[1]),
            (rows_in[0], d_hidden_g),
            (rows_in[0], d_hidden_u),
            (act, d_out[0]),
            *[(w, dlog_wide) for w in rows_in],
        ]
        if peers == 2
        else [],
    )
    gate_blocks = more[: peers - 1]
    if peers == 2:
        router_parts = more[-peers:]
        d_gu_weight, d_sd, *others, gate_own, up_own, down_own = more[1:-peers]
    else:
        d_gu_weight = outer(hid_plane, d_gu).astype(bf16)
        d_sd = outer(shared_scaled, cot_plane).astype(bf16)
        others = [up_term(r).astype(bf16) for r in turns]
        others = others + [down_term(r).astype(bf16) for r in turns]
        gate_own, up_own, down_own = gate_term(0), up_term(0), down_term(0)
        router_parts = [outer(w, dlog_rows) for w in rows_in]
    d_sd = d_sd[:units]
    out_part, d_hidden_two = lax.optimization_barrier((out_part, d_hidden_two))
    out_sum = lax.psum_scatter(
        out_part.reshape(plane_rows, dim), "expert", scatter_dimension=0, tiled=True
    )
    egate_grad = plus(gate_own.astype(f32), gate_blocks)[None]
    d_hidden_two = d_hidden_two + back(dlog_own, w_router)
    router_parts = jnp.stack([w[:, :expert_count].astype(f32) for w in router_parts])
    router_grad = jnp.roll(router_parts, fid, axis=0).reshape(dim, -1) + outer(hidden_two, dlog_own)
    d_gu_blocks = d_gu_weight.reshape(group, peers, dim // (group * peers), -1)
    d_sd_blocks = d_sd.reshape(peers, units // peers, dim)

    def gu_term(r):
        return lax.dynamic_index_in_dim(d_gu_blocks, (fid + r) % peers, axis=1, keepdims=False)

    def sd_term(r):
        return lax.dynamic_index_in_dim(d_sd_blocks, (fid + r) % peers, axis=0, keepdims=False)

    gu_sum = plus(gu_term(0).astype(f32), sum_to_peers(gu_term)).astype(bf16)
    sdown_grad = plus(sd_term(0).astype(f32), sum_to_peers(sd_term))
    grad_out = cotangent.astype(f32) * (valid_mask * fill_scale)[:, None]
    d_residual, d_ffn_gain = norm_back(d_hidden_two, residual, inverse_two, gain_ffn)
    d_residual = d_residual + grad_out
    d_residual_low = d_residual.astype(bf16)
    d_query, d_keyval_all, d_key_rot = attend_back(
        d_residual_low, w_output, query_all, keyval, probs_attn, all_rot, rotations
    )
    d_key_rot = d_key_rot[:, :DR]

    def own_rows(array, r):
        return lax.dynamic_slice_in_dim(array, (fid + r) % peers * tok_rows, tok_rows, axis=0)

    swapped = [(own_rows(d_keyval_all, r).astype(bf16), r) for r in turns]
    swapped = swapped + [(own_rows(d_key_rot, r).astype(bf16), r) for r in turns]
    *arrived, d_output_w, d_query_w, d_hidden_one = exchange(
        4,
        swapped,
        [(context, d_residual_low), (hidden_one, d_query)],
        d_query,
        w_query,
    )
    up_others, arrived[0] = lax.optimization_barrier((others[: peers - 1], arrived[0]))
    size = peers
    up_blocks = [
        lax.ppermute(w, "fsdp", [(j, (j + r) % size) for j in range(size)])
        for w, r in zip(up_others, turns)
    ]
    own_dkeyval = plus(own_rows(d_keyval_all, 0).astype(f32), arrived[: peers - 1])
    own_dkeyrot = plus(own_rows(d_key_rot, 0), arrived[peers - 1 :])
    gu_sum, own_dkeyval = lax.optimization_barrier((gu_sum, own_dkeyval))
    gu_sum = lax.all_to_all(gu_sum, "expert", split_axis=0, concat_axis=0, tiled=True)
    d_keyval = own_dkeyval.astype(bf16)
    d_latent = back(d_keyval, w_expand)
    d_latent_raw, d_latent_gain = norm_back(d_latent, latent_raw, inverse_kv, gain_latent)
    d_compressed = jnp.concatenate(
        [d_latent_raw, rotate_back(own_dkeyrot, cosine, sine_vals)], axis=-1
    ).astype(bf16)
    d_compress_w, d_expand_w = outer_products([(hidden_one, d_compressed), (latent, d_keyval)])
    d_hidden_one = d_hidden_one + back(d_compressed, w_compress)
    d_tokens, d_attn_gain = norm_back(d_hidden_one, tokens_f, inverse_one, gain_attn)
    tokens_grad = d_tokens + d_residual
    def lanes(vector):
        piece = vector.reshape(devices, -1)
        return jnp.pad(piece, ((0, 0), (0, tok_rows - piece.shape[1])))

    small_grads = jnp.stack(
        [
            lanes(d_attn_gain),
            lanes(d_latent_gain),
            lanes(d_ffn_gain),
            lanes(jnp.tile(local_shares, devices)),
        ]
        + [jnp.zeros((devices, tok_rows), f32)] * 4,
        axis=1,
    )
    dense = [
        w.astype(bf16).reshape(devices, -1, w.shape[-1])
        for w in (d_query_w, d_compress_w, d_expand_w, d_output_w, router_grad)
    ]
    q_grad, kva_grad, kvb_grad, out_grad, router_out, smalls, *blocks = scatter(
        dense + [small_grads],
        True,
        3,
        [(w, r) for w, r in zip(others[peers - 1 :], turns)],
    )
    gu_sum, out_sum, smalls = lax.optimization_barrier((gu_sum, out_sum, smalls))
    mixed = (residual + out_sum.astype(f32)).astype(bf16)
    gu_sum = gu_sum.astype(f32).transpose(1, 0, 2)
    sgate_grad = gu_sum[:, :, :units].reshape(shared_gate.shape)
    sup_grad = gu_sum[:, :, units + lanes_more : 2 * units + lanes_more].reshape(shared_up.shape)
    eup_grad = plus(up_own.astype(f32), up_blocks)[None]
    edown_grad = plus(down_own.astype(f32), blocks)[None]
    attn_gain_grad = smalls[0, : attn_gain.shape[0]]
    kv_gain_grad = smalls[1, : kv_gain.shape[0]]
    ffn_gain_grad = smalls[2, : ffn_gain.shape[0]]
    balance = jnp.sum(frequency * (smalls[3, :expert_count] / valid_total))
    return (
        mixed,
        tokens_grad,
        balance,
        attn_gain_grad,
        q_grad,
        kva_grad,
        kv_gain_grad,
        kvb_grad,
        out_grad,
        ffn_gain_grad,
        router_out,
        sgate_grad,
        sup_grad,
        sdown_grad,
        egate_grad,
        eup_grad,
        edown_grad,
    )


def solution(mesh):
    return jax.shard_map(
        body,
        mesh=mesh,
        in_specs=(
            P(("expert", "fsdp"), None),
            P(("expert", "fsdp"), None),
            P(("expert", "fsdp"), None),
            P("expert"),
            P(("expert", "fsdp")),
            P(("expert", "fsdp"), None),
            P(("expert", "fsdp"), None),
            P(("expert", "fsdp")),
            P(("expert", "fsdp"), None),
            P(("expert", "fsdp"), None),
            P(("expert", "fsdp")),
            P(("expert", "fsdp"), None),
            P(("expert", "fsdp"), None),
            P(("expert", "fsdp"), None),
            P(("expert", "fsdp"), None),
            P("expert", "fsdp", None),
            P("expert", "fsdp", None),
            P("expert", None, "fsdp"),
        ),
        out_specs=(
            P(("expert", "fsdp"), None),
            P(("expert", "fsdp"), None),
            P(),
            P(("expert", "fsdp")),
            P(("expert", "fsdp"), None),
            P(("expert", "fsdp"), None),
            P(("expert", "fsdp")),
            P(("expert", "fsdp"), None),
            P(("expert", "fsdp"), None),
            P(("expert", "fsdp")),
            P(("expert", "fsdp"), None),
            P(("expert", "fsdp"), None),
            P(("expert", "fsdp"), None),
            P(("expert", "fsdp"), None),
            P("expert", "fsdp", None),
            P("expert", "fsdp", None),
            P("expert", None, "fsdp"),
        ),
        check_vma=False,
    )
```
